128 devices in a mesh: dp: 32 (over z, y, core), seq: 4 (over x).
Axes of the slice: x: 4, y: 4, z: 4, core: 2. Of those that a mesh axis runs over, the one named last changes fastest.
Arguments:
- bases: int32 [32, 65536], P('dp', 'seq'), may hold values from 0 to 3
- skip: bfloat16 [32, 1024, 1536], P('dp', 'seq'), may hold values from -6 to 6
- base_table: float32 [4, 1536], replicated, may hold values from -3 to 3
- conv_weight: bfloat16 [5, 1536, 1536], replicated, may hold values from -0.0625 to 0.0625
- conv_gain: float32 [1536], replicated, may hold values from 0.25 to 1.75
- attn_gain: float32 [1536], replicated, may hold values from 0.25 to 1.75
- w_query: bfloat16 [1536, 1024], P(('dp', 'seq')), may hold values from -3.1001355 to 3.1001355
- w_kv: bfloat16 [1536, 320], P(('dp', 'seq')), may hold values from -0.10333785 to 0.10333785
- w_out: bfloat16 [1536, 1536], P(('dp', 'seq')), may hold values from -0.15625 to 0.15625
- cotangent: bfloat16 [32, 512, 1536], P('dp', 'seq'), may hold values from -6 to 6
Outputs:
- coarse: bfloat16 [32, 512, 1536], P('dp', 'seq')
- skip_grad: bfloat16 [32, 1024, 1536], P('dp', 'seq')
- grad_query: float32 [1536, 1024], P(('dp', 'seq'))
- grad_kv: float32 [1536, 320], P(('dp', 'seq'))
- grad_out: float32 [1536, 1536], P(('dp', 'seq'))
The draws below stay inside these ranges and needn't reach their ends.
All inputs are finite; a program needn't handle non-finite values.
Results may differ from the reference program's by a relative error of at most 0.013.
Values may be sent and summed in bfloat16 or wider, within the bound.
No kernel may reach another device: no remote copies, remote signals or barrier semaphores. Data moves between devices by JAX's collectives and lax.ppermute only.
A program may use at most 192 MiB of HBM per device.

```python
import jax
import jax.numpy as jnp
from jax import lax

C = 1536
HQ = 8
HD = 128
VD = 192
COARSE = 512
CELLS = 1024
BASES = 65536
SAMPLES = 32


def shared_keys(key):
    return jnp.clip(jax.random.normal(jax.random.fold_in(key, 11), (C, HD), jnp.float32), -4.0, 4.0) * C ** (-0.5)


def draw_w_kv(key, part):
    base = shared_keys(key)
    key = jax.random.fold_in(key, 3)
    values = jnp.clip(jax.random.normal(key, (C, VD), jnp.float32), -4.0, 4.0) * C ** (-0.5)
    return jnp.concatenate([base, values], axis=1).astype(jnp.bfloat16)


def draw_w_query(key, part):
    key = jax.random.fold_in(key, 5)
    query = jnp.clip(jax.random.normal(key, (C, HQ * HD), jnp.float32), -4.0, 4.0) * C ** (-0.5)
    return query.astype(jnp.bfloat16)


def place_ends(array, own_key, low, high):
    extent = array.shape
    place = [jax.random.randint(jax.random.fold_in(own_key, axis), (), 0, extent[axis]) for axis in range(len(extent))]
    array = array.at[tuple(place)].set(low)
    longest = extent.index(max(extent))
    place[longest] = (place[longest] + 1) % extent[longest]
    return array.at[tuple(place)].set(high)


def shard_levels(key, dims, shards, least, top_value):
    factor_of = 1.0
    for dim, blocks in shards:
        steps = jax.random.uniform(jax.random.fold_in(jax.random.fold_in(key, 6), dim), (blocks,), jnp.float32, least / len(shards), top_value / len(shards))
        factor_of = factor_of * jnp.repeat(jnp.exp(steps), dims[dim] // blocks).reshape((-1,) + (1,) * (len(dims) - 1 - dim))
    return factor_of


def gaussian(rng, dims, deviation, limit, shards=(), kind=jnp.bfloat16):
    array = deviation * jax.random.normal(rng, dims, jnp.float32)
    if shards:
        array = array * shard_levels(rng, dims, shards, -0.22, 0.18)
    return jnp.clip(array, -limit, limit).astype(kind)


def setup_inputs(seed: int = 0) -> dict:
    splits = jax.random.split(jax.random.key(seed), 11)
    bases = place_ends(jax.random.randint(splits[0], (SAMPLES, BASES), 0, 4), jax.random.fold_in(splits[0], 1), 0, 3).astype(jnp.int32)
    skip = gaussian(splits[1], (SAMPLES, CELLS, C), 1.0, 6.0, ((0, 32), (1, 4)))
    base_table = gaussian(splits[2], (4, C), 4 ** -0.5, 3.0, (), jnp.float32)
    conv_weight = gaussian(splits[3], (5, C, C), (5 * C) ** -0.5, 0.0625)
    conv_gain = jnp.clip(1.0 + 0.15 * jax.random.normal(splits[4], (C,), jnp.float32), 0.25, 1.75)
    attn_gain = jnp.clip(1.0 + 0.15 * jax.random.normal(splits[5], (C,), jnp.float32), 0.25, 1.75)
    w_query = draw_w_query(jax.random.fold_in(splits[10], 71), 0)
    w_kv = draw_w_kv(jax.random.fold_in(splits[10], 71), 0)
    w_out = gaussian(splits[8], (HQ * VD, C), (HQ * VD) ** -0.5, 0.15625, ((0, 128),))
    cotangent = gaussian(splits[9], (SAMPLES, COARSE, C), 1.0, 6.0, ((0, 32), (1, 4)))
    return dict(bases=bases, skip=skip, base_table=base_table, conv_weight=conv_weight, conv_gain=conv_gain, attn_gain=attn_gain, w_query=w_query, w_kv=w_kv, w_out=w_out, cotangent=cotangent)


HIGH = lax.Precision.HIGHEST

def rms_scale(value):
    return lax.rsqrt(lax.optimization_barrier(jnp.mean(value * value, axis=-1, keepdims=True)) + 1e-06)

def rms_back(value, gain, grad):
    scale = rms_scale(value)
    scaled = grad * gain
    return scale * scaled - value * (scale * scale * scale) * lax.optimization_barrier(jnp.mean(value * scaled, axis=-1, keepdims=True))

def gelu_fwd(value):
    return 0.5 * value * (1.0 + jax.scipy.special.erf(value * 0.7071067811865476))

def gelu_slope(value):
    return 0.5 * (1.0 + jax.scipy.special.erf(value * 0.7071067811865476)) + value * jnp.exp(-0.5 * value * value) * 0.3989422804014327

def conv_forward(padded, weight):
    length = padded.shape[0] - 4
    window = jnp.stack([padded[k:k + length] for k in range(5)], axis=1)
    return lax.dot_general(window, weight, (((1, 2), (0, 1)), ((), ())), preferred_element_type=jnp.float32)

def conv_backward(padded, weight):
    length = padded.shape[0] - 4
    window = jnp.stack([padded[4 - k:4 - k + length] for k in range(5)], axis=1)
    return lax.dot_general(window, weight, (((1, 2), (0, 2)), ((), ())), preferred_element_type=jnp.float32)

def tdot(left, right):
    return lax.dot_general(left, right, (((0,), (0,)), ((), ())), preferred_element_type=jnp.float32)

def rdot(left, right):
    return lax.dot_general(left, right, (((1,), (1,)), ((), ())), preferred_element_type=jnp.float32)

def sample_pass(sample_bases, sample_skip, sample_cot, base_table, conv_weight, conv_gain, attn_gain, w_query, w_kv, w_out):
    cells = sample_bases.reshape(-1, 64)
    counts = lax.optimization_barrier(jnp.sum((cells[:, :, None] == jnp.arange(4, dtype=jnp.int32)).astype(jnp.float32), axis=1))
    embed = jnp.dot((counts - 16.0) * 0.25, base_table, precision=HIGH)
    state = sample_skip.astype(jnp.float32) + embed
    pre = state * rms_scale(state) * conv_gain
    active = gelu_fwd(pre).astype(jnp.bfloat16)
    level = state + conv_forward(jnp.pad(active, ((2, 2), (0, 0))), conv_weight)
    pairs = level.reshape(-1, 2, level.shape[1])
    pooled = (pairs[:, 0] + pairs[:, 1]) * 0.5
    normed = (pooled * rms_scale(pooled) * attn_gain).astype(jnp.bfloat16)
    query = jnp.dot(normed, w_query, preferred_element_type=jnp.float32).astype(jnp.bfloat16)
    keyval = jnp.dot(normed, w_kv, preferred_element_type=jnp.float32).astype(jnp.bfloat16)
    keys = keyval[:, :HD]
    values = keyval[:, HD:]
    positions = query.shape[0]
    heads_q = query.reshape(positions, HQ, HD)
    inv = 1.0 / HD ** 0.5
    scores = jnp.einsum('thd,sd->hts', heads_q.astype(jnp.float32), keys.astype(jnp.float32)) * inv
    peak = lax.optimization_barrier(jnp.max(scores, axis=-1, keepdims=True))
    expo = jnp.exp(scores - peak)
    probs = expo / lax.optimization_barrier(jnp.sum(expo, axis=-1, keepdims=True))
    weights = probs.astype(jnp.bfloat16)
    heads = jnp.einsum('hts,se->the', weights.astype(jnp.float32), values.astype(jnp.float32)).reshape(positions, HQ * VD).astype(jnp.bfloat16)
    coarse = (pooled + jnp.dot(heads, w_out, preferred_element_type=jnp.float32)).astype(jnp.bfloat16)
    term_out = tdot(heads, sample_cot)
    d_heads = rdot(sample_cot, w_out).astype(jnp.bfloat16)
    d_split = d_heads.reshape(positions, HQ, VD).astype(jnp.float32)
    d_probs = jnp.einsum('the,se->hts', d_split, values.astype(jnp.float32))
    d_scores = (probs * (d_probs - lax.optimization_barrier(jnp.sum(probs * d_probs, axis=-1, keepdims=True))) * inv).astype(jnp.bfloat16)
    d_query = jnp.einsum('hts,sd->thd', d_scores.astype(jnp.float32), keys.astype(jnp.float32)).reshape(positions, HQ * HD).astype(jnp.bfloat16)
    d_keys = jnp.einsum('hts,thd->sd', d_scores.astype(jnp.float32), heads_q.astype(jnp.float32))
    d_values = jnp.einsum('hts,the->se', weights.astype(jnp.float32), d_split)
    d_keyval = jnp.concatenate([d_keys, d_values], axis=1).astype(jnp.bfloat16)
    term_query = tdot(normed, d_query)
    term_kv = tdot(normed, d_keyval)
    d_normed = rdot(d_query, w_query) + rdot(d_keyval, w_kv)
    d_pooled = sample_cot.astype(jnp.float32) + rms_back(pooled, attn_gain, d_normed)
    d_level = jnp.repeat(d_pooled * 0.5, 2, axis=0).astype(jnp.bfloat16)
    d_active = conv_backward(jnp.pad(d_level, ((2, 2), (0, 0))), conv_weight)
    skip_grad = (d_level.astype(jnp.float32) + rms_back(state, conv_gain, gelu_slope(pre) * d_active)).astype(jnp.bfloat16)
    return (coarse, skip_grad, term_query, term_kv, term_out)

def reference(bases, skip, base_table, conv_weight, conv_gain, attn_gain, w_query, w_kv, w_out, cotangent):
    width = skip.shape[2]
    zero_q = jnp.zeros((width, w_query.shape[1]), jnp.float32)
    zero_kv = jnp.zeros((width, w_kv.shape[1]), jnp.float32)
    zero_out = jnp.zeros((w_out.shape[0], width), jnp.float32)

    def step(carry, inputs):
        coarse, skip_grad, term_query, term_kv, term_out = sample_pass(inputs[0], inputs[1], inputs[2], base_table, conv_weight, conv_gain, attn_gain, w_query, w_kv, w_out)
        return ((carry[0] + term_query, carry[1] + term_kv, carry[2] + term_out), (coarse, skip_grad))
    totals, outputs = lax.scan(step, (zero_q, zero_kv, zero_out), (bases, skip, cotangent))
    factor = 1.0 / SAMPLES
    return (outputs[0], outputs[1], totals[0] * factor, totals[1] * factor, totals[2] * factor)
```

```python
import jax
import jax.numpy as jnp
from jax import lax
from jax.experimental import pallas as pl
from jax.experimental.pallas import tpu as pltpu
from jax.sharding import Mesh
from jax.sharding import PartitionSpec as P

HQ = 8
HD = 128
VD = 192
VMEM_LIMIT = 60 * 1024 * 1024
F32 = jnp.float32
BF16 = jnp.bfloat16


def ndot(left, right):
    return lax.dot_general(
        left, right, (((1,), (0,)), ((), ())), preferred_element_type=F32
    )


def rdot(left, right):
    return lax.dot_general(
        left, right, (((1,), (1,)), ((), ())), preferred_element_type=F32
    )


def tdot(left, right):
    return lax.dot_general(
        left, right, (((0,), (0,)), ((), ())), preferred_element_type=F32
    )


def embed_counts(counts, skip, table):
    state = skip.astype(F32)
    for base in range(4):
        state = state + ((counts[base] - 16.0) * 0.25) * table[base : base + 1, :]
    return state


def embed_rows(cells, skip, table):
    counts = [jnp.sum((cells == base).astype(F32), axis=1, keepdims=True) for base in range(4)]
    return embed_counts(counts, skip, table)


def row_scale(value):
    return lax.rsqrt(jnp.mean(value * value, axis=-1, keepdims=True) + 1e-06)


def front_kernel(
    ends, cells, skip, edge_prev, edge_next, table, gain, attn_gain,
    weight, pooled, normed, state_buf, active_buf, lhs, weight_buf, arrived,
):
    rows = skip.shape[0]
    half = rows // 2
    width = skip.shape[1]
    steps, _, _, block = weight_buf.shape

    def fetch(step):
        cols = pl.ds(pl.multiple_of(step * block, block), block)
        return pltpu.make_async_copy(weight.at[:, :, cols], weight_buf.at[step], arrived.at[step])

    for step in range(steps):
        fetch(step).start()

    def rows_in(state, at, keep):
        pre = state * row_scale(state) * gain[...]
        active = 0.5 * pre * (1.0 + lax.erf(pre * 0.7071067811865476))
        active = active.astype(BF16).astype(F32)
        if keep is not None:
            active = jnp.where(keep > 0, active, 0.0)
        count = state.shape[0]
        for tile in range(skip.shape[1] // 128):
            lanes = slice(tile * 128, (tile + 1) * 128)
            state_buf[tile, pl.ds(at, count), :] = state[:, lanes]
            active_buf[tile, pl.ds(at, count), :] = active[:, lanes]

    def edge_rows(edge):
        counts = [edge[:, width + base : width + base + 1].astype(F32) for base in range(4)]
        return embed_counts(counts, edge[:, 0:width], table)

    rows_in(edge_rows(edge_prev), 0, ends[0])
    rows_in(edge_rows(edge_next), rows + 8, ends[1])

    chunk = 64

    def one(i, carry):
        at = pl.multiple_of(i * chunk, chunk)
        state = embed_rows(cells[pl.ds(at, chunk), :], skip[pl.ds(at, chunk), :], table)
        rows_in(state, pl.multiple_of(at + 8, 8), None)
        return carry

    lax.fori_loop(0, rows // chunk, one, 0)
    for tile in range(width // 128):
        cols = slice(tile * 128, (tile + 1) * 128)
        part = [active_buf[tile, pl.ds(6 + j, half, 2), :] for j in range(6)]
        for k in range(5):
            lhs[k, :, cols] = ((part[k] + part[k + 1]) * 0.5).astype(BF16)
        pooled[:, cols] = (
            state_buf[tile, pl.ds(8, half, 2), :] + state_buf[tile, pl.ds(9, half, 2), :]
        ) * 0.5

    def one_block(step, carry):
        fetch(step).wait()
        total = ndot(lhs[0], weight_buf[step, 0])
        for k in range(1, 5):
            total = total + ndot(lhs[k], weight_buf[step, k])
        cols = pl.ds(pl.multiple_of(step * block, block), block)
        pooled[:, cols] = pooled[:, cols] + total
        return carry

    lax.fori_loop(0, steps, one_block, 0)

    def finish_rows(i, carry):
        rows_at = pl.ds(pl.multiple_of(i * 64, 64), 64)
        value = pooled[rows_at, :]
        normed[rows_at, :] = (value * row_scale(value) * attn_gain[...]).astype(BF16)
        return carry

    lax.fori_loop(0, half // 64, finish_rows, 0)


def front(ends, cells, skip, edge_prev, edge_next, table, gain, attn_gain, weight, block=256):
    rows, width = skip.shape
    half = rows // 2
    whole = lambda array: pl.BlockSpec(array.shape, lambda n, s: (0,) * array.ndim)
    small = (cells, skip, edge_prev, edge_next, table, gain, attn_gain)
    return pl.pallas_call(
        front_kernel,
        grid_spec=pltpu.PrefetchScalarGridSpec(
            num_scalar_prefetch=1,
            grid=(1,),
            in_specs=[whole(a) for a in small] + [pl.BlockSpec(memory_space=pl.ANY)],
            out_specs=[
                pl.BlockSpec((half, width), lambda n, s: (0, 0)),
                pl.BlockSpec((half, width), lambda n, s: (0, 0)),
            ],
            scratch_shapes=[
                pltpu.VMEM((width // 128, rows + 16, 128), F32),
                pltpu.VMEM((width // 128, rows + 16, 128), F32),
                pltpu.VMEM((5, half, width), BF16),
                pltpu.VMEM((width // block, 5, width, block), BF16),
                pltpu.SemaphoreType.DMA((width // block,)),
            ],
        ),
        out_shape=[
            jax.ShapeDtypeStruct((half, width), F32),
            jax.ShapeDtypeStruct((half, width), BF16),
        ],
        compiler_params=pltpu.CompilerParams(vmem_limit_bytes=VMEM_LIMIT),
        cost_estimate=pl.CostEstimate(
            flops=2 * half * 5 * width * width, bytes_accessed=10 * width * width + 8 * rows * width, transcendentals=rows * width
        ),
        name="front",
    )(ends, *small, weight)


def back_kernel(
    cells, skip, table, gain, grad, grad_prev, grad_next, weight, out,
    state_buf, scaled_buf, grad_buf, turned_buf, level_buf, scale_buf, sum_buf, weight_buf, arrived,
):
    rows, width = skip.shape
    half = rows // 2
    steps, _, block, _ = weight_buf.shape
    chunk = 64

    def fetch(step):
        at = pl.ds(pl.multiple_of(step * block, block), block)
        return pltpu.make_async_copy(weight.at[:, at, :], weight_buf.at[step], arrived.at[step])

    for step in range(steps):
        fetch(step).start()

    grad_buf[pl.ds(0, 16), :] = grad_prev[...].astype(F32)
    grad_buf[pl.ds(16, half), :] = grad[...].astype(F32)
    grad_buf[pl.ds(half + 16, 16), :] = grad_next[...].astype(F32)
    for tile in range(width // 128):
        lanes = slice(tile * 128, (tile + 1) * 128)
        before, here, later = [
            grad_buf[pl.ds(15 + shift, half), lanes].T.astype(BF16) for shift in range(3)
        ]
        pairs = ((later, later), (here, later), (here, here), (before, here), (before, before))
        for tap, (even, odd) in enumerate(pairs):
            turned_buf[tap, lanes, 0:half] = even
            turned_buf[tap, lanes, half:rows] = odd

    def one(i, carry):
        at = pl.ds(pl.multiple_of(i * chunk, chunk), chunk)
        state = embed_rows(cells[at, :], skip[at, :], table)
        state_buf[at, :] = state
        scale_buf[at, :] = row_scale(state)
        return carry

    lax.fori_loop(0, rows // chunk, one, 0, unroll=2)
    sum_buf[...] = jnp.zeros_like(sum_buf)

    def one_block(step, carry):
        fetch(step).wait()
        total = None
        for k in range(5):
            part = ndot(weight_buf[step, k], turned_buf[k])
            total = part if total is None else total + part
        for tile in range(block // 128):
            level = total[tile * 128 : (tile + 1) * 128, :].T
            level_buf[tile, pl.ds(0, half, 2), :] = level[0:half]
            level_buf[tile, pl.ds(1, half, 2), :] = level[half:]
        cols = pl.ds(pl.multiple_of(step * block, block), block)

        def two(i, carry):
            at = pl.ds(pl.multiple_of(i * 256, 256), 256)
            state = state_buf[at, cols]
            pre = state * scale_buf[at, :] * gain[:, cols]
            slope = 0.5 * (1.0 + lax.erf(pre * 0.7071067811865476)) + pre * jnp.exp(
                -0.5 * pre * pre
            ) * 0.3989422804014327
            level = jnp.concatenate([level_buf[t, at, :] for t in range(block // 128)], axis=1)
            scaled = slope * level * gain[:, cols]
            scaled_buf[at, cols] = scaled
            product = state * scaled
            folded = product[:, 0:128]
            for tile in range(1, block // 128):
                folded = folded + product[:, tile * 128 : (tile + 1) * 128]
            sum_buf[at, :] = sum_buf[at, :] + folded
            return carry

        lax.fori_loop(0, rows // 256, two, 0)
        return carry

    lax.fori_loop(0, steps, one_block, 0)

    scale = scale_buf[...]
    coef = (scale * scale * scale) * (jnp.sum(sum_buf[...], axis=1, keepdims=True) * (1.0 / width))
    for tile in range(width // 128):
        lanes = slice(tile * 128, (tile + 1) * 128)
        own = grad_buf[pl.ds(16, half), lanes]
        scaled = scaled_buf[:, lanes]
        state = state_buf[:, lanes]
        level_buf[0, pl.ds(0, half, 2), :] = own
        level_buf[0, pl.ds(1, half, 2), :] = own
        out[:, lanes] = (level_buf[0] + (scale * scaled - state * coef)).astype(BF16)


def back(cells, skip, table, gain, grad, grad_prev, grad_next, weight, block=256):
    rows, width = skip.shape
    half = rows // 2
    whole = lambda array: pl.BlockSpec(array.shape, lambda n: (0,) * array.ndim)
    small = (cells, skip, table, gain, grad, grad_prev, grad_next)
    return pl.pallas_call(
        back_kernel,
        grid=(1,),
        in_specs=[whole(a) for a in small] + [pl.BlockSpec(memory_space=pl.ANY)],
        out_specs=pl.BlockSpec((rows, width), lambda n: (0, 0)),
        scratch_shapes=[
            pltpu.VMEM((rows, width), F32),
            pltpu.VMEM((rows, width), F32),
            pltpu.VMEM((half + 32, width), F32),
            pltpu.VMEM((5, width, rows), BF16),
            pltpu.VMEM((block // 128, rows, 128), F32),
            pltpu.VMEM((rows, 1), F32),
            pltpu.VMEM((rows, 128), F32),
            pltpu.VMEM((width // block, 5, block, width), BF16),
            pltpu.SemaphoreType.DMA((width // block,)),
        ],
        out_shape=jax.ShapeDtypeStruct((rows, width), BF16),
        compiler_params=pltpu.CompilerParams(vmem_limit_bytes=VMEM_LIMIT),
        cost_estimate=pl.CostEstimate(
            flops=2 * half * 5 * width * width, bytes_accessed=10 * width * width + 8 * rows * width, transcendentals=2 * rows * width
        ),
        name="back",
    )(*small, weight)


def attend_kernel(
    place, norm0, norm1, norm2, norm3, cot0, cot1, cot2, near, far,
    d_in, heads, normed, cot, w_out, own, part1, part2, part3, w_in, query_kv, acc,
):
    head = pl.program_id(0)
    seq, core, depth, level = place[0], place[1], place[2], place[3]
    inv = 1.0 / HD**0.5
    half = own.shape[0]
    cols = w_in.shape[1]
    side = near.shape[2]
    first = cols - side + HD

    def rows_of(index):
        return pl.ds(pl.multiple_of(index * half, half), half)

    @pl.when(head == 0)
    def _():
        for source, side_core in ((near, core), (far, 1 - core)):
            for turn in range(4):
                z = lax.rem(depth + turn, 4)
                for other in range(4):
                    y = lax.rem(level + other, 4)
                    at = pl.ds(pl.multiple_of((z * 4 + y) * 96 + side_core * 48, 16), 48)
                    w_in[at, 0:side] = source[turn, other * 48 : (other + 1) * 48, :]
                    w_in[at, side:cols] = source[turn, 336:384, other * 128 : (other + 1) * 128]
                at = pl.ds(pl.multiple_of(z * 96 + side_core * 48, 16), 48)
                for b in range(3):
                    w_out[at, b * side : (b + 1) * side] = source[
                        turn, 192 + b * 48 : 240 + b * 48, :
                    ]
        for piece, value in enumerate((norm0, norm1, norm2, norm3)):
            normed[rows_of(lax.rem(seq + piece, 4)), :] = value[...]
        beside = seq + 1 - 2 * lax.rem(seq, 2)
        cot[rows_of(seq), :] = cot0[...]
        cot[rows_of(beside), :] = cot1[...]
        cot[rows_of(3 - seq), :] = cot2[0]
        cot[rows_of(3 - beside), :] = cot2[1]
        query_kv[...] = ndot(normed[...], w_in[...]).astype(BF16)

    keys = query_kv[:, first : first + HD]
    values = query_kv[:, first + HD : first + HD + VD]
    lanes = pl.ds(pl.multiple_of(head * HD, HD), HD)
    q = query_kv[:, lanes]
    d_heads = rdot(cot[...], w_out[pl.ds(pl.multiple_of(head * VD, VD), VD), :]).astype(BF16)
    scores = rdot(q, keys) * inv
    expo = jnp.exp(scores - jnp.max(scores, axis=1, keepdims=True))
    probs = expo * (1.0 / jnp.sum(expo, axis=1, keepdims=True))
    weights = probs.astype(BF16)
    heads[0] = ndot(weights, values).astype(BF16)
    d_probs = rdot(d_heads, values)
    inner = jnp.sum(probs * d_probs, axis=1, keepdims=True)
    d_scores = (probs * (d_probs - inner) * inv).astype(BF16)
    d_in[:, lanes] = ndot(d_scores, keys).astype(BF16)
    d_keys = tdot(d_scores, q)
    d_values = tdot(weights, d_heads)

    @pl.when(head == 0)
    def _():
        acc[:, 0:HD] = d_keys
        acc[:, HD : HD + VD] = d_values

    @pl.when(head > 0)
    def _():
        acc[:, 0:HD] += d_keys
        acc[:, HD : HD + VD] += d_values

    @pl.when(head == pl.num_programs(0) - 1)
    def _():
        d_in[:, first + HD :] = jnp.zeros((4 * half, cols - first - HD), BF16)
        d_in[:, first : first + HD + VD] = acc[...].astype(BF16)
        for piece, out in enumerate((own, part1, part2, part3)):
            rows = d_in[rows_of(lax.rem(seq + piece, 4)), :]
            out[...] = rdot(rows, w_in[...]).astype(out.dtype)


def attend(place, norms, cots, near, far):
    half, width = norms[0].shape
    rows = 4 * half
    cols = near.shape[2] + 128
    heads = 2
    whole = lambda array: pl.BlockSpec(array.shape, lambda h, s: (0,) * array.ndim)
    outs = [
        jax.ShapeDtypeStruct((rows, cols), BF16),
        jax.ShapeDtypeStruct((heads, rows, VD), BF16),
        jax.ShapeDtypeStruct((rows, width), BF16),
        jax.ShapeDtypeStruct((rows, width), BF16),
        jax.ShapeDtypeStruct((heads * VD, width), BF16),
        jax.ShapeDtypeStruct((half, width), F32),
    ] + [jax.ShapeDtypeStruct((half, width), BF16)] * 3
    specs = [whole(out) for out in outs]
    specs[1] = pl.BlockSpec((1, rows, VD), lambda h, s: (h, 0, 0))
    ins = (*norms, *cots, near, far)
    return pl.pallas_call(
        attend_kernel,
        grid_spec=pltpu.PrefetchScalarGridSpec(
            num_scalar_prefetch=1,
            grid=(heads,),
            in_specs=[whole(a) for a in ins],
            out_specs=specs,
            scratch_shapes=[
                pltpu.VMEM((width, cols), BF16),
                pltpu.VMEM((rows, cols), BF16),
                pltpu.VMEM((rows, HD + VD), F32),
            ],
        ),
        out_shape=outs,
        compiler_params=pltpu.CompilerParams(vmem_limit_bytes=VMEM_LIMIT),
        cost_estimate=pl.CostEstimate(
            flops=2 * rows * heads * (VD * width + 3 * rows * (HD + VD)) + 4 * rows * cols * width,
            bytes_accessed=8 * rows * width + 2 * heads * VD * width + 2 * cols * width,
            transcendentals=rows * heads * rows,
        ),
        name="attend",
    )(place, *ins)


def grads_kernel(place, normed, d_in, heads, cot, own, other, rows_in, rows_out):
    core, depth = place[1], place[2]
    width = cot.shape[1]
    cols = d_in.shape[1]
    side = width // 2
    blocks = rows_in.shape[1] // 128
    for turn, out in enumerate((other, own)):
        half = core if turn else 1 - core
        lanes = pl.ds(pl.multiple_of(half * side, side), side)
        rows_in[:, 0:cols] = tdot(normed[:, lanes], d_in[...]).astype(BF16)
        rows_out[...] = tdot(heads[half], cot[...]).astype(BF16)
        for k in range(4):
            quarter = lax.rem(depth + k, 4)
            count = side // 4
            at = pl.ds(pl.multiple_of(quarter * count, count), count)
            for b in range(blocks):
                out[k, b * count : (b + 1) * count, :] = rows_in[at, b * 128 : (b + 1) * 128]
            base = blocks * count
            count = VD // 4
            at = pl.ds(pl.multiple_of(quarter * count, count), count)
            for b in range(width // 128):
                out[k, base + b * count : base + (b + 1) * count, :] = rows_out[
                    at, b * 128 : (b + 1) * 128
                ]


def grads(place, normed, d_in, heads, cot):
    rows, width = cot.shape
    cols = d_in.shape[1]
    blocks = (cols + 127) // 128
    length = blocks * (width // 8) + width // 128 * (VD // 4)
    whole = lambda array: pl.BlockSpec(array.shape, lambda n, s: (0,) * array.ndim)
    outs = [jax.ShapeDtypeStruct((4, length, 128), BF16)] * 2
    ins = (normed, d_in, heads, cot)
    return pl.pallas_call(
        grads_kernel,
        grid_spec=pltpu.PrefetchScalarGridSpec(
            num_scalar_prefetch=1,
            grid=(1,),
            in_specs=[whole(a) for a in ins],
            out_specs=[whole(a) for a in outs],
            scratch_shapes=[
                pltpu.VMEM((width // 2, blocks * 128), BF16),
                pltpu.VMEM((VD, width), BF16),
            ],
        ),
        out_shape=outs,
        compiler_params=pltpu.CompilerParams(vmem_limit_bytes=VMEM_LIMIT),
        cost_estimate=pl.CostEstimate(
            flops=2 * rows * width * (cols + 2 * VD),
            bytes_accessed=16 * rows * width,
            transcendentals=0,
        ),
        name="grads",
    )(place, *ins)


def mix_kernel(place, heads, w_out, out):
    total = ndot(heads[0], w_out[0:VD, :]) + ndot(heads[1], w_out[VD : 2 * VD, :])
    out[0] = total.astype(BF16)


def mix(place, heads, w_out):
    rows = heads.shape[1] // 4
    width = w_out.shape[1]
    return pl.pallas_call(
        mix_kernel,
        grid_spec=pltpu.PrefetchScalarGridSpec(
            num_scalar_prefetch=1,
            grid=(4,),
            in_specs=[
                pl.BlockSpec((2, rows, VD), lambda n, s: (0, lax.rem(s[0] + n, 4), 0)),
                pl.BlockSpec(w_out.shape, lambda n, s: (0, 0)),
            ],
            out_specs=pl.BlockSpec((1, rows, width), lambda n, s: (n, 0, 0)),
        ),
        out_shape=jax.ShapeDtypeStruct((4, rows, width), BF16),
        compiler_params=pltpu.CompilerParams(vmem_limit_bytes=VMEM_LIMIT),
        cost_estimate=pl.CostEstimate(
            flops=16 * rows * width * VD, bytes_accessed=12 * rows * width, transcendentals=0
        ),
        name="mix",
    )(place, heads, w_out)


AXES = ("z", "y", "c", "x")
SIZES = (4, 4, 2, 4)


def place(z, y, c, x):
    return ((z * 4 + y) * 2 + c) * 4 + x


def moved(value, target):
    pairs = []
    for z in range(4):
        for y in range(4):
            for c in range(2):
                for x in range(4):
                    pairs.append((place(z, y, c, x), place(*target(z, y, c, x))))
    return lax.ppermute(value, AXES, pairs)


def flipped(value):
    return moved(value, lambda z, y, c, x: (z, y, 1 - c, x))


def turned(value, axis, by):
    return lax.ppermute(value, axis, [(i, (i + by) % 4) for i in range(4)])


def gathered(value, axis):
    me = lax.axis_index(axis)
    parts = [value, turned(value, axis, 3), turned(value, axis, 2), turned(value, axis, 1)]
    out = jnp.zeros((4, *value.shape), value.dtype)
    for j in range(4):
        out = lax.dynamic_update_index_in_dim(out, parts[j], lax.rem(me + j, 4), 0)
    return out


def summed(value, axis, dtype=BF16):
    me = lax.axis_index(axis)
    parts = [
        lax.dynamic_index_in_dim(value, lax.rem(me + j, 4), 0, keepdims=False) for j in range(4)
    ]
    total = parts[0].astype(F32)
    for j in range(1, 4):
        total = total + turned(parts[j], axis, j).astype(F32)
    return total.astype(dtype)


def by_core(own, other):
    first = lax.axis_index("c") == 0
    return jnp.where(first, own, other), jnp.where(first, other, own)


def around(value, axis="x"):
    return [value, turned(value, axis, 3), turned(value, axis, 2), turned(value, axis, 1)]


def returned(pieces):
    total = pieces[0].astype(F32)
    for k in range(1, 4):
        total = total + turned(pieces[k], "x", k).astype(F32)
    return total


def returned_along(pieces, axis):
    total = pieces[0].astype(F32)
    for k in range(1, 4):
        total = total + turned(pieces[k], axis, k).astype(F32)
    return total.astype(BF16)


def gather_in_x(w_query, w_kv):
    seq = lax.axis_index("x")
    cols = w_query.shape[1] // 4
    rows = jnp.zeros((4, w_query.shape[0], cols + w_kv.shape[1]), BF16)
    for k in range(4):
        head_cols = lax.dynamic_slice_in_dim(w_query, lax.rem(seq + k, 4) * cols, cols, 1)
        piece = jnp.concatenate([head_cols, w_kv], axis=1)
        if k:
            piece = turned(piece, "x", k)
        rows = lax.dynamic_update_index_in_dim(rows, piece, lax.rem(seq + 4 - k, 4), 0)
    return rows.reshape(48, rows.shape[2])


def after(value, *others):
    return lax.optimization_barrier((value, *others))[0]


def split_rows(pieces):
    first = pieces[:960].reshape(5, 4, 48, 128).transpose(1, 0, 2, 3).reshape(4, 240, 128)
    second = pieces[960:].reshape(12, 4, 12, 128).transpose(1, 0, 2, 3).reshape(4, 144, 128)
    return jnp.concatenate([first, second], axis=1)


def finish(value, cols, width):
    seq = lax.axis_index("x")
    pieces = value[:240].reshape(5, 4, 12, 128).transpose(1, 2, 0, 3).reshape(4, 12, 640)
    grad_query = jnp.zeros((4, 12, cols), F32)
    grad_kv = jnp.zeros((12, HD + VD), F32)
    for k in range(4):

        def home(z, y, c, x):
            block = 16 * c + 4 * z + y
            return block // 8, block // 2 % 4, block % 2, (x + k) % 4

        piece = lax.dynamic_index_in_dim(pieces, lax.rem(seq + k, 4), 0, keepdims=False)
        piece = moved(piece, home).astype(F32)
        grad_query = lax.dynamic_update_index_in_dim(
            grad_query, piece[:, :cols], lax.rem(seq + 4 - k, 4), 0
        )
        grad_kv = grad_kv + piece[:, cols : cols + HD + VD]
    grad_query = grad_query.transpose(1, 0, 2).reshape(12, 4 * cols)
    grad_out = value[240:].reshape(12, 12, 128).transpose(1, 0, 2).reshape(12, width)
    grad_out = moved(grad_out, lambda z, y, c, x: (x, 2 * c + z // 2, z % 2, y)).astype(F32)
    return grad_query, grad_kv, grad_out


def rms_back(value, gain, grad):
    scale = row_scale(value)
    scaled = grad * gain
    return scale * scaled - value * (scale * scale * scale) * jnp.mean(
        value * scaled, axis=-1, keepdims=True
    )


def per_device(
    bases, skip, base_table, conv_weight, conv_gain, attn_gain, w_query, w_kv, w_out, cotangent
):
    skip = skip[0]
    cot = cotangent[0]
    rows, width = skip.shape
    half = rows // 2
    cells = bases.reshape(rows, bases.shape[1] // rows)
    seq = lax.axis_index("x")
    ends = jnp.stack([seq, 3 - seq]).astype(jnp.int32)

    def ahead(value):
        return lax.ppermute(value, "x", [(i, i + 1) for i in range(3)])

    def behind(value):
        return lax.ppermute(value, "x", [(i + 1, i) for i in range(3)])

    def edge(tokens, features):
        tokens = tokens.reshape(8, -1)
        counts = [jnp.sum((tokens == b).astype(F32), axis=1, keepdims=True) for b in range(4)]
        counts = jnp.concatenate(counts + [jnp.zeros((8, 124), F32)], axis=1)
        return jnp.concatenate([features, counts.astype(BF16)], axis=1)

    span = 8 * (bases.shape[1] // rows)
    edge_prev = ahead(edge(bases[0, bases.shape[1] - span :], skip[rows - 8 :]))
    edge_next = behind(edge(bases[0, :span], skip[:8]))
    w_rows = gather_in_x(w_query, w_kv)
    out_home = moved(w_out, lambda z, y, c, x: (y, x, c, z))
    beside = lax.ppermute(after(cot, w_rows), "x", [(i, i ^ 1) for i in range(4)])
    across = lax.ppermute(jnp.stack([cot, beside]), "x", [(i, 3 - i) for i in range(4)])
    pieces = around(w_rows, "y")
    out_rows = gathered(out_home, "y").reshape(48, width)
    side = width // 3
    joint = jnp.concatenate(
        [piece[:, :side] for piece in pieces]
        + [out_rows[:, p * side : (p + 1) * side] for p in range(3)]
        + [
            jnp.concatenate(
                [jnp.pad(piece[:, side:], ((0, 0), (0, 64))) for piece in pieces], axis=1
            )
        ],
        axis=0,
    )
    near = jnp.stack(around(joint, "z"))

    gain = conv_gain[None, :]
    pooled, normed = front(
        ends, cells, skip, edge_prev, edge_next, base_table, gain, attn_gain[None, :], conv_weight
    )
    norms = around(normed)
    far = flipped(after(near, normed, across))

    spot = [seq, lax.axis_index("c"), lax.axis_index("z"), lax.axis_index("y")]
    spot = jnp.stack(spot).astype(jnp.int32)
    d_in, heads, normed_all, cot_all, full_out, *d_parts = attend(spot, norms, (cot, beside, across), near, far)
    d_parts[1:] = [turned(d_parts[k], "x", k) for k in range(1, 4)]
    own, other = grads(spot, normed_all, d_in, heads, cot_all)
    mine = (own.astype(F32) + flipped(other).astype(F32)).astype(BF16)
    out_parts = mix(spot, after(heads, mine), full_out)
    d_normed = d_parts[0]
    for k in range(1, 4):
        d_normed = d_normed + after(d_parts[k], mine).astype(F32)
    mine = returned_along(mine, "z")

    d_pooled = cot.astype(F32) + rms_back(pooled, attn_gain, d_normed)
    grad = (d_pooled * 0.5).astype(BF16)
    grad_prev, grad_next = ahead(grad[half - 16 :]), behind(grad[:16])
    coarse = (pooled + returned(after(out_parts, grad_prev))).astype(BF16)
    skip_grad = back(cells, skip, base_table, gain, grad, grad_prev, grad_next, conv_weight)

    factor = 1.0 / 32
    mine = summed(split_rows(mine), "y")
    cols = w_query.shape[1] // 4
    grad_query, grad_kv, grad_out = finish(mine, cols, width)
    return (
        coarse[None],
        skip_grad[None],
        grad_query * factor,
        grad_kv * factor,
        grad_out * factor,
    )


def solution(mesh):
    inner = Mesh(mesh.devices.reshape(SIZES), AXES)
    dp = ("z", "y", "c")
    every = AXES
    placed = (
        P(dp, "x"),
        P(dp, "x", None),
        P(),
        P(),
        P(),
        P(),
        P(every, None),
        P(every, None),
        P(every, None),
        P(dp, "x", None),
    )
    return jax.shard_map(
        per_device,
        mesh=inner,
        in_specs=placed,
        out_specs=(
            P(dp, "x", None),
            P(dp, "x", None),
            P(every, None),
            P(every, None),
            P(every, None),
        ),
        check_vma=False,
    )
```

```python
import jax
import jax.numpy as jnp
from jax import lax
from jax.experimental import pallas as pl
from jax.experimental.pallas import tpu as pltpu
from jax.sharding import Mesh
from jax.sharding import PartitionSpec as P

HQ = 8
HD = 128
VD = 192
VMEM_LIMIT = 60 * 1024 * 1024
F32 = jnp.float32
BF16 = jnp.bfloat16


def ndot(left, right):
    return lax.dot_general(
        left, right, (((1,), (0,)), ((), ())), preferred_element_type=F32
    )


def rdot(left, right):
    return lax.dot_general(
        left, right, (((1,), (1,)), ((), ())), preferred_element_type=F32
    )


def tdot(left, right):
    return lax.dot_general(
        left, right, (((0,), (0,)), ((), ())), preferred_element_type=F32
    )


def embed_counts(counts, skip, table):
    state = skip.astype(F32)
    for base in range(4):
        state = state + ((counts[base] - 16.0) * 0.25) * table[base : base + 1, :]
    return state


def embed_rows(cells, skip, table):
    counts = [jnp.sum((cells == base).astype(F32), axis=1, keepdims=True) for base in range(4)]
    return embed_counts(counts, skip, table)


def row_scale(value):
    return lax.rsqrt(jnp.mean(value * value, axis=-1, keepdims=True) + 1e-06)


def front_kernel(
    ends, cells, skip, edge_prev, edge_next, table, gain, attn_gain,
    weight, pooled, normed, state_buf, active_buf, lhs, weight_buf, arrived,
):
    rows = skip.shape[0]
    half = rows // 2
    width = skip.shape[1]
    steps, _, _, block = weight_buf.shape

    def fetch(step):
        cols = pl.ds(pl.multiple_of(step * block, block), block)
        return pltpu.make_async_copy(weight.at[:, :, cols], weight_buf.at[step], arrived.at[step])

    for step in range(steps):
        fetch(step).start()

    def rows_in(state, at, keep):
        pre = state * row_scale(state) * gain[...]
        active = 0.5 * pre * (1.0 + lax.erf(pre * 0.7071067811865476))
        active = active.astype(BF16).astype(F32)
        if keep is not None:
            active = jnp.where(keep > 0, active, 0.0)
        count = state.shape[0]
        for tile in range(skip.shape[1] // 128):
            lanes = slice(tile * 128, (tile + 1) * 128)
            state_buf[tile, pl.ds(at, count), :] = state[:, lanes]
            active_buf[tile, pl.ds(at, count), :] = active[:, lanes]

    def edge_rows(edge):
        counts = [edge[:, width + base : width + base + 1].astype(F32) for base in range(4)]
        return embed_counts(counts, edge[:, 0:width], table)

    rows_in(edge_rows(edge_prev), 0, ends[0])
    rows_in(edge_rows(edge_next), rows + 8, ends[1])

    chunk = 64

    def one(i, carry):
        at = pl.multiple_of(i * chunk, chunk)
        state = embed_rows(cells[pl.ds(at, chunk), :], skip[pl.ds(at, chunk), :], table)
        rows_in(state, pl.multiple_of(at + 8, 8), None)
        return carry

    lax.fori_loop(0, rows // chunk, one, 0)
    for tile in range(width // 128):
        cols = slice(tile * 128, (tile + 1) * 128)
        part = [active_buf[tile, pl.ds(6 + j, half, 2), :] for j in range(6)]
        for k in range(5):
            lhs[k, :, cols] = ((part[k] + part[k + 1]) * 0.5).astype(BF16)
        pooled[:, cols] = (
            state_buf[tile, pl.ds(8, half, 2), :] + state_buf[tile, pl.ds(9, half, 2), :]
        ) * 0.5

    def one_block(step, carry):
        fetch(step).wait()
        total = ndot(lhs[0], weight_buf[step, 0])
        for k in range(1, 5):
            total = total + ndot(lhs[k], weight_buf[step, k])
        cols = pl.ds(pl.multiple_of(step * block, block), block)
        pooled[:, cols] = pooled[:, cols] + total
        return carry

    lax.fori_loop(0, steps, one_block, 0)

    def finish_rows(i, carry):
        rows_at = pl.ds(pl.multiple_of(i * 64, 64), 64)
        value = pooled[rows_at, :]
        normed[rows_at, :] = (value * row_scale(value) * attn_gain[...]).astype(BF16)
        return carry

    lax.fori_loop(0, half // 64, finish_rows, 0)


def front(ends, cells, skip, edge_prev, edge_next, table, gain, attn_gain, weight, block=256):
    rows, width = skip.shape
    half = rows // 2
    whole = lambda array: pl.BlockSpec(array.shape, lambda n, s: (0,) * array.ndim)
    small = (cells, skip, edge_prev, edge_next, table, gain, attn_gain)
    return pl.pallas_call(
        front_kernel,
        grid_spec=pltpu.PrefetchScalarGridSpec(
            num_scalar_prefetch=1,
            grid=(1,),
            in_specs=[whole(a) for a in small] + [pl.BlockSpec(memory_space=pl.ANY)],
            out_specs=[
                pl.BlockSpec((half, width), lambda n, s: (0, 0)),
                pl.BlockSpec((half, width), lambda n, s: (0, 0)),
            ],
            scratch_shapes=[
                pltpu.VMEM((width // 128, rows + 16, 128), F32),
                pltpu.VMEM((width // 128, rows + 16, 128), F32),
                pltpu.VMEM((5, half, width), BF16),
                pltpu.VMEM((width // block, 5, width, block), BF16),
                pltpu.SemaphoreType.DMA((width // block,)),
            ],
        ),
        out_shape=[
            jax.ShapeDtypeStruct((half, width), F32),
            jax.ShapeDtypeStruct((half, width), BF16),
        ],
        compiler_params=pltpu.CompilerParams(vmem_limit_bytes=VMEM_LIMIT),
        cost_estimate=pl.CostEstimate(
            flops=2 * half * 5 * width * width, bytes_accessed=10 * width * width + 8 * rows * width, transcendentals=rows * width
        ),
        name="front",
    )(ends, *small, weight)


def back_kernel(
    cells, skip, table, gain, grad, grad_prev, grad_next, weight, out,
    state_buf, scaled_buf, grad_buf, turned_buf, level_buf, scale_buf, sum_buf, weight_buf, arrived,
):
    rows, width = skip.shape
    half = rows // 2
    steps, _, block, _ = weight_buf.shape
    chunk = 64

    def fetch(step):
        at = pl.ds(pl.multiple_of(step * block, block), block)
        return pltpu.make_async_copy(weight.at[:, at, :], weight_buf.at[step], arrived.at[step])

    for step in range(steps):
        fetch(step).start()

    grad_buf[pl.ds(0, 16), :] = grad_prev[...].astype(F32)
    grad_buf[pl.ds(16, half), :] = grad[...].astype(F32)
    grad_buf[pl.ds(half + 16, 16), :] = grad_next[...].astype(F32)
    for tile in range(width // 128):
        lanes = slice(tile * 128, (tile + 1) * 128)
        before, here, later = [
            grad_buf[pl.ds(15 + shift, half), lanes].T.astype(BF16) for shift in range(3)
        ]
        pairs = ((later, later), (here, later), (here, here), (before, here), (before, before))
        for tap, (even, odd) in enumerate(pairs):
            turned_buf[tap, lanes, 0:half] = even
            turned_buf[tap, lanes, half:rows] = odd

    def one(i, carry):
        at = pl.ds(pl.multiple_of(i * chunk, chunk), chunk)
        state = embed_rows(cells[at, :], skip[at, :], table)
        state_buf[at, :] = state
        scale_buf[at, :] = row_scale(state)
        return carry

    lax.fori_loop(0, rows // chunk, one, 0, unroll=2)
    sum_buf[...] = jnp.zeros_like(sum_buf)

    def one_block(step, carry):
        fetch(step).wait()
        total = None
        for k in range(5):
            part = ndot(weight_buf[step, k], turned_buf[k])
            total = part if total is None else total + part
        for tile in range(block // 128):
            level = total[tile * 128 : (tile + 1) * 128, :].T
            level_buf[tile, pl.ds(0, half, 2), :] = level[0:half]
            level_buf[tile, pl.ds(1, half, 2), :] = level[half:]
        cols = pl.ds(pl.multiple_of(step * block, block), block)

        def two(i, carry):
            at = pl.ds(pl.multiple_of(i * 256, 256), 256)
            state = state_buf[at, cols]
            pre = state * scale_buf[at, :] * gain[:, cols]
            slope = 0.5 * (1.0 + lax.erf(pre * 0.7071067811865476)) + pre * jnp.exp(
                -0.5 * pre * pre
            ) * 0.3989422804014327
            level = jnp.concatenate([level_buf[t, at, :] for t in range(block // 128)], axis=1)
            scaled = slope * level * gain[:, cols]
            scaled_buf[at, cols] = scaled
            product = state * scaled
            folded = product[:, 0:128]
            for tile in range(1, block // 128):
                folded = folded + product[:, tile * 128 : (tile + 1) * 128]
            sum_buf[at, :] = sum_buf[at, :] + folded
            return carry

        lax.fori_loop(0, rows // 256, two, 0)
        return carry

    lax.fori_loop(0, steps, one_block, 0)

    scale = scale_buf[...]
    coef = (scale * scale * scale) * (jnp.sum(sum_buf[...], axis=1, keepdims=True) * (1.0 / width))
    for tile in range(width // 128):
        lanes = slice(tile * 128, (tile + 1) * 128)
        own = grad_buf[pl.ds(16, half), lanes]
        scaled = scaled_buf[:, lanes]
        state = state_buf[:, lanes]
        level_buf[0, pl.ds(0, half, 2), :] = own
        level_buf[0, pl.ds(1, half, 2), :] = own
        out[:, lanes] = (level_buf[0] + (scale * scaled - state * coef)).astype(BF16)


def back(cells, skip, table, gain, grad, grad_prev, grad_next, weight, block=256):
    rows, width = skip.shape
    half = rows // 2
    whole = lambda array: pl.BlockSpec(array.shape, lambda n: (0,) * array.ndim)
    small = (cells, skip, table, gain, grad, grad_prev, grad_next)
    return pl.pallas_call(
        back_kernel,
        grid=(1,),
        in_specs=[whole(a) for a in small] + [pl.BlockSpec(memory_space=pl.ANY)],
        out_specs=pl.BlockSpec((rows, width), lambda n: (0, 0)),
        scratch_shapes=[
            pltpu.VMEM((rows, width), F32),
            pltpu.VMEM((rows, width), F32),
            pltpu.VMEM((half + 32, width), F32),
            pltpu.VMEM((5, width, rows), BF16),
            pltpu.VMEM((block // 128, rows, 128), F32),
            pltpu.VMEM((rows, 1), F32),
            pltpu.VMEM((rows, 128), F32),
            pltpu.VMEM((width // block, 5, block, width), BF16),
            pltpu.SemaphoreType.DMA((width // block,)),
        ],
        out_shape=jax.ShapeDtypeStruct((rows, width), BF16),
        compiler_params=pltpu.CompilerParams(vmem_limit_bytes=VMEM_LIMIT),
        cost_estimate=pl.CostEstimate(
            flops=2 * half * 5 * width * width, bytes_accessed=10 * width * width + 8 * rows * width, transcendentals=2 * rows * width
        ),
        name="back",
    )(*small, weight)


def attend_kernel(
    place, norm0, norm1, norm2, norm3, cot0, cot1, cot2, near, far,
    d_in, heads, normed, cot, w_out, own, part1, part2, part3, w_in, query_kv, acc,
):
    head = pl.program_id(0)
    seq, core, depth, level = place[0], place[1], place[2], place[3]
    inv = 1.0 / HD**0.5
    half = own.shape[0]
    cols = w_in.shape[1]
    side = near.shape[2]
    first = cols - side + HD

    def rows_of(index):
        return pl.ds(pl.multiple_of(index * half, half), half)

    @pl.when(head == 0)
    def _():
        for source, side_core in ((near, core), (far, 1 - core)):
            for turn in range(4):
                z = lax.rem(depth + turn, 4)
                for other in range(4):
                    y = lax.rem(level + other, 4)
                    at = pl.ds(pl.multiple_of((z * 4 + y) * 96 + side_core * 48, 16), 48)
                    w_in[at, 0:side] = source[turn, other * 48 : (other + 1) * 48, :]
                    w_in[at, side:cols] = source[turn, 336:384, other * 128 : (other + 1) * 128]
                at = pl.ds(pl.multiple_of(z * 96 + side_core * 48, 16), 48)
                for b in range(3):
                    w_out[at, b * side : (b + 1) * side] = source[
                        turn, 192 + b * 48 : 240 + b * 48, :
                    ]
        for piece, value in enumerate((norm0, norm1, norm2, norm3)):
            normed[rows_of(lax.rem(seq + piece, 4)), :] = value[...]
        beside = seq + 1 - 2 * lax.rem(seq, 2)
        cot[rows_of(seq), :] = cot0[...]
        cot[rows_of(beside), :] = cot1[...]
        cot[rows_of(3 - seq), :] = cot2[0]
        cot[rows_of(3 - beside), :] = cot2[1]
        query_kv[...] = ndot(normed[...], w_in[...]).astype(BF16)

    keys = query_kv[:, first : first + HD]
    values = query_kv[:, first + HD : first + HD + VD]
    lanes = pl.ds(pl.multiple_of(head * HD, HD), HD)
    q = query_kv[:, lanes]
    d_heads = rdot(cot[...], w_out[pl.ds(pl.multiple_of(head * VD, VD), VD), :]).astype(BF16)
    scores = rdot(q, keys) * inv
    expo = jnp.exp(scores - jnp.max(scores, axis=1, keepdims=True))
    probs = expo * (1.0 / jnp.sum(expo, axis=1, keepdims=True))
    weights = probs.astype(BF16)
    heads[0] = ndot(weights, values).astype(BF16)
    d_probs = rdot(d_heads, values)
    inner = jnp.sum(probs * d_probs, axis=1, keepdims=True)
    d_scores = (probs * (d_probs - inner) * inv).astype(BF16)
    d_in[:, lanes] = ndot(d_scores, keys).astype(BF16)
    d_keys = tdot(d_scores, q)
    d_values = tdot(weights, d_heads)

    @pl.when(head == 0)
    def _():
        acc[:, 0:HD] = d_keys
        acc[:, HD : HD + VD] = d_values

    @pl.when(head > 0)
    def _():
        acc[:, 0:HD] += d_keys
        acc[:, HD : HD + VD] += d_values

    @pl.when(head == pl.num_programs(0) - 1)
    def _():
        d_in[:, first + HD :] = jnp.zeros((4 * half, cols - first - HD), BF16)
        d_in[:, first : first + HD + VD] = acc[...].astype(BF16)
        for piece, out in enumerate((own, part1, part2, part3)):
            rows = d_in[rows_of(lax.rem(seq + piece, 4)), :]
            out[...] = rdot(rows, w_in[...]).astype(out.dtype)


def attend(place, norms, cots, near, far):
    half, width = norms[0].shape
    rows = 4 * half
    cols = near.shape[2] + 128
    heads = 2
    whole = lambda array: pl.BlockSpec(array.shape, lambda h, s: (0,) * array.ndim)
    outs = [
        jax.ShapeDtypeStruct((rows, cols), BF16),
        jax.ShapeDtypeStruct((heads, rows, VD), BF16),
        jax.ShapeDtypeStruct((rows, width), BF16),
        jax.ShapeDtypeStruct((rows, width), BF16),
        jax.ShapeDtypeStruct((heads * VD, width), BF16),
        jax.ShapeDtypeStruct((half, width), F32),
    ] + [jax.ShapeDtypeStruct((half, width), BF16)] * 3
    specs = [whole(out) for out in outs]
    specs[1] = pl.BlockSpec((1, rows, VD), lambda h, s: (h, 0, 0))
    ins = (*norms, *cots, near, far)
    return pl.pallas_call(
        attend_kernel,
        grid_spec=pltpu.PrefetchScalarGridSpec(
            num_scalar_prefetch=1,
            grid=(heads,),
            in_specs=[whole(a) for a in ins],
            out_specs=specs,
            scratch_shapes=[
                pltpu.VMEM((width, cols), BF16),
                pltpu.VMEM((rows, cols), BF16),
                pltpu.VMEM((rows, HD + VD), F32),
            ],
        ),
        out_shape=outs,
        compiler_params=pltpu.CompilerParams(vmem_limit_bytes=VMEM_LIMIT),
        cost_estimate=pl.CostEstimate(
            flops=2 * rows * heads * (VD * width + 3 * rows * (HD + VD)) + 4 * rows * cols * width,
            bytes_accessed=8 * rows * width + 2 * heads * VD * width + 2 * cols * width,
            transcendentals=rows * heads * rows,
        ),
        name="attend",
    )(place, *ins)


def grads_kernel(place, normed, d_in, heads, cot, own, other, rows_in, rows_out):
    core, depth = place[1], place[2]
    width = cot.shape[1]
    cols = d_in.shape[1]
    side = width // 2
    blocks = rows_in.shape[1] // 128
    for turn, out in enumerate((other, own)):
        half = core if turn else 1 - core
        lanes = pl.ds(pl.multiple_of(half * side, side), side)
        rows_in[:, 0:cols] = tdot(normed[:, lanes], d_in[...]).astype(BF16)
        rows_out[...] = tdot(heads[half], cot[...]).astype(BF16)
        for k in range(4):
            quarter = lax.rem(depth + k, 4)
            count = side // 4
            at = pl.ds(pl.multiple_of(quarter * count, count), count)
            for b in range(blocks):
                out[k, b * count : (b + 1) * count, :] = rows_in[at, b * 128 : (b + 1) * 128]
            base = blocks * count
            count = VD // 4
            at = pl.ds(pl.multiple_of(quarter * count, count), count)
            for b in range(width // 128):
                out[k, base + b * count : base + (b + 1) * count, :] = rows_out[
                    at, b * 128 : (b + 1) * 128
                ]


def grads(place, normed, d_in, heads, cot):
    rows, width = cot.shape
    cols = d_in.shape[1]
    blocks = (cols + 127) // 128
    length = blocks * (width // 8) + width // 128 * (VD // 4)
    whole = lambda array: pl.BlockSpec(array.shape, lambda n, s: (0,) * array.ndim)
    outs = [jax.ShapeDtypeStruct((4, length, 128), BF16)] * 2
    ins = (normed, d_in, heads, cot)
    return pl.pallas_call(
        grads_kernel,
        grid_spec=pltpu.PrefetchScalarGridSpec(
            num_scalar_prefetch=1,
            grid=(1,),
            in_specs=[whole(a) for a in ins],
            out_specs=[whole(a) for a in outs],
            scratch_shapes=[
                pltpu.VMEM((width // 2, blocks * 128), BF16),
                pltpu.VMEM((VD, width), BF16),
            ],
        ),
        out_shape=outs,
        compiler_params=pltpu.CompilerParams(vmem_limit_bytes=VMEM_LIMIT),
        cost_estimate=pl.CostEstimate(
            flops=2 * rows * width * (cols + 2 * VD),
            bytes_accessed=16 * rows * width,
            transcendentals=0,
        ),
        name="grads",
    )(place, *ins)


def mix_kernel(place, heads, w_out, out):
    total = ndot(heads[0], w_out[0:VD, :]) + ndot(heads[1], w_out[VD : 2 * VD, :])
    out[0] = total.astype(BF16)


def mix(place, heads, w_out):
    rows = heads.shape[1] // 4
    width = w_out.shape[1]
    return pl.pallas_call(
        mix_kernel,
        grid_spec=pltpu.PrefetchScalarGridSpec(
            num_scalar_prefetch=1,
            grid=(4,),
            in_specs=[
                pl.BlockSpec((2, rows, VD), lambda n, s: (0, lax.rem(s[0] + n, 4), 0)),
                pl.BlockSpec(w_out.shape, lambda n, s: (0, 0)),
            ],
            out_specs=pl.BlockSpec((1, rows, width), lambda n, s: (n, 0, 0)),
        ),
        out_shape=jax.ShapeDtypeStruct((4, rows, width), BF16),
        compiler_params=pltpu.CompilerParams(vmem_limit_bytes=VMEM_LIMIT),
        cost_estimate=pl.CostEstimate(
            flops=16 * rows * width * VD, bytes_accessed=12 * rows * width, transcendentals=0
        ),
        name="mix",
    )(place, heads, w_out)


AXES = ("z", "y", "c", "x")
SIZES = (4, 4, 2, 4)


def place(z, y, c, x):
    return ((z * 4 + y) * 2 + c) * 4 + x


def moved(value, target):
    pairs = []
    for z in range(4):
        for y in range(4):
            for c in range(2):
                for x in range(4):
                    pairs.append((place(z, y, c, x), place(*target(z, y, c, x))))
    return lax.ppermute(value, AXES, pairs)


def flipped(value):
    return moved(value, lambda z, y, c, x: (z, y, 1 - c, x))


def turned(value, axis, by):
    return lax.ppermute(value, axis, [(i, (i + by) % 4) for i in range(4)])


def gathered(value, axis):
    me = lax.axis_index(axis)
    parts = [value, turned(value, axis, 3), turned(value, axis, 2), turned(value, axis, 1)]
    out = jnp.zeros((4, *value.shape), value.dtype)
    for j in range(4):
        out = lax.dynamic_update_index_in_dim(out, parts[j], lax.rem(me + j, 4), 0)
    return out


def summed(value, axis, dtype=BF16):
    me = lax.axis_index(axis)
    parts = [
        lax.dynamic_index_in_dim(value, lax.rem(me + j, 4), 0, keepdims=False) for j in range(4)
    ]
    total = parts[0].astype(F32)
    for j in range(1, 4):
        total = total + turned(parts[j], axis, j).astype(F32)
    return total.astype(dtype)


def by_core(own, other):
    first = lax.axis_index("c") == 0
    return jnp.where(first, own, other), jnp.where(first, other, own)


def around(value, axis="x"):
    return [value, turned(value, axis, 3), turned(value, axis, 2), turned(value, axis, 1)]


def returned(pieces):
    total = pieces[0].astype(F32)
    for k in range(1, 4):
        total = total + turned(pieces[k], "x", k).astype(F32)
    return total


def gather_in_x(w_query, w_kv):
    seq = lax.axis_index("x")
    cols = w_query.shape[1] // 4
    rows = jnp.zeros((4, w_query.shape[0], cols + w_kv.shape[1]), BF16)
    for k in range(4):
        head_cols = lax.dynamic_slice_in_dim(w_query, lax.rem(seq + k, 4) * cols, cols, 1)
        piece = jnp.concatenate([head_cols, w_kv], axis=1)
        if k:
            piece = turned(piece, "x", k)
        rows = lax.dynamic_update_index_in_dim(rows, piece, lax.rem(seq + 4 - k, 4), 0)
    return rows.reshape(48, rows.shape[2])


def after(value, *others):
    return lax.optimization_barrier((value, *others))[0]


def split_rows(pieces):
    first = pieces[:960].reshape(5, 4, 48, 128).transpose(1, 0, 2, 3).reshape(4, 240, 128)
    second = pieces[960:].reshape(12, 4, 12, 128).transpose(1, 0, 2, 3).reshape(4, 144, 128)
    return jnp.concatenate([first, second], axis=1)


def finish(value, cols, width):
    seq = lax.axis_index("x")
    pieces = value[:240].reshape(5, 4, 12, 128).transpose(1, 2, 0, 3).reshape(4, 12, 640)
    grad_query = jnp.zeros((4, 12, cols), F32)
    grad_kv = jnp.zeros((12, HD + VD), F32)
    for k in range(4):

        def home(z, y, c, x):
            block = 16 * c + 4 * z + y
            return block // 8, block // 2 % 4, block % 2, (x + k) % 4

        piece = lax.dynamic_index_in_dim(pieces, lax.rem(seq + k, 4), 0, keepdims=False)
        piece = moved(piece, home).astype(F32)
        grad_query = lax.dynamic_update_index_in_dim(
            grad_query, piece[:, :cols], lax.rem(seq + 4 - k, 4), 0
        )
        grad_kv = grad_kv + piece[:, cols : cols + HD + VD]
    grad_query = grad_query.transpose(1, 0, 2).reshape(12, 4 * cols)
    grad_out = value[240:].reshape(12, 12, 128).transpose(1, 0, 2).reshape(12, width)
    grad_out = moved(grad_out, lambda z, y, c, x: (x, 2 * c + z // 2, z % 2, y)).astype(F32)
    return grad_query, grad_kv, grad_out


def rms_back(value, gain, grad):
    scale = row_scale(value)
    scaled = grad * gain
    return scale * scaled - value * (scale * scale * scale) * jnp.mean(
        value * scaled, axis=-1, keepdims=True
    )


def per_device(
    bases, skip, base_table, conv_weight, conv_gain, attn_gain, w_query, w_kv, w_out, cotangent
):
    skip = skip[0]
    cot = cotangent[0]
    rows, width = skip.shape
    half = rows // 2
    cells = bases.reshape(rows, bases.shape[1] // rows)
    seq = lax.axis_index("x")
    ends = jnp.stack([seq, 3 - seq]).astype(jnp.int32)

    def ahead(value):
        return lax.ppermute(value, "x", [(i, i + 1) for i in range(3)])

    def behind(value):
        return lax.ppermute(value, "x", [(i + 1, i) for i in range(3)])

    def edge(tokens, features):
        tokens = tokens.reshape(8, -1)
        counts = [jnp.sum((tokens == b).astype(F32), axis=1, keepdims=True) for b in range(4)]
        counts = jnp.concatenate(counts + [jnp.zeros((8, 124), F32)], axis=1)
        return jnp.concatenate([features, counts.astype(BF16)], axis=1)

    span = 8 * (bases.shape[1] // rows)
    edge_prev = ahead(edge(bases[0, bases.shape[1] - span :], skip[rows - 8 :]))
    edge_next = behind(edge(bases[0, :span], skip[:8]))
    w_rows = gather_in_x(w_query, w_kv)
    out_home = moved(w_out, lambda z, y, c, x: (y, x, c, z))
    beside = lax.ppermute(cot, "x", [(i, i ^ 1) for i in range(4)])
    across = lax.ppermute(jnp.stack([cot, beside]), "x", [(i, 3 - i) for i in range(4)])
    pieces = around(w_rows, "y")
    out_rows = gathered(out_home, "y").reshape(48, width)
    side = width // 3
    joint = jnp.concatenate(
        [piece[:, :side] for piece in pieces]
        + [out_rows[:, p * side : (p + 1) * side] for p in range(3)]
        + [
            jnp.concatenate(
                [jnp.pad(piece[:, side:], ((0, 0), (0, 64))) for piece in pieces], axis=1
            )
        ],
        axis=0,
    )
    edge_next = after(edge_next, beside, out_home)
    gain = conv_gain[None, :]
    pooled, normed = front(
        ends, cells, skip, edge_prev, edge_next, base_table, gain, attn_gain[None, :], conv_weight
    )
    norms = around(normed)
    joint = after(joint, normed, across)
    near = jnp.stack(around(joint, "z"))
    far = flipped(after(near, *norms))

    spot = [seq, lax.axis_index("c"), lax.axis_index("z"), lax.axis_index("y")]
    spot = jnp.stack(spot).astype(jnp.int32)
    d_in, heads, normed_all, cot_all, full_out, *d_parts = attend(spot, norms, (cot, beside, across), near, far)
    d_parts[1:] = [turned(d_parts[k], "x", k) for k in range(1, 4)]
    own, other = grads(spot, normed_all, d_in, heads, cot_all)
    out_parts = mix(spot, heads, full_out)
    mine = (own.astype(F32) + flipped(other).astype(F32)).astype(BF16)
    total = mine[0].astype(F32)
    for k in range(1, 4):
        total = total + turned(mine[k], "z", k).astype(F32)
    mine = total.astype(BF16)
    d_normed = d_parts[0]
    for k in range(1, 4):
        d_normed = d_normed + after(d_parts[k], mine).astype(F32)
    mine = summed(split_rows(mine), "y")

    d_pooled = cot.astype(F32) + rms_back(pooled, attn_gain, d_normed)
    grad = (d_pooled * 0.5).astype(BF16)
    grad_prev, grad_next = ahead(grad[half - 16 :]), behind(grad[:16])
    grad_next = after(grad_next, mine)
    coarse = (pooled + returned(after(out_parts, grad_prev))).astype(BF16)
    skip_grad = back(cells, skip, base_table, gain, grad, grad_prev, grad_next, conv_weight)

    factor = 1.0 / 32
    cols = w_query.shape[1] // 4
    grad_query, grad_kv, grad_out = finish(mine, cols, width)
    return (
        coarse[None],
        skip_grad[None],
        grad_query * factor,
        grad_kv * factor,
        grad_out * factor,
    )


def solution(mesh):
    inner = Mesh(mesh.devices.reshape(SIZES), AXES)
    dp = ("z", "y", "c")
    every = AXES
    placed = (
        P(dp, "x"),
        P(dp, "x", None),
        P(),
        P(),
        P(),
        P(),
        P(every, None),
        P(every, None),
        P(every, None),
        P(dp, "x", None),
    )
    return jax.shard_map(
        per_device,
        mesh=inner,
        in_specs=placed,
        out_specs=(
            P(dp, "x", None),
            P(dp, "x", None),
            P(every, None),
            P(every, None),
            P(every, None),
        ),
        check_vma=False,
    )
```

```python
import jax
import jax.numpy as jnp
from jax import lax
from jax.experimental import pallas as pl
from jax.experimental.pallas import tpu as pltpu
from jax.sharding import Mesh
from jax.sharding import PartitionSpec as P

HQ = 8
HD = 128
VD = 192
VMEM_LIMIT = 60 * 1024 * 1024
F32 = jnp.float32
BF16 = jnp.bfloat16


def ndot(left, right):
    return lax.dot_general(
        left, right, (((1,), (0,)), ((), ())), preferred_element_type=F32
    )


def rdot(left, right):
    return lax.dot_general(
        left, right, (((1,), (1,)), ((), ())), preferred_element_type=F32
    )


def tdot(left, right):
    return lax.dot_general(
        left, right, (((0,), (0,)), ((), ())), preferred_element_type=F32
    )


def embed_counts(counts, skip, table):
    state = skip.astype(F32)
    for base in range(4):
        state = state + ((counts[base] - 16.0) * 0.25) * table[base : base + 1, :]
    return state


def embed_rows(cells, skip, table):
    counts = [jnp.sum((cells == base).astype(F32), axis=1, keepdims=True) for base in range(4)]
    return embed_counts(counts, skip, table)


def row_scale(value):
    return lax.rsqrt(jnp.mean(value * value, axis=-1, keepdims=True) + 1e-06)


def front_kernel(
    ends, cells, skip, edge_prev, edge_next, table,
    weight, pooled, normed, state_buf, active_buf, lhs, weight_buf, arrived,
):
    gain, attn_gain = table.at[4:5], table.at[5:6]
    rows = skip.shape[0]
    half = rows // 2
    width = skip.shape[1]
    steps, _, _, block = weight_buf.shape

    def fetch(step):
        cols = pl.ds(pl.multiple_of(step * block, block), block)
        return pltpu.make_async_copy(weight.at[:, :, cols], weight_buf.at[step], arrived.at[step])

    for step in range(steps):
        fetch(step).start()

    def rows_in(state, at, keep):
        pre = state * row_scale(state) * gain[...]
        active = 0.5 * pre * (1.0 + lax.erf(pre * 0.7071067811865476))
        active = active.astype(BF16).astype(F32)
        if keep is not None:
            active = jnp.where(keep > 0, active, 0.0)
        count = state.shape[0]
        for tile in range(skip.shape[1] // 128):
            lanes = slice(tile * 128, (tile + 1) * 128)
            state_buf[tile, pl.ds(at, count), :] = state[:, lanes]
            active_buf[tile, pl.ds(at, count), :] = active[:, lanes]

    def edge_rows(edge):
        counts = [edge[:, width + base : width + base + 1].astype(F32) for base in range(4)]
        return embed_counts(counts, edge[:, 0:width], table)

    rows_in(edge_rows(edge_prev), 0, ends[0])
    rows_in(edge_rows(edge_next), rows + 8, ends[1])

    chunk = 64

    def one(i, carry):
        at = pl.multiple_of(i * chunk, chunk)
        state = embed_rows(cells[pl.ds(at, chunk), :], skip[pl.ds(at, chunk), :], table)
        rows_in(state, pl.multiple_of(at + 8, 8), None)
        return carry

    lax.fori_loop(0, rows // chunk, one, 0)
    for tile in range(width // 128):
        cols = slice(tile * 128, (tile + 1) * 128)
        part = [active_buf[tile, pl.ds(6 + j, half, 2), :] for j in range(6)]
        for k in range(5):
            lhs[k, :, cols] = ((part[k] + part[k + 1]) * 0.5).astype(BF16)
        pooled[:, cols] = (
            state_buf[tile, pl.ds(8, half, 2), :] + state_buf[tile, pl.ds(9, half, 2), :]
        ) * 0.5

    def one_block(step, carry):
        fetch(step).wait()
        total = ndot(lhs[0], weight_buf[step, 0])
        for k in range(1, 5):
            total = total + ndot(lhs[k], weight_buf[step, k])
        cols = pl.ds(pl.multiple_of(step * block, block), block)
        pooled[:, cols] = pooled[:, cols] + total
        return carry

    lax.fori_loop(0, steps, one_block, 0)

    def finish_rows(i, carry):
        rows_at = pl.ds(pl.multiple_of(i * 64, 64), 64)
        value = pooled[rows_at, :]
        normed[rows_at, :] = (value * row_scale(value) * attn_gain[...]).astype(BF16)
        return carry

    lax.fori_loop(0, half // 64, finish_rows, 0)


def front(ends, cells, skip, edge_prev, edge_next, table, weight, block=256):
    rows, width = skip.shape
    half = rows // 2
    whole = lambda array: pl.BlockSpec(array.shape, lambda n, s: (0,) * array.ndim)
    small = (cells, skip, edge_prev, edge_next, table)
    return pl.pallas_call(
        front_kernel,
        grid_spec=pltpu.PrefetchScalarGridSpec(
            num_scalar_prefetch=1,
            grid=(1,),
            in_specs=[whole(a) for a in small] + [pl.BlockSpec(memory_space=pl.ANY)],
            out_specs=[
                pl.BlockSpec((half, width), lambda n, s: (0, 0)),
                pl.BlockSpec((half, width), lambda n, s: (0, 0)),
            ],
            scratch_shapes=[
                pltpu.VMEM((width // 128, rows + 16, 128), F32),
                pltpu.VMEM((width // 128, rows + 16, 128), F32),
                pltpu.VMEM((5, half, width), BF16),
                pltpu.VMEM((width // block, 5, width, block), BF16),
                pltpu.SemaphoreType.DMA((width // block,)),
            ],
        ),
        out_shape=[
            jax.ShapeDtypeStruct((half, width), F32),
            jax.ShapeDtypeStruct((half, width), BF16),
        ],
        compiler_params=pltpu.CompilerParams(vmem_limit_bytes=VMEM_LIMIT),
        cost_estimate=pl.CostEstimate(
            flops=2 * half * 5 * width * width, bytes_accessed=10 * width * width + 8 * rows * width, transcendentals=rows * width
        ),
        name="front",
    )(ends, *small, weight)


def back_kernel(
    cells, skip, table, grad, grad_prev, grad_next, weight, out,
    state_buf, scaled_buf, grad_buf, turned_buf, level_buf, scale_buf, sum_buf, weight_buf, arrived,
):
    gain = table.at[4:5]
    rows, width = skip.shape
    half = rows // 2
    steps, _, block, _ = weight_buf.shape
    chunk = 64

    def fetch(step):
        at = pl.ds(pl.multiple_of(step * block, block), block)
        return pltpu.make_async_copy(weight.at[:, at, :], weight_buf.at[step], arrived.at[step])

    for step in range(steps):
        fetch(step).start()

    grad_buf[pl.ds(0, 16), :] = grad_prev[...].astype(F32)
    grad_buf[pl.ds(16, half), :] = grad[...].astype(F32)
    grad_buf[pl.ds(half + 16, 16), :] = grad_next[...].astype(F32)
    for tile in range(width // 128):
        lanes = slice(tile * 128, (tile + 1) * 128)
        before, here, later = [
            grad_buf[pl.ds(15 + shift, half), lanes].T.astype(BF16) for shift in range(3)
        ]
        pairs = ((later, later), (here, later), (here, here), (before, here), (before, before))
        for tap, (even, odd) in enumerate(pairs):
            turned_buf[tap, lanes, 0:half] = even
            turned_buf[tap, lanes, half:rows] = odd

    def one(i, carry):
        at = pl.ds(pl.multiple_of(i * chunk, chunk), chunk)
        state = embed_rows(cells[at, :], skip[at, :], table)
        state_buf[at, :] = state
        scale_buf[at, :] = row_scale(state)
        return carry

    lax.fori_loop(0, rows // chunk, one, 0, unroll=2)
    sum_buf[...] = jnp.zeros_like(sum_buf)

    def one_block(step, carry):
        fetch(step).wait()
        total = None
        for k in range(5):
            part = ndot(weight_buf[step, k], turned_buf[k])
            total = part if total is None else total + part
        for tile in range(block // 128):
            level = total[tile * 128 : (tile + 1) * 128, :].T
            level_buf[tile, pl.ds(0, half, 2), :] = level[0:half]
            level_buf[tile, pl.ds(1, half, 2), :] = level[half:]
        cols = pl.ds(pl.multiple_of(step * block, block), block)

        def two(i, carry):
            at = pl.ds(pl.multiple_of(i * 256, 256), 256)
            state = state_buf[at, cols]
            pre = state * scale_buf[at, :] * gain[:, cols]
            slope = 0.5 * (1.0 + lax.erf(pre * 0.7071067811865476)) + pre * jnp.exp(
                -0.5 * pre * pre
            ) * 0.3989422804014327
            level = jnp.concatenate([level_buf[t, at, :] for t in range(block // 128)], axis=1)
            scaled = slope * level * gain[:, cols]
            scaled_buf[at, cols] = scaled
            product = state * scaled
            folded = product[:, 0:128]
            for tile in range(1, block // 128):
                folded = folded + product[:, tile * 128 : (tile + 1) * 128]
            sum_buf[at, :] = sum_buf[at, :] + folded
            return carry

        lax.fori_loop(0, rows // 256, two, 0)
        return carry

    lax.fori_loop(0, steps, one_block, 0)

    scale = scale_buf[...]
    coef = (scale * scale * scale) * (jnp.sum(sum_buf[...], axis=1, keepdims=True) * (1.0 / width))
    for tile in range(width // 128):
        lanes = slice(tile * 128, (tile + 1) * 128)
        own = grad_buf[pl.ds(16, half), lanes]
        scaled = scaled_buf[:, lanes]
        state = state_buf[:, lanes]
        level_buf[0, pl.ds(0, half, 2), :] = own
        level_buf[0, pl.ds(1, half, 2), :] = own
        out[:, lanes] = (level_buf[0] + (scale * scaled - state * coef)).astype(BF16)


def back(cells, skip, table, grad, grad_prev, grad_next, weight, block=256):
    rows, width = skip.shape
    half = rows // 2
    whole = lambda array: pl.BlockSpec(array.shape, lambda n: (0,) * array.ndim)
    small = (cells, skip, table, grad, grad_prev, grad_next)
    return pl.pallas_call(
        back_kernel,
        grid=(1,),
        in_specs=[whole(a) for a in small] + [pl.BlockSpec(memory_space=pl.ANY)],
        out_specs=pl.BlockSpec((rows, width), lambda n: (0, 0)),
        scratch_shapes=[
            pltpu.VMEM((rows, width), F32),
            pltpu.VMEM((rows, width), F32),
            pltpu.VMEM((half + 32, width), F32),
            pltpu.VMEM((5, width, rows), BF16),
            pltpu.VMEM((block // 128, rows, 128), F32),
            pltpu.VMEM((rows, 1), F32),
            pltpu.VMEM((rows, 128), F32),
            pltpu.VMEM((width // block, 5, block, width), BF16),
            pltpu.SemaphoreType.DMA((width // block,)),
        ],
        out_shape=jax.ShapeDtypeStruct((rows, width), BF16),
        compiler_params=pltpu.CompilerParams(vmem_limit_bytes=VMEM_LIMIT),
        cost_estimate=pl.CostEstimate(
            flops=2 * half * 5 * width * width, bytes_accessed=10 * width * width + 8 * rows * width, transcendentals=2 * rows * width
        ),
        name="back",
    )(*small, weight)


def attend_kernel(
    place, norm0, norm1, norm2, norm3, cot0, cot1, cot2, near, far,
    d_in, heads, normed, cot, w_out, own, part1, part2, part3, w_in, query_kv, acc,
):
    head = pl.program_id(0)
    seq, core, depth, level = place[0], place[1], place[2], place[3]
    inv = 1.0 / HD**0.5
    half = own.shape[0]
    cols = w_in.shape[1]
    side = near.shape[2]
    first = cols - side + HD

    def rows_of(index):
        return pl.ds(pl.multiple_of(index * half, half), half)

    @pl.when(head == 0)
    def _():
        for source, side_core in ((near, core), (far, 1 - core)):
            for turn in range(4):
                z = lax.rem(depth + turn, 4)
                for other in range(4):
                    y = lax.rem(level + other, 4)
                    at = pl.ds(pl.multiple_of((z * 4 + y) * 96 + side_core * 48, 16), 48)
                    w_in[at, 0:side] = source[turn, other * 48 : (other + 1) * 48, :]
                    w_in[at, side:cols] = source[turn, 336:384, other * 128 : (other + 1) * 128]
                at = pl.ds(pl.multiple_of(z * 96 + side_core * 48, 16), 48)
                for b in range(3):
                    w_out[at, b * side : (b + 1) * side] = source[
                        turn, 192 + b * 48 : 240 + b * 48, :
                    ]
        for piece, value in enumerate((norm0, norm1, norm2, norm3)):
            normed[rows_of(lax.rem(seq + piece, 4)), :] = value[...]
        beside = seq + 1 - 2 * lax.rem(seq, 2)
        cot[rows_of(seq), :] = cot0[...]
        cot[rows_of(beside), :] = cot1[...]
        cot[rows_of(3 - seq), :] = cot2[0]
        cot[rows_of(3 - beside), :] = cot2[1]
        query_kv[...] = ndot(normed[...], w_in[...]).astype(BF16)

    keys = query_kv[:, first : first + HD]
    values = query_kv[:, first + HD : first + HD + VD]
    lanes = pl.ds(pl.multiple_of(head * HD, HD), HD)
    q = query_kv[:, lanes]
    d_heads = rdot(cot[...], w_out[pl.ds(pl.multiple_of(head * VD, VD), VD), :]).astype(BF16)
    scores = rdot(q, keys) * inv
    expo = jnp.exp(scores - jnp.max(scores, axis=1, keepdims=True))
    probs = expo * (1.0 / jnp.sum(expo, axis=1, keepdims=True))
    weights = probs.astype(BF16)
    heads[0] = ndot(weights, values).astype(BF16)
    d_probs = rdot(d_heads, values)
    inner = jnp.sum(probs * d_probs, axis=1, keepdims=True)
    d_scores = (probs * (d_probs - inner) * inv).astype(BF16)
    d_in[:, lanes] = ndot(d_scores, keys).astype(BF16)
    d_keys = tdot(d_scores, q)
    d_values = tdot(weights, d_heads)

    @pl.when(head == 0)
    def _():
        acc[:, 0:HD] = d_keys
        acc[:, HD : HD + VD] = d_values

    @pl.when(head > 0)
    def _():
        acc[:, 0:HD] += d_keys
        acc[:, HD : HD + VD] += d_values

    @pl.when(head == pl.num_programs(0) - 1)
    def _():
        d_in[:, first + HD :] = jnp.zeros((4 * half, cols - first - HD), BF16)
        d_in[:, first : first + HD + VD] = acc[...].astype(BF16)
        for piece, out in enumerate((own, part1, part2, part3)):
            rows = d_in[rows_of(lax.rem(seq + piece, 4)), :]
            out[...] = rdot(rows, w_in[...]).astype(out.dtype)


def attend(place, norms, cots, near, far):
    half, width = norms[0].shape
    rows = 4 * half
    cols = near.shape[2] + 128
    heads = 2
    whole = lambda array: pl.BlockSpec(array.shape, lambda h, s: (0,) * array.ndim)
    outs = [
        jax.ShapeDtypeStruct((rows, cols), BF16),
        jax.ShapeDtypeStruct((heads, rows, VD), BF16),
        jax.ShapeDtypeStruct((rows, width), BF16),
        jax.ShapeDtypeStruct((rows, width), BF16),
        jax.ShapeDtypeStruct((heads * VD, width), BF16),
        jax.ShapeDtypeStruct((half, width), F32),
    ] + [jax.ShapeDtypeStruct((half, width), BF16)] * 3
    specs = [whole(out) for out in outs]
    specs[1] = pl.BlockSpec((1, rows, VD), lambda h, s: (h, 0, 0))
    ins = (*norms, *cots, near, far)
    return pl.pallas_call(
        attend_kernel,
        grid_spec=pltpu.PrefetchScalarGridSpec(
            num_scalar_prefetch=1,
            grid=(heads,),
            in_specs=[whole(a) for a in ins],
            out_specs=specs,
            scratch_shapes=[
                pltpu.VMEM((width, cols), BF16),
                pltpu.VMEM((rows, cols), BF16),
                pltpu.VMEM((rows, HD + VD), F32),
            ],
        ),
        out_shape=outs,
        compiler_params=pltpu.CompilerParams(vmem_limit_bytes=VMEM_LIMIT),
        cost_estimate=pl.CostEstimate(
            flops=2 * rows * heads * (VD * width + 3 * rows * (HD + VD)) + 4 * rows * cols * width,
            bytes_accessed=8 * rows * width + 2 * heads * VD * width + 2 * cols * width,
            transcendentals=rows * heads * rows,
        ),
        name="attend",
    )(place, *ins)


def grads_kernel(place, normed, d_in, heads, cot, own, other, rows_in, rows_out):
    core, depth = place[1], place[2]
    width = cot.shape[1]
    cols = d_in.shape[1]
    side = width // 2
    blocks = rows_in.shape[1] // 128
    for turn, out in enumerate((other, own)):
        half = core if turn else 1 - core
        lanes = pl.ds(pl.multiple_of(half * side, side), side)
        rows_in[:, 0:cols] = tdot(normed[:, lanes], d_in[...]).astype(BF16)
        rows_out[...] = tdot(heads[half], cot[...]).astype(BF16)
        for k in range(4):
            quarter = lax.rem(depth + k, 4)
            count = side // 4
            at = pl.ds(pl.multiple_of(quarter * count, count), count)
            for b in range(blocks):
                out[k, b * count : (b + 1) * count, :] = rows_in[at, b * 128 : (b + 1) * 128]
            base = blocks * count
            count = VD // 4
            at = pl.ds(pl.multiple_of(quarter * count, count), count)
            for b in range(width // 128):
                out[k, base + b * count : base + (b + 1) * count, :] = rows_out[
                    at, b * 128 : (b + 1) * 128
                ]


def grads(place, normed, d_in, heads, cot):
    rows, width = cot.shape
    cols = d_in.shape[1]
    blocks = (cols + 127) // 128
    length = blocks * (width // 8) + width // 128 * (VD // 4)
    whole = lambda array: pl.BlockSpec(array.shape, lambda n, s: (0,) * array.ndim)
    outs = [jax.ShapeDtypeStruct((4, length, 128), BF16)] * 2
    ins = (normed, d_in, heads, cot)
    return pl.pallas_call(
        grads_kernel,
        grid_spec=pltpu.PrefetchScalarGridSpec(
            num_scalar_prefetch=1,
            grid=(1,),
            in_specs=[whole(a) for a in ins],
            out_specs=[whole(a) for a in outs],
            scratch_shapes=[
                pltpu.VMEM((width // 2, blocks * 128), BF16),
                pltpu.VMEM((VD, width), BF16),
            ],
        ),
        out_shape=outs,
        compiler_params=pltpu.CompilerParams(vmem_limit_bytes=VMEM_LIMIT),
        cost_estimate=pl.CostEstimate(
            flops=2 * rows * width * (cols + 2 * VD),
            bytes_accessed=16 * rows * width,
            transcendentals=0,
        ),
        name="grads",
    )(place, *ins)


def mix_kernel(place, heads, w_out, out):
    total = ndot(heads[0], w_out[0:VD, :]) + ndot(heads[1], w_out[VD : 2 * VD, :])
    out[0] = total.astype(BF16)


def mix(place, heads, w_out):
    rows = heads.shape[1] // 4
    width = w_out.shape[1]
    return pl.pallas_call(
        mix_kernel,
        grid_spec=pltpu.PrefetchScalarGridSpec(
            num_scalar_prefetch=1,
            grid=(4,),
            in_specs=[
                pl.BlockSpec((2, rows, VD), lambda n, s: (0, lax.rem(s[0] + n, 4), 0)),
                pl.BlockSpec(w_out.shape, lambda n, s: (0, 0)),
            ],
            out_specs=pl.BlockSpec((1, rows, width), lambda n, s: (n, 0, 0)),
        ),
        out_shape=jax.ShapeDtypeStruct((4, rows, width), BF16),
        compiler_params=pltpu.CompilerParams(vmem_limit_bytes=VMEM_LIMIT),
        cost_estimate=pl.CostEstimate(
            flops=16 * rows * width * VD, bytes_accessed=12 * rows * width, transcendentals=0
        ),
        name="mix",
    )(place, heads, w_out)


AXES = ("z", "y", "c", "x")
SIZES = (4, 4, 2, 4)


def place(z, y, c, x):
    return ((z * 4 + y) * 2 + c) * 4 + x


def moved(value, target):
    pairs = []
    for z in range(4):
        for y in range(4):
            for c in range(2):
                for x in range(4):
                    pairs.append((place(z, y, c, x), place(*target(z, y, c, x))))
    return lax.ppermute(value, AXES, pairs)


def flipped(value):
    return moved(value, lambda z, y, c, x: (z, y, 1 - c, x))


def turned(value, axis, by):
    return lax.ppermute(value, axis, [(i, (i + by) % 4) for i in range(4)])


def gathered(value, axis):
    me = lax.axis_index(axis)
    parts = [value, turned(value, axis, 3), turned(value, axis, 2), turned(value, axis, 1)]
    out = jnp.zeros((4, *value.shape), value.dtype)
    for j in range(4):
        out = lax.dynamic_update_index_in_dim(out, parts[j], lax.rem(me + j, 4), 0)
    return out


def summed(value, axis, dtype=BF16):
    me = lax.axis_index(axis)
    parts = [
        lax.dynamic_index_in_dim(value, lax.rem(me + j, 4), 0, keepdims=False) for j in range(4)
    ]
    total = parts[0].astype(F32)
    for j in range(1, 4):
        total = total + turned(parts[j], axis, j).astype(F32)
    return total.astype(dtype)


def by_core(own, other):
    first = lax.axis_index("c") == 0
    return jnp.where(first, own, other), jnp.where(first, other, own)


def around(value, axis="x"):
    return [value, turned(value, axis, 3), turned(value, axis, 2), turned(value, axis, 1)]


def returned(pieces):
    total = pieces[0].astype(F32)
    for k in range(1, 4):
        total = total + turned(pieces[k], "x", k).astype(F32)
    return total


def gather_in_x(w_query, w_kv):
    seq = lax.axis_index("x")
    cols = w_query.shape[1] // 4
    rows = jnp.zeros((4, w_query.shape[0], cols + w_kv.shape[1] + 64), BF16)
    w_kv = jnp.pad(w_kv, ((0, 0), (0, 64)))
    for k in range(4):
        head_cols = lax.dynamic_slice_in_dim(w_query, lax.rem(seq + k, 4) * cols, cols, 1)
        piece = jnp.concatenate([head_cols, w_kv], axis=1)
        if k:
            piece = turned(piece, "x", k)
        rows = lax.dynamic_update_index_in_dim(rows, piece, lax.rem(seq + 4 - k, 4), 0)
    return rows


def after(value, *others):
    return lax.optimization_barrier((value, *others))[0]


def split_rows(pieces):
    first = pieces[:960].reshape(5, 4, 48, 128).transpose(1, 0, 2, 3).reshape(4, 240, 128)
    second = pieces[960:].reshape(12, 4, 12, 128).transpose(1, 0, 2, 3).reshape(4, 144, 128)
    return jnp.concatenate([first, second], axis=1)


def finish(value, cols, width):
    seq = lax.axis_index("x")
    pieces = value[:240].reshape(5, 4, 12, 128).transpose(1, 2, 0, 3).reshape(4, 12, 640)
    grad_query = jnp.zeros((4, 12, cols), F32)
    grad_kv = jnp.zeros((12, HD + VD), F32)
    for k in range(4):

        def home(z, y, c, x):
            block = 16 * c + 4 * z + y
            return block // 8, block // 2 % 4, block % 2, (x + k) % 4

        piece = lax.dynamic_index_in_dim(pieces, lax.rem(seq + k, 4), 0, keepdims=False)
        piece = moved(piece, home).astype(F32)
        grad_query = lax.dynamic_update_index_in_dim(
            grad_query, piece[:, :cols], lax.rem(seq + 4 - k, 4), 0
        )
        grad_kv = grad_kv + piece[:, cols : cols + HD + VD]
    grad_query = grad_query.transpose(1, 0, 2).reshape(12, 4 * cols)
    grad_out = value[240:].reshape(12, 12, 128).transpose(1, 0, 2).reshape(12, width)
    grad_out = moved(grad_out, lambda z, y, c, x: (x, 2 * c + z // 2, z % 2, y)).astype(F32)
    return grad_query, grad_kv, grad_out


def rms_back(value, gain, grad):
    scale = row_scale(value)
    scaled = grad * gain
    return scale * scaled - value * (scale * scale * scale) * jnp.mean(
        value * scaled, axis=-1, keepdims=True
    )


def per_device(
    bases, skip, base_table, conv_weight, conv_gain, attn_gain, w_query, w_kv, w_out, cotangent
):
    skip = skip[0]
    cot = cotangent[0]
    rows, width = skip.shape
    half = rows // 2
    cells = bases.reshape(rows, bases.shape[1] // rows)
    seq = lax.axis_index("x")
    ends = jnp.stack([seq, 3 - seq]).astype(jnp.int32)

    def ahead(value):
        return lax.ppermute(value, "x", [(i, i + 1) for i in range(3)])

    def behind(value):
        return lax.ppermute(value, "x", [(i + 1, i) for i in range(3)])

    def edge(tokens, features):
        tokens = tokens.reshape(8, -1)
        counts = [jnp.sum((tokens == b).astype(F32), axis=1, keepdims=True) for b in range(4)]
        counts = jnp.concatenate(counts + [jnp.zeros((8, 124), F32)], axis=1)
        return jnp.concatenate([features, counts.astype(BF16)], axis=1)

    span = 8 * (bases.shape[1] // rows)
    edge_prev = ahead(edge(bases[0, bases.shape[1] - span :], skip[rows - 8 :]))
    edge_next = behind(edge(bases[0, :span], skip[:8]))
    w_rows = gather_in_x(w_query, w_kv)
    out_home = moved(w_out, lambda z, y, c, x: (y, x, c, z))
    beside = lax.ppermute(after(cot, w_rows), "x", [(i, i ^ 1) for i in range(4)])
    across = lax.ppermute(jnp.stack([cot, beside]), "x", [(i, 3 - i) for i in range(4)])
    side = width // 3
    cols = w_rows.shape[2]
    chunks = out_home.reshape(12, 4, width // 4).transpose(1, 0, 2)
    pieces = jnp.stack(around(jnp.concatenate([w_rows, chunks], axis=2), "y"))
    out_rows = jnp.roll(pieces[:, :, :, cols:], lax.axis_index("y"), axis=0)
    out_rows = out_rows.transpose(0, 2, 1, 3).reshape(48, width)
    rest = pieces[:, :, :, side:cols].reshape(4, 48, cols - side)
    joint = jnp.concatenate(
        [
            pieces[:, :, :, :side].reshape(192, side),
            out_rows.reshape(48, 3, side).transpose(1, 0, 2).reshape(144, side),
            rest.transpose(1, 0, 2).reshape(48, side),
        ],
        axis=0,
    )
    near = jnp.stack(around(joint, "z"))
    table = jnp.concatenate([base_table, conv_gain[None, :], attn_gain[None, :]], axis=0)
    pooled, normed = front(
        ends, cells, skip, edge_prev, edge_next, table, conv_weight
    )
    norms = around(normed)
    far = flipped(after(near, normed, across))

    spot = [seq, lax.axis_index("c"), lax.axis_index("z"), lax.axis_index("y")]
    spot = jnp.stack(spot).astype(jnp.int32)
    d_in, heads, normed_all, cot_all, full_out, *d_parts = attend(spot, norms, (cot, beside, across), near, far)
    d_parts[1:] = [turned(d_parts[k], "x", k) for k in range(1, 4)]
    own, other = grads(spot, normed_all, d_in, heads, cot_all)
    mine = (own.astype(F32) + flipped(other).astype(F32)).astype(BF16)
    total = mine[0].astype(F32)
    for k in range(1, 4):
        total = total + turned(mine[k], "z", k).astype(F32)
    mine = total.astype(BF16)
    d_normed = d_parts[0]
    for k in range(1, 4):
        d_normed = d_normed + after(d_parts[k], mine).astype(F32)
    mine = summed(split_rows(mine), "y")

    d_pooled = cot.astype(F32) + rms_back(pooled, attn_gain, d_normed)
    grad = (d_pooled * 0.5).astype(BF16)
    out_parts = mix(spot, after(heads, grad), full_out)
    grad_prev, grad_next = ahead(grad[half - 16 :]), behind(grad[:16])
    grad_next = after(grad_next, mine)
    coarse = (pooled + returned(after(out_parts, grad_prev))).astype(BF16)
    skip_grad = back(cells, skip, table, grad, grad_prev, grad_next, conv_weight)

    factor = 1.0 / 32
    cols = w_query.shape[1] // 4
    grad_query, grad_kv, grad_out = finish(mine, cols, width)
    return (
        coarse[None],
        skip_grad[None],
        grad_query * factor,
        grad_kv * factor,
        grad_out * factor,
    )


def solution(mesh):
    inner = Mesh(mesh.devices.reshape(SIZES), AXES)
    dp = ("z", "y", "c")
    every = AXES
    placed = (
        P(dp, "x"),
        P(dp, "x", None),
        P(),
        P(),
        P(),
        P(),
        P(every, None),
        P(every, None),
        P(every, None),
        P(dp, "x", None),
    )
    return jax.shard_map(
        per_device,
        mesh=inner,
        in_specs=placed,
        out_specs=(
            P(dp, "x", None),
            P(dp, "x", None),
            P(every, None),
            P(every, None),
            P(every, None),
        ),
        check_vma=False,
    )
```

```python
import jax
import jax.numpy as jnp
from jax import lax
from jax.experimental import pallas as pl
from jax.experimental.pallas import tpu as pltpu
from jax.sharding import Mesh
from jax.sharding import PartitionSpec as P

HQ = 8
HD = 128
VD = 192
VMEM_LIMIT = 60 * 1024 * 1024
F32 = jnp.float32
BF16 = jnp.bfloat16


def ndot(left, right):
    return lax.dot_general(
        left, right, (((1,), (0,)), ((), ())), preferred_element_type=F32
    )


def rdot(left, right):
    return lax.dot_general(
        left, right, (((1,), (1,)), ((), ())), preferred_element_type=F32
    )


def tdot(left, right):
    return lax.dot_general(
        left, right, (((0,), (0,)), ((), ())), preferred_element_type=F32
    )


def embed_counts(counts, skip, table):
    state = skip.astype(F32)
    for base in range(4):
        state = state + ((counts[base] - 16.0) * 0.25) * table[base : base + 1, :]
    return state


def embed_rows(cells, skip, table):
    counts = [jnp.sum((cells == base).astype(F32), axis=1, keepdims=True) for base in range(4)]
    return embed_counts(counts, skip, table)


def row_scale(value):
    return lax.rsqrt(jnp.mean(value * value, axis=-1, keepdims=True) + 1e-06)


def front_kernel(
    ends, cells, skip, edge_prev, edge_next, table,
    weight, pooled, normed, state_buf, active_buf, lhs, weight_buf, arrived,
):
    gain, attn_gain = table.at[4:5], table.at[5:6]
    rows = skip.shape[0]
    half = rows // 2
    width = skip.shape[1]
    steps, _, _, block = weight_buf.shape

    def fetch(step):
        cols = pl.ds(pl.multiple_of(step * block, block), block)
        return pltpu.make_async_copy(weight.at[:, :, cols], weight_buf.at[step], arrived.at[step])

    for step in range(steps):
        fetch(step).start()

    def rows_in(state, at, keep):
        pre = state * row_scale(state) * gain[...]
        active = 0.5 * pre * (1.0 + lax.erf(pre * 0.7071067811865476))
        active = active.astype(BF16).astype(F32)
        if keep is not None:
            active = jnp.where(keep > 0, active, 0.0)
        count = state.shape[0]
        for tile in range(skip.shape[1] // 128):
            lanes = slice(tile * 128, (tile + 1) * 128)
            state_buf[tile, pl.ds(at, count), :] = state[:, lanes]
            active_buf[tile, pl.ds(at, count), :] = active[:, lanes]

    def edge_rows(edge):
        counts = [edge[:, width + base : width + base + 1].astype(F32) for base in range(4)]
        return embed_counts(counts, edge[:, 0:width], table)

    rows_in(edge_rows(edge_prev), 0, ends[0])
    rows_in(edge_rows(edge_next), rows + 8, ends[1])

    chunk = 64

    def one(i, carry):
        at = pl.multiple_of(i * chunk, chunk)
        state = embed_rows(cells[pl.ds(at, chunk), :], skip[pl.ds(at, chunk), :], table)
        rows_in(state, pl.multiple_of(at + 8, 8), None)
        return carry

    lax.fori_loop(0, rows // chunk, one, 0)
    for tile in range(width // 128):
        cols = slice(tile * 128, (tile + 1) * 128)
        part = [active_buf[tile, pl.ds(6 + j, half, 2), :] for j in range(6)]
        for k in range(5):
            lhs[k, :, cols] = ((part[k] + part[k + 1]) * 0.5).astype(BF16)
        pooled[:, cols] = (
            state_buf[tile, pl.ds(8, half, 2), :] + state_buf[tile, pl.ds(9, half, 2), :]
        ) * 0.5

    def one_block(step, carry):
        fetch(step).wait()
        total = ndot(lhs[0], weight_buf[step, 0])
        for k in range(1, 5):
            total = total + ndot(lhs[k], weight_buf[step, k])
        cols = pl.ds(pl.multiple_of(step * block, block), block)
        pooled[:, cols] = pooled[:, cols] + total
        return carry

    lax.fori_loop(0, steps, one_block, 0)

    def finish_rows(i, carry):
        rows_at = pl.ds(pl.multiple_of(i * 64, 64), 64)
        value = pooled[rows_at, :]
        normed[rows_at, :] = (value * row_scale(value) * attn_gain[...]).astype(BF16)
        return carry

    lax.fori_loop(0, half // 64, finish_rows, 0)


def front(ends, cells, skip, edge_prev, edge_next, table, weight, block=256):
    rows, width = skip.shape
    half = rows // 2
    whole = lambda array: pl.BlockSpec(array.shape, lambda n, s: (0,) * array.ndim)
    small = (cells, skip, edge_prev, edge_next, table)
    return pl.pallas_call(
        front_kernel,
        grid_spec=pltpu.PrefetchScalarGridSpec(
            num_scalar_prefetch=1,
            grid=(1,),
            in_specs=[whole(a) for a in small] + [pl.BlockSpec(memory_space=pl.ANY)],
            out_specs=[
                pl.BlockSpec((half, width), lambda n, s: (0, 0)),
                pl.BlockSpec((half, width), lambda n, s: (0, 0)),
            ],
            scratch_shapes=[
                pltpu.VMEM((width // 128, rows + 16, 128), F32),
                pltpu.VMEM((width // 128, rows + 16, 128), F32),
                pltpu.VMEM((5, half, width), BF16),
                pltpu.VMEM((width // block, 5, width, block), BF16),
                pltpu.SemaphoreType.DMA((width // block,)),
            ],
        ),
        out_shape=[
            jax.ShapeDtypeStruct((half, width), F32),
            jax.ShapeDtypeStruct((half, width), BF16),
        ],
        compiler_params=pltpu.CompilerParams(vmem_limit_bytes=VMEM_LIMIT),
        cost_estimate=pl.CostEstimate(
            flops=2 * half * 5 * width * width, bytes_accessed=10 * width * width + 8 * rows * width, transcendentals=rows * width
        ),
        name="front",
    )(ends, *small, weight)


def back_kernel(
    cells, skip, table, grad, grad_prev, grad_next, weight, out,
    state_buf, scaled_buf, grad_buf, turned_buf, level_buf, scale_buf, sum_buf, weight_buf, arrived,
):
    gain = table.at[4:5]
    rows, width = skip.shape
    half = rows // 2
    steps, _, block, _ = weight_buf.shape
    chunk = 64

    def fetch(step):
        at = pl.ds(pl.multiple_of(step * block, block), block)
        return pltpu.make_async_copy(weight.at[:, at, :], weight_buf.at[step], arrived.at[step])

    for step in range(steps):
        fetch(step).start()

    grad_buf[pl.ds(0, 16), :] = grad_prev[...].astype(F32)
    grad_buf[pl.ds(16, half), :] = grad[...].astype(F32)
    grad_buf[pl.ds(half + 16, 16), :] = grad_next[...].astype(F32)
    for tile in range(width // 128):
        lanes = slice(tile * 128, (tile + 1) * 128)
        before, here, later = [
            grad_buf[pl.ds(15 + shift, half), lanes].T.astype(BF16) for shift in range(3)
        ]
        pairs = ((later, later), (here, later), (here, here), (before, here), (before, before))
        for tap, (even, odd) in enumerate(pairs):
            turned_buf[tap, lanes, 0:half] = even
            turned_buf[tap, lanes, half:rows] = odd

    def one(i, carry):
        at = pl.ds(pl.multiple_of(i * chunk, chunk), chunk)
        state = embed_rows(cells[at, :], skip[at, :], table)
        state_buf[at, :] = state
        scale_buf[at, :] = row_scale(state)
        return carry

    lax.fori_loop(0, rows // chunk, one, 0, unroll=2)
    sum_buf[...] = jnp.zeros_like(sum_buf)

    def one_block(step, carry):
        fetch(step).wait()
        total = None
        for k in range(5):
            part = ndot(weight_buf[step, k], turned_buf[k])
            total = part if total is None else total + part
        for tile in range(block // 128):
            level = total[tile * 128 : (tile + 1) * 128, :].T
            level_buf[tile, pl.ds(0, half, 2), :] = level[0:half]
            level_buf[tile, pl.ds(1, half, 2), :] = level[half:]
        cols = pl.ds(pl.multiple_of(step * block, block), block)

        def two(i, carry):
            at = pl.ds(pl.multiple_of(i * 256, 256), 256)
            state = state_buf[at, cols]
            pre = state * scale_buf[at, :] * gain[:, cols]
            slope = 0.5 * (1.0 + lax.erf(pre * 0.7071067811865476)) + pre * jnp.exp(
                -0.5 * pre * pre
            ) * 0.3989422804014327
            level = jnp.concatenate([level_buf[t, at, :] for t in range(block // 128)], axis=1)
            scaled = slope * level * gain[:, cols]
            scaled_buf[at, cols] = scaled
            product = state * scaled
            folded = product[:, 0:128]
            for tile in range(1, block // 128):
                folded = folded + product[:, tile * 128 : (tile + 1) * 128]
            sum_buf[at, :] = sum_buf[at, :] + folded
            return carry

        lax.fori_loop(0, rows // 256, two, 0)
        return carry

    lax.fori_loop(0, steps, one_block, 0)

    scale = scale_buf[...]
    coef = (scale * scale * scale) * (jnp.sum(sum_buf[...], axis=1, keepdims=True) * (1.0 / width))
    for tile in range(width // 128):
        lanes = slice(tile * 128, (tile + 1) * 128)
        own = grad_buf[pl.ds(16, half), lanes]
        scaled = scaled_buf[:, lanes]
        state = state_buf[:, lanes]
        level_buf[0, pl.ds(0, half, 2), :] = own
        level_buf[0, pl.ds(1, half, 2), :] = own
        out[:, lanes] = (level_buf[0] + (scale * scaled - state * coef)).astype(BF16)


def back(cells, skip, table, grad, grad_prev, grad_next, weight, block=256):
    rows, width = skip.shape
    half = rows // 2
    whole = lambda array: pl.BlockSpec(array.shape, lambda n: (0,) * array.ndim)
    small = (cells, skip, table, grad, grad_prev, grad_next)
    return pl.pallas_call(
        back_kernel,
        grid=(1,),
        in_specs=[whole(a) for a in small] + [pl.BlockSpec(memory_space=pl.ANY)],
        out_specs=pl.BlockSpec((rows, width), lambda n: (0, 0)),
        scratch_shapes=[
            pltpu.VMEM((rows, width), F32),
            pltpu.VMEM((rows, width), F32),
            pltpu.VMEM((half + 32, width), F32),
            pltpu.VMEM((5, width, rows), BF16),
            pltpu.VMEM((block // 128, rows, 128), F32),
            pltpu.VMEM((rows, 1), F32),
            pltpu.VMEM((rows, 128), F32),
            pltpu.VMEM((width // block, 5, block, width), BF16),
            pltpu.SemaphoreType.DMA((width // block,)),
        ],
        out_shape=jax.ShapeDtypeStruct((rows, width), BF16),
        compiler_params=pltpu.CompilerParams(vmem_limit_bytes=VMEM_LIMIT),
        cost_estimate=pl.CostEstimate(
            flops=2 * half * 5 * width * width, bytes_accessed=10 * width * width + 8 * rows * width, transcendentals=2 * rows * width
        ),
        name="back",
    )(*small, weight)


def attend_kernel(
    place, norm0, norm1, norm2, norm3, cot0, cot1, cot2, near, far,
    heads, w_out, own, part1, part2, part3, near_sum, far_sum,
    d_in, normed, cot, w_in, query_kv, acc, rows_in, rows_out,
):
    head = pl.program_id(0)
    seq, core, depth, level = place[0], place[1], place[2], place[3]
    inv = 1.0 / HD**0.5
    half = own.shape[0]
    cols = w_in.shape[1]
    side = near.shape[2]
    first = cols - side + HD

    def rows_of(index):
        return pl.ds(pl.multiple_of(index * half, half), half)

    @pl.when(head == 0)
    def _():
        for source, side_core in ((near, core), (far, 1 - core)):
            for turn in range(4):
                z = lax.rem(depth + turn, 4)
                for other in range(4):
                    y = lax.rem(level + other, 4)
                    at = pl.ds(pl.multiple_of((z * 4 + y) * 96 + side_core * 48, 16), 48)
                    w_in[at, 0:side] = source[turn, other * 48 : (other + 1) * 48, :]
                    w_in[at, side:cols] = source[turn, 336:384, other * 128 : (other + 1) * 128]
                at = pl.ds(pl.multiple_of(z * 96 + side_core * 48, 16), 48)
                for b in range(3):
                    w_out[at, b * side : (b + 1) * side] = source[
                        turn, 192 + b * 48 : 240 + b * 48, :
                    ]
        for piece, value in enumerate((norm0, norm1, norm2, norm3)):
            normed[rows_of(lax.rem(seq + piece, 4)), :] = value[...]
        beside = seq + 1 - 2 * lax.rem(seq, 2)
        cot[rows_of(seq), :] = cot0[...]
        cot[rows_of(beside), :] = cot1[...]
        cot[rows_of(3 - seq), :] = cot2[0]
        cot[rows_of(3 - beside), :] = cot2[1]
        query_kv[...] = ndot(normed[...], w_in[...]).astype(BF16)

    keys = query_kv[:, first : first + HD]
    values = query_kv[:, first + HD : first + HD + VD]
    lanes = pl.ds(pl.multiple_of(head * HD, HD), HD)
    q = query_kv[:, lanes]
    d_heads = rdot(cot[...], w_out[pl.ds(pl.multiple_of(head * VD, VD), VD), :]).astype(BF16)
    scores = rdot(q, keys) * inv
    expo = jnp.exp(scores - jnp.max(scores, axis=1, keepdims=True))
    probs = expo * (1.0 / jnp.sum(expo, axis=1, keepdims=True))
    weights = probs.astype(BF16)
    heads[head] = ndot(weights, values).astype(BF16)
    d_probs = rdot(d_heads, values)
    inner = jnp.sum(probs * d_probs, axis=1, keepdims=True)
    d_scores = (probs * (d_probs - inner) * inv).astype(BF16)
    d_in[:, lanes] = ndot(d_scores, keys).astype(BF16)
    d_keys = tdot(d_scores, q)
    d_values = tdot(weights, d_heads)

    @pl.when(head == 0)
    def _():
        acc[:, 0:HD] = d_keys
        acc[:, HD : HD + VD] = d_values

    @pl.when(head > 0)
    def _():
        acc[:, 0:HD] += d_keys
        acc[:, HD : HD + VD] += d_values

    @pl.when(head == pl.num_programs(0) - 1)
    def _():
        d_in[:, first + HD :] = jnp.zeros((4 * half, cols - first - HD), BF16)
        d_in[:, first : first + HD + VD] = acc[...].astype(BF16)
        for piece, out in enumerate((own, part1, part2, part3)):
            rows = d_in[rows_of(lax.rem(seq + piece, 4)), :]
            out[...] = rdot(rows, w_in[...]).astype(out.dtype)
        width = cot.shape[1]
        blocks = cols // 128
        for half_core, out in ((1 - core, far_sum), (core, near_sum)):
            tall = width // 2
            lanes = pl.ds(pl.multiple_of(half_core * tall, tall), tall)
            rows_in[...] = tdot(normed[:, lanes], d_in[...]).astype(BF16)
            rows_out[...] = tdot(heads[half_core], cot[...]).astype(BF16)
            for turn in range(4):
                quarter = lax.rem(depth + turn, 4)
                count = tall // 4
                at = pl.ds(pl.multiple_of(quarter * count, count), count)
                for b in range(blocks):
                    out[turn, b * count : (b + 1) * count, :] = rows_in[at, b * 128 : (b + 1) * 128]
                base = blocks * count
                count = VD // 4
                at = pl.ds(pl.multiple_of(quarter * count, count), count)
                for b in range(width // 128):
                    out[turn, base + b * count : base + (b + 1) * count, :] = rows_out[
                        at, b * 128 : (b + 1) * 128
                    ]


def attend(place, norms, cots, near, far):
    half, width = norms[0].shape
    rows = 4 * half
    cols = near.shape[2] + 128
    heads = 2
    whole = lambda array: pl.BlockSpec(array.shape, lambda h, s: (0,) * array.ndim)
    length = cols // 128 * (width // 8) + width // 128 * (VD // 4)
    outs = (
        [
            jax.ShapeDtypeStruct((heads, rows, VD), BF16),
            jax.ShapeDtypeStruct((heads * VD, width), BF16),
            jax.ShapeDtypeStruct((half, width), F32),
        ]
        + [jax.ShapeDtypeStruct((half, width), BF16)] * 3
        + [jax.ShapeDtypeStruct((4, length, 128), BF16)] * 2
    )
    specs = [whole(out) for out in outs]
    ins = (*norms, *cots, near, far)
    return pl.pallas_call(
        attend_kernel,
        grid_spec=pltpu.PrefetchScalarGridSpec(
            num_scalar_prefetch=1,
            grid=(heads,),
            in_specs=[whole(a) for a in ins],
            out_specs=specs,
            scratch_shapes=[
                pltpu.VMEM((rows, cols), BF16),
                pltpu.VMEM((rows, width), BF16),
                pltpu.VMEM((rows, width), BF16),
                pltpu.VMEM((width, cols), BF16),
                pltpu.VMEM((rows, cols), BF16),
                pltpu.VMEM((rows, HD + VD), F32),
                pltpu.VMEM((width // 2, cols), BF16),
                pltpu.VMEM((VD, width), BF16),
            ],
        ),
        out_shape=outs,
        compiler_params=pltpu.CompilerParams(vmem_limit_bytes=VMEM_LIMIT),
        cost_estimate=pl.CostEstimate(
            flops=2 * rows * heads * (2 * VD * width + 3 * rows * (HD + VD)) + 6 * rows * cols * width,
            bytes_accessed=8 * rows * width + 2 * heads * VD * width + 2 * cols * width,
            transcendentals=rows * heads * rows,
        ),
        name="attend",
    )(place, *ins)


def mix_kernel(place, heads, w_out, out):
    total = ndot(heads[0], w_out[0:VD, :]) + ndot(heads[1], w_out[VD : 2 * VD, :])
    out[0] = total.astype(BF16)


def mix(place, heads, w_out):
    rows = heads.shape[1] // 4
    width = w_out.shape[1]
    return pl.pallas_call(
        mix_kernel,
        grid_spec=pltpu.PrefetchScalarGridSpec(
            num_scalar_prefetch=1,
            grid=(4,),
            in_specs=[
                pl.BlockSpec((2, rows, VD), lambda n, s: (0, lax.rem(s[0] + n, 4), 0)),
                pl.BlockSpec(w_out.shape, lambda n, s: (0, 0)),
            ],
            out_specs=pl.BlockSpec((1, rows, width), lambda n, s: (n, 0, 0)),
        ),
        out_shape=jax.ShapeDtypeStruct((4, rows, width), BF16),
        compiler_params=pltpu.CompilerParams(vmem_limit_bytes=VMEM_LIMIT),
        cost_estimate=pl.CostEstimate(
            flops=16 * rows * width * VD, bytes_accessed=12 * rows * width, transcendentals=0
        ),
        name="mix",
    )(place, heads, w_out)


AXES = ("z", "y", "c", "x")
SIZES = (4, 4, 2, 4)


def place(z, y, c, x):
    return ((z * 4 + y) * 2 + c) * 4 + x


def moved(value, target):
    pairs = []
    for z in range(4):
        for y in range(4):
            for c in range(2):
                for x in range(4):
                    pairs.append((place(z, y, c, x), place(*target(z, y, c, x))))
    return lax.ppermute(value, AXES, pairs)


def flipped(value):
    return moved(value, lambda z, y, c, x: (z, y, 1 - c, x))


def turned(value, axis, by):
    return lax.ppermute(value, axis, [(i, (i + by) % 4) for i in range(4)])


def gathered(value, axis):
    me = lax.axis_index(axis)
    parts = [value, turned(value, axis, 3), turned(value, axis, 2), turned(value, axis, 1)]
    out = jnp.zeros((4, *value.shape), value.dtype)
    for j in range(4):
        out = lax.dynamic_update_index_in_dim(out, parts[j], lax.rem(me + j, 4), 0)
    return out


def summed(value, axis, dtype=BF16):
    me = lax.axis_index(axis)
    parts = [
        lax.dynamic_index_in_dim(value, lax.rem(me + j, 4), 0, keepdims=False) for j in range(4)
    ]
    total = parts[0].astype(F32)
    for j in range(1, 4):
        total = total + turned(parts[j], axis, j).astype(F32)
    return total.astype(dtype)


def by_core(own, other):
    first = lax.axis_index("c") == 0
    return jnp.where(first, own, other), jnp.where(first, other, own)


def around(value, axis="x"):
    return [value, turned(value, axis, 3), turned(value, axis, 2), turned(value, axis, 1)]


def returned(pieces):
    total = pieces[0].astype(F32)
    for k in range(1, 4):
        total = total + turned(pieces[k], "x", k).astype(F32)
    return total


def gather_in_x(w_query, w_kv):
    seq = lax.axis_index("x")
    cols = w_query.shape[1] // 4
    rows = jnp.zeros((4, w_query.shape[0], cols + w_kv.shape[1] + 64), BF16)
    w_kv = jnp.pad(w_kv, ((0, 0), (0, 64)))
    for k in range(4):
        head_cols = lax.dynamic_slice_in_dim(w_query, lax.rem(seq + k, 4) * cols, cols, 1)
        piece = jnp.concatenate([head_cols, w_kv], axis=1)
        if k:
            piece = turned(piece, "x", k)
        rows = lax.dynamic_update_index_in_dim(rows, piece, lax.rem(seq + 4 - k, 4), 0)
    return rows


def after(value, *others):
    return lax.optimization_barrier((value, *others))[0]


def split_rows(pieces):
    first = pieces[:960].reshape(5, 4, 48, 128).transpose(1, 0, 2, 3).reshape(4, 240, 128)
    second = pieces[960:].reshape(12, 4, 12, 128).transpose(1, 0, 2, 3).reshape(4, 144, 128)
    return jnp.concatenate([first, second], axis=1)


def finish(value, cols, width):
    seq = lax.axis_index("x")
    pieces = value[:240].reshape(5, 4, 12, 128).transpose(1, 2, 0, 3).reshape(4, 12, 640)
    grad_query = jnp.zeros((4, 12, cols), F32)
    grad_kv = jnp.zeros((12, HD + VD), F32)
    for k in range(4):

        def home(z, y, c, x):
            block = 16 * c + 4 * z + y
            return block // 8, block // 2 % 4, block % 2, (x + k) % 4

        piece = lax.dynamic_index_in_dim(pieces, lax.rem(seq + k, 4), 0, keepdims=False)
        piece = moved(piece, home).astype(F32)
        grad_query = lax.dynamic_update_index_in_dim(
            grad_query, piece[:, :cols], lax.rem(seq + 4 - k, 4), 0
        )
        grad_kv = grad_kv + piece[:, cols : cols + HD + VD]
    grad_query = grad_query.transpose(1, 0, 2).reshape(12, 4 * cols)
    grad_out = value[240:].reshape(12, 12, 128).transpose(1, 0, 2).reshape(12, width)
    grad_out = moved(grad_out, lambda z, y, c, x: (x, 2 * c + z // 2, z % 2, y)).astype(F32)
    return grad_query, grad_kv, grad_out


def rms_back(value, gain, grad):
    scale = row_scale(value)
    scaled = grad * gain
    return scale * scaled - value * (scale * scale * scale) * jnp.mean(
        value * scaled, axis=-1, keepdims=True
    )


def per_device(
    bases, skip, base_table, conv_weight, conv_gain, attn_gain, w_query, w_kv, w_out, cotangent
):
    skip = skip[0]
    cot = cotangent[0]
    rows, width = skip.shape
    half = rows // 2
    cells = bases.reshape(rows, bases.shape[1] // rows)
    seq = lax.axis_index("x")
    ends = jnp.stack([seq, 3 - seq]).astype(jnp.int32)

    def ahead(value):
        return lax.ppermute(value, "x", [(i, i + 1) for i in range(3)])

    def behind(value):
        return lax.ppermute(value, "x", [(i + 1, i) for i in range(3)])

    def edge(tokens, features):
        tokens = tokens.reshape(8, -1)
        counts = [jnp.sum((tokens == b).astype(F32), axis=1, keepdims=True) for b in range(4)]
        counts = jnp.concatenate(counts + [jnp.zeros((8, 124), F32)], axis=1)
        return jnp.concatenate([features, counts.astype(BF16)], axis=1)

    span = 8 * (bases.shape[1] // rows)
    edge_prev = ahead(edge(bases[0, bases.shape[1] - span :], skip[rows - 8 :]))
    edge_next = behind(edge(bases[0, :span], skip[:8]))
    w_rows = gather_in_x(w_query, w_kv)
    out_home = moved(w_out, lambda z, y, c, x: (y, x, c, z))
    beside = lax.ppermute(after(cot, w_rows), "x", [(i, i ^ 1) for i in range(4)])
    across = lax.ppermute(jnp.stack([cot, beside]), "x", [(i, 3 - i) for i in range(4)])
    side = width // 3
    cols = w_rows.shape[2]
    chunks = out_home.reshape(12, 4, width // 4).transpose(1, 0, 2)
    pieces = jnp.stack(around(jnp.concatenate([w_rows, chunks], axis=2), "y"))
    out_rows = jnp.roll(pieces[:, :, :, cols:], lax.axis_index("y"), axis=0)
    out_rows = out_rows.transpose(0, 2, 1, 3).reshape(48, width)
    rest = pieces[:, :, :, side:cols].reshape(4, 48, cols - side)
    joint = jnp.concatenate(
        [
            pieces[:, :, :, :side].reshape(192, side),
            out_rows.reshape(48, 3, side).transpose(1, 0, 2).reshape(144, side),
            rest.transpose(1, 0, 2).reshape(48, side),
        ],
        axis=0,
    )
    near = jnp.stack(around(joint, "z"))
    table = jnp.concatenate([base_table, conv_gain[None, :], attn_gain[None, :]], axis=0)
    pooled, normed = front(
        ends, cells, skip, edge_prev, edge_next, table, conv_weight
    )
    norms = around(normed)
    far = flipped(after(near, normed, across))

    spot = [seq, lax.axis_index("c"), lax.axis_index("z"), lax.axis_index("y")]
    spot = jnp.stack(spot).astype(jnp.int32)
    heads, full_out, *d_parts, own, other = attend(spot, norms, (cot, beside, across), near, far)
    d_parts[1:] = [turned(d_parts[k], "x", k) for k in range(1, 4)]
    mine = (own.astype(F32) + flipped(other).astype(F32)).astype(BF16)
    total = mine[0].astype(F32)
    for k in range(1, 4):
        total = total + turned(mine[k], "z", k).astype(F32)
    mine = total.astype(BF16)
    d_normed = d_parts[0]
    for k in range(1, 4):
        d_normed = d_normed + after(d_parts[k], mine).astype(F32)
    mine = summed(split_rows(mine), "y")

    d_pooled = cot.astype(F32) + rms_back(pooled, attn_gain, d_normed)
    grad = (d_pooled * 0.5).astype(BF16)
    out_parts = mix(spot, heads, full_out)
    grad_prev, grad_next = ahead(grad[half - 16 :]), behind(grad[:16])
    grad_next = after(grad_next, mine)
    coarse = (pooled + returned(after(out_parts, grad_prev))).astype(BF16)
    skip_grad = back(cells, skip, table, grad, grad_prev, grad_next, conv_weight)

    factor = 1.0 / 32
    cols = w_query.shape[1] // 4
    grad_query, grad_kv, grad_out = finish(mine, cols, width)
    grad_query = after(grad_query, coarse)
    return (
        coarse[None],
        skip_grad[None],
        grad_query * factor,
        grad_kv * factor,
        grad_out * factor,
    )


def solution(mesh):
    inner = Mesh(mesh.devices.reshape(SIZES), AXES)
    dp = ("z", "y", "c")
    every = AXES
    placed = (
        P(dp, "x"),
        P(dp, "x", None),
        P(),
        P(),
        P(),
        P(),
        P(every, None),
        P(every, None),
        P(every, None),
        P(dp, "x", None),
    )
    return jax.shard_map(
        per_device,
        mesh=inner,
        in_specs=placed,
        out_specs=(
            P(dp, "x", None),
            P(dp, "x", None),
            P(every, None),
            P(every, None),
            P(every, None),
        ),
        check_vma=False,
    )
```

```python
import jax
import jax.numpy as jnp
from jax import lax
from jax.experimental import pallas as pl
from jax.experimental.pallas import tpu as pltpu
from jax.sharding import Mesh
from jax.sharding import PartitionSpec as P

HQ = 8
HD = 128
VD = 192
VMEM_LIMIT = 60 * 1024 * 1024
F32 = jnp.float32
BF16 = jnp.bfloat16


def ndot(left, right):
    return lax.dot_general(
        left, right, (((1,), (0,)), ((), ())), preferred_element_type=F32
    )


def rdot(left, right):
    return lax.dot_general(
        left, right, (((1,), (1,)), ((), ())), preferred_element_type=F32
    )


def tdot(left, right):
    return lax.dot_general(
        left, right, (((0,), (0,)), ((), ())), preferred_element_type=F32
    )


def embed_counts(counts, skip, table):
    state = skip.astype(F32)
    for base in range(4):
        state = state + ((counts[base] - 16.0) * 0.25) * table[base : base + 1, :]
    return state


def embed_rows(cells, skip, table):
    counts = [jnp.sum((cells == base).astype(F32), axis=1, keepdims=True) for base in range(4)]
    return embed_counts(counts, skip, table)


def row_scale(value):
    return lax.rsqrt(jnp.mean(value * value, axis=-1, keepdims=True) + 1e-06)


def front_kernel(
    ends, cells, skip, edge_prev, edge_next, table,
    weight, pooled, normed, state_buf, active_buf, lhs, weight_buf, arrived,
):
    gain, attn_gain = table.at[4:5], table.at[5:6]
    rows = skip.shape[0]
    half = rows // 2
    width = skip.shape[1]
    steps, _, _, block = weight_buf.shape

    def fetch(step):
        cols = pl.ds(pl.multiple_of(step * block, block), block)
        return pltpu.make_async_copy(weight.at[:, :, cols], weight_buf.at[step], arrived.at[step])

    for step in range(steps):
        fetch(step).start()

    def rows_in(state, at, keep):
        pre = state * row_scale(state) * gain[...]
        active = 0.5 * pre * (1.0 + lax.erf(pre * 0.7071067811865476))
        active = active.astype(BF16).astype(F32)
        if keep is not None:
            active = jnp.where(keep > 0, active, 0.0)
        count = state.shape[0]
        for tile in range(skip.shape[1] // 128):
            lanes = slice(tile * 128, (tile + 1) * 128)
            state_buf[tile, pl.ds(at, count), :] = state[:, lanes]
            active_buf[tile, pl.ds(at, count), :] = active[:, lanes]

    def edge_rows(edge):
        counts = [edge[:, width + base : width + base + 1].astype(F32) for base in range(4)]
        return embed_counts(counts, edge[:, 0:width], table)

    rows_in(edge_rows(edge_prev), 0, ends[0])
    rows_in(edge_rows(edge_next), rows + 8, ends[1])

    chunk = 64

    def one(i, carry):
        at = pl.multiple_of(i * chunk, chunk)
        state = embed_rows(cells[pl.ds(at, chunk), :], skip[pl.ds(at, chunk), :], table)
        rows_in(state, pl.multiple_of(at + 8, 8), None)
        return carry

    lax.fori_loop(0, rows // chunk, one, 0)
    for tile in range(width // 128):
        cols = slice(tile * 128, (tile + 1) * 128)
        part = [active_buf[tile, pl.ds(6 + j, half, 2), :] for j in range(6)]
        for k in range(5):
            lhs[k, :, cols] = ((part[k] + part[k + 1]) * 0.5).astype(BF16)
        pooled[:, cols] = (
            state_buf[tile, pl.ds(8, half, 2), :] + state_buf[tile, pl.ds(9, half, 2), :]
        ) * 0.5

    def one_block(step, carry):
        fetch(step).wait()
        total = ndot(lhs[0], weight_buf[step, 0])
        for k in range(1, 5):
            total = total + ndot(lhs[k], weight_buf[step, k])
        cols = pl.ds(pl.multiple_of(step * block, block), block)
        pooled[:, cols] = pooled[:, cols] + total
        return carry

    lax.fori_loop(0, steps, one_block, 0)

    def finish_rows(i, carry):
        rows_at = pl.ds(pl.multiple_of(i * 64, 64), 64)
        value = pooled[rows_at, :]
        normed[rows_at, :] = (value * row_scale(value) * attn_gain[...]).astype(BF16)
        return carry

    lax.fori_loop(0, half // 64, finish_rows, 0)


def front(ends, cells, skip, edge_prev, edge_next, table, weight, block=256):
    rows, width = skip.shape
    half = rows // 2
    whole = lambda array: pl.BlockSpec(array.shape, lambda n, s: (0,) * array.ndim)
    small = (cells, skip, edge_prev, edge_next, table)
    return pl.pallas_call(
        front_kernel,
        grid_spec=pltpu.PrefetchScalarGridSpec(
            num_scalar_prefetch=1,
            grid=(1,),
            in_specs=[whole(a) for a in small] + [pl.BlockSpec(memory_space=pl.ANY)],
            out_specs=[
                pl.BlockSpec((half, width), lambda n, s: (0, 0)),
                pl.BlockSpec((half, width), lambda n, s: (0, 0)),
            ],
            scratch_shapes=[
                pltpu.VMEM((width // 128, rows + 16, 128), F32),
                pltpu.VMEM((width // 128, rows + 16, 128), F32),
                pltpu.VMEM((5, half, width), BF16),
                pltpu.VMEM((width // block, 5, width, block), BF16),
                pltpu.SemaphoreType.DMA((width // block,)),
            ],
        ),
        out_shape=[
            jax.ShapeDtypeStruct((half, width), F32),
            jax.ShapeDtypeStruct((half, width), BF16),
        ],
        compiler_params=pltpu.CompilerParams(vmem_limit_bytes=VMEM_LIMIT),
        cost_estimate=pl.CostEstimate(
            flops=2 * half * 5 * width * width, bytes_accessed=10 * width * width + 8 * rows * width, transcendentals=rows * width
        ),
        name="front",
    )(ends, *small, weight)


def back_kernel(
    cells, skip, table, grad, grad_prev, grad_next, weight, out,
    state_buf, scaled_buf, grad_buf, turned_buf, level_buf, scale_buf, sum_buf, weight_buf, arrived,
):
    gain = table.at[4:5]
    rows, width = skip.shape
    half = rows // 2
    steps, _, block, _ = weight_buf.shape
    chunk = 64

    def fetch(step):
        at = pl.ds(pl.multiple_of(step * block, block), block)
        return pltpu.make_async_copy(weight.at[:, at, :], weight_buf.at[step], arrived.at[step])

    for step in range(steps):
        fetch(step).start()

    grad_buf[pl.ds(0, 16), :] = grad_prev[...].astype(F32)
    grad_buf[pl.ds(16, half), :] = grad[...].astype(F32)
    grad_buf[pl.ds(half + 16, 16), :] = grad_next[...].astype(F32)
    for tile in range(width // 128):
        lanes = slice(tile * 128, (tile + 1) * 128)
        before, here, later = [
            grad_buf[pl.ds(15 + shift, half), lanes].T.astype(BF16) for shift in range(3)
        ]
        pairs = ((later, later), (here, later), (here, here), (before, here), (before, before))
        for tap, (even, odd) in enumerate(pairs):
            turned_buf[tap, lanes, 0:half] = even
            turned_buf[tap, lanes, half:rows] = odd

    def one(i, carry):
        at = pl.ds(pl.multiple_of(i * chunk, chunk), chunk)
        state = embed_rows(cells[at, :], skip[at, :], table)
        state_buf[at, :] = state
        scale_buf[at, :] = row_scale(state)
        return carry

    lax.fori_loop(0, rows // chunk, one, 0, unroll=2)
    sum_buf[...] = jnp.zeros_like(sum_buf)

    def one_block(step, carry):
        fetch(step).wait()
        total = None
        for k in range(5):
            part = ndot(weight_buf[step, k], turned_buf[k])
            total = part if total is None else total + part
        for tile in range(block // 128):
            level = total[tile * 128 : (tile + 1) * 128, :].T
            level_buf[tile, pl.ds(0, half, 2), :] = level[0:half]
            level_buf[tile, pl.ds(1, half, 2), :] = level[half:]
        cols = pl.ds(pl.multiple_of(step * block, block), block)

        def two(i, carry):
            at = pl.ds(pl.multiple_of(i * 256, 256), 256)
            state = state_buf[at, cols]
            pre = state * scale_buf[at, :] * gain[:, cols]
            slope = 0.5 * (1.0 + lax.erf(pre * 0.7071067811865476)) + pre * jnp.exp(
                -0.5 * pre * pre
            ) * 0.3989422804014327
            level = jnp.concatenate([level_buf[t, at, :] for t in range(block // 128)], axis=1)
            scaled = slope * level * gain[:, cols]
            scaled_buf[at, cols] = scaled
            product = state * scaled
            folded = product[:, 0:128]
            for tile in range(1, block // 128):
                folded = folded + product[:, tile * 128 : (tile + 1) * 128]
            sum_buf[at, :] = sum_buf[at, :] + folded
            return carry

        lax.fori_loop(0, rows // 256, two, 0)
        return carry

    lax.fori_loop(0, steps, one_block, 0)

    scale = scale_buf[...]
    coef = (scale * scale * scale) * (jnp.sum(sum_buf[...], axis=1, keepdims=True) * (1.0 / width))
    for tile in range(width // 128):
        lanes = slice(tile * 128, (tile + 1) * 128)
        own = grad_buf[pl.ds(16, half), lanes]
        scaled = scaled_buf[:, lanes]
        state = state_buf[:, lanes]
        level_buf[0, pl.ds(0, half, 2), :] = own
        level_buf[0, pl.ds(1, half, 2), :] = own
        out[:, lanes] = (level_buf[0] + (scale * scaled - state * coef)).astype(BF16)


def back(cells, skip, table, grad, grad_prev, grad_next, weight, block=256):
    rows, width = skip.shape
    half = rows // 2
    whole = lambda array: pl.BlockSpec(array.shape, lambda n: (0,) * array.ndim)
    small = (cells, skip, table, grad, grad_prev, grad_next)
    return pl.pallas_call(
        back_kernel,
        grid=(1,),
        in_specs=[whole(a) for a in small] + [pl.BlockSpec(memory_space=pl.ANY)],
        out_specs=pl.BlockSpec((rows, width), lambda n: (0, 0)),
        scratch_shapes=[
            pltpu.VMEM((rows, width), F32),
            pltpu.VMEM((rows, width), F32),
            pltpu.VMEM((half + 32, width), F32),
            pltpu.VMEM((5, width, rows), BF16),
            pltpu.VMEM((block // 128, rows, 128), F32),
            pltpu.VMEM((rows, 1), F32),
            pltpu.VMEM((rows, 128), F32),
            pltpu.VMEM((width // block, 5, block, width), BF16),
            pltpu.SemaphoreType.DMA((width // block,)),
        ],
        out_shape=jax.ShapeDtypeStruct((rows, width), BF16),
        compiler_params=pltpu.CompilerParams(vmem_limit_bytes=VMEM_LIMIT),
        cost_estimate=pl.CostEstimate(
            flops=2 * half * 5 * width * width, bytes_accessed=10 * width * width + 8 * rows * width, transcendentals=2 * rows * width
        ),
        name="back",
    )(*small, weight)


def prep_kernel(place, cot0, cot1, cot2, near, far, w_in, w_out, cot, d_heads):
    seq, core, depth, level = place[0], place[1], place[2], place[3]
    half = cot0.shape[0]
    side = near.shape[2]
    cols = w_in.shape[1]

    def rows_of(index):
        return pl.ds(pl.multiple_of(index * half, half), half)

    for source, side_core in ((near, core), (far, 1 - core)):
        for turn in range(4):
            z = lax.rem(depth + turn, 4)
            for other in range(4):
                y = lax.rem(level + other, 4)
                at = pl.ds(pl.multiple_of((z * 4 + y) * 96 + side_core * 48, 16), 48)
                w_in[at, 0:side] = source[turn, other * 48 : (other + 1) * 48, :]
                w_in[at, side:cols] = source[turn, 336:384, other * 128 : (other + 1) * 128]
            at = pl.ds(pl.multiple_of(z * 96 + side_core * 48, 16), 48)
            for b in range(3):
                w_out[at, b * side : (b + 1) * side] = source[
                    turn, 192 + b * 48 : 240 + b * 48, :
                ]
    beside = seq + 1 - 2 * lax.rem(seq, 2)
    cot[rows_of(seq), :] = cot0[...]
    cot[rows_of(beside), :] = cot1[...]
    cot[rows_of(3 - seq), :] = cot2[0]
    cot[rows_of(3 - beside), :] = cot2[1]
    for head in range(d_heads.shape[0]):
        d_heads[head] = rdot(cot[...], w_out[head * VD : (head + 1) * VD, :]).astype(BF16)


def prep(place, cots, near, far):
    half, width = cots[0].shape
    rows = 4 * half
    whole = lambda array: pl.BlockSpec(array.shape, lambda n, s: (0,) * array.ndim)
    outs = [
        jax.ShapeDtypeStruct((width, near.shape[2] + 128), BF16),
        jax.ShapeDtypeStruct((2 * VD, width), BF16),
        jax.ShapeDtypeStruct((rows, width), BF16),
        jax.ShapeDtypeStruct((2, rows, VD), BF16),
    ]
    ins = (*cots, near, far)
    return pl.pallas_call(
        prep_kernel,
        grid_spec=pltpu.PrefetchScalarGridSpec(
            num_scalar_prefetch=1,
            grid=(1,),
            in_specs=[whole(a) for a in ins],
            out_specs=[whole(a) for a in outs],
        ),
        out_shape=outs,
        compiler_params=pltpu.CompilerParams(vmem_limit_bytes=VMEM_LIMIT),
        cost_estimate=pl.CostEstimate(
            flops=4 * rows * VD * width, bytes_accessed=10 * width * width, transcendentals=0
        ),
        name="prep",
    )(place, *ins)


def attend_kernel(
    place, norm0, norm1, norm2, norm3, w_in, cot, d_heads_all,
    heads, own, part1, part2, part3, near_sum, far_sum,
    d_in, normed, query_kv, acc, rows_in, rows_out,
):
    head = pl.program_id(0)
    seq, core, depth = place[0], place[1], place[2]
    inv = 1.0 / HD**0.5
    half = own.shape[0]
    cols = w_in.shape[1]
    first = cols - 128 - HD - HD

    def rows_of(index):
        return pl.ds(pl.multiple_of(index * half, half), half)

    @pl.when(head == 0)
    def _():
        for piece, value in enumerate((norm0, norm1, norm2, norm3)):
            normed[rows_of(lax.rem(seq + piece, 4)), :] = value[...]
        query_kv[...] = ndot(normed[...], w_in[...]).astype(BF16)

    keys = query_kv[:, first : first + HD]
    values = query_kv[:, first + HD : first + HD + VD]
    lanes = pl.ds(pl.multiple_of(head * HD, HD), HD)
    q = query_kv[:, lanes]
    d_heads = d_heads_all[head]
    scores = rdot(q, keys) * inv
    expo = jnp.exp(scores - jnp.max(scores, axis=1, keepdims=True))
    probs = expo * (1.0 / jnp.sum(expo, axis=1, keepdims=True))
    weights = probs.astype(BF16)
    heads[head] = ndot(weights, values).astype(BF16)
    d_probs = rdot(d_heads, values)
    inner = jnp.sum(probs * d_probs, axis=1, keepdims=True)
    d_scores = (probs * (d_probs - inner) * inv).astype(BF16)
    d_in[:, lanes] = ndot(d_scores, keys).astype(BF16)
    d_keys = tdot(d_scores, q)
    d_values = tdot(weights, d_heads)

    @pl.when(head == 0)
    def _():
        acc[:, 0:HD] = d_keys
        acc[:, HD : HD + VD] = d_values

    @pl.when(head > 0)
    def _():
        acc[:, 0:HD] += d_keys
        acc[:, HD : HD + VD] += d_values

    @pl.when(head == pl.num_programs(0) - 1)
    def _():
        d_in[:, first + HD :] = jnp.zeros((4 * half, cols - first - HD), BF16)
        d_in[:, first : first + HD + VD] = acc[...].astype(BF16)
        for piece, out in enumerate((own, part1, part2, part3)):
            rows = d_in[rows_of(lax.rem(seq + piece, 4)), :]
            out[...] = rdot(rows, w_in[...]).astype(out.dtype)
        width = cot.shape[1]
        blocks = cols // 128
        for half_core, out in ((1 - core, far_sum), (core, near_sum)):
            tall = width // 2
            lanes = pl.ds(pl.multiple_of(half_core * tall, tall), tall)
            rows_in[...] = tdot(normed[:, lanes], d_in[...]).astype(BF16)
            rows_out[...] = tdot(heads[half_core], cot[...]).astype(BF16)
            for turn in range(4):
                quarter = lax.rem(depth + turn, 4)
                count = tall // 4
                at = pl.ds(pl.multiple_of(quarter * count, count), count)
                for b in range(blocks):
                    out[turn, b * count : (b + 1) * count, :] = rows_in[at, b * 128 : (b + 1) * 128]
                base = blocks * count
                count = VD // 4
                at = pl.ds(pl.multiple_of(quarter * count, count), count)
                for b in range(width // 128):
                    out[turn, base + b * count : base + (b + 1) * count, :] = rows_out[
                        at, b * 128 : (b + 1) * 128
                    ]


def attend(place, norms, w_in, cot, d_heads):
    half, width = norms[0].shape
    rows = 4 * half
    cols = w_in.shape[1]
    heads = d_heads.shape[0]
    whole = lambda array: pl.BlockSpec(array.shape, lambda h, s: (0,) * array.ndim)
    length = cols // 128 * (width // 8) + width // 128 * (VD // 4)
    outs = (
        [
            jax.ShapeDtypeStruct((heads, rows, VD), BF16),
            jax.ShapeDtypeStruct((half, width), F32),
        ]
        + [jax.ShapeDtypeStruct((half, width), BF16)] * 3
        + [jax.ShapeDtypeStruct((4, length, 128), BF16)] * 2
    )
    specs = [whole(out) for out in outs]
    ins = (*norms, w_in, cot, d_heads)
    return pl.pallas_call(
        attend_kernel,
        grid_spec=pltpu.PrefetchScalarGridSpec(
            num_scalar_prefetch=1,
            grid=(heads,),
            in_specs=[whole(a) for a in ins],
            out_specs=specs,
            scratch_shapes=[
                pltpu.VMEM((rows, cols), BF16),
                pltpu.VMEM((rows, width), BF16),
                pltpu.VMEM((rows, cols), BF16),
                pltpu.VMEM((rows, HD + VD), F32),
                pltpu.VMEM((width // 2, cols), BF16),
                pltpu.VMEM((VD, width), BF16),
            ],
        ),
        out_shape=outs,
        compiler_params=pltpu.CompilerParams(vmem_limit_bytes=VMEM_LIMIT),
        cost_estimate=pl.CostEstimate(
            flops=2 * rows * heads * (2 * VD * width + 3 * rows * (HD + VD)) + 6 * rows * cols * width,
            bytes_accessed=8 * rows * width + 2 * heads * VD * width + 2 * cols * width,
            transcendentals=rows * heads * rows,
        ),
        name="attend",
    )(place, *ins)


def mix_kernel(place, heads, w_out, out):
    total = ndot(heads[0], w_out[0:VD, :]) + ndot(heads[1], w_out[VD : 2 * VD, :])
    out[0] = total.astype(BF16)


def mix(place, heads, w_out):
    rows = heads.shape[1] // 4
    width = w_out.shape[1]
    return pl.pallas_call(
        mix_kernel,
        grid_spec=pltpu.PrefetchScalarGridSpec(
            num_scalar_prefetch=1,
            grid=(4,),
            in_specs=[
                pl.BlockSpec((2, rows, VD), lambda n, s: (0, lax.rem(s[0] + n, 4), 0)),
                pl.BlockSpec(w_out.shape, lambda n, s: (0, 0)),
            ],
            out_specs=pl.BlockSpec((1, rows, width), lambda n, s: (n, 0, 0)),
        ),
        out_shape=jax.ShapeDtypeStruct((4, rows, width), BF16),
        compiler_params=pltpu.CompilerParams(vmem_limit_bytes=VMEM_LIMIT),
        cost_estimate=pl.CostEstimate(
            flops=16 * rows * width * VD, bytes_accessed=12 * rows * width, transcendentals=0
        ),
        name="mix",
    )(place, heads, w_out)


AXES = ("z", "y", "c", "x")
SIZES = (4, 4, 2, 4)


def place(z, y, c, x):
    return ((z * 4 + y) * 2 + c) * 4 + x


def moved(value, target):
    pairs = []
    for z in range(4):
        for y in range(4):
            for c in range(2):
                for x in range(4):
                    pairs.append((place(z, y, c, x), place(*target(z, y, c, x))))
    return lax.ppermute(value, AXES, pairs)


def flipped(value):
    return moved(value, lambda z, y, c, x: (z, y, 1 - c, x))


def turned(value, axis, by):
    return lax.ppermute(value, axis, [(i, (i + by) % 4) for i in range(4)])


def gathered(value, axis):
    me = lax.axis_index(axis)
    parts = [value, turned(value, axis, 3), turned(value, axis, 2), turned(value, axis, 1)]
    out = jnp.zeros((4, *value.shape), value.dtype)
    for j in range(4):
        out = lax.dynamic_update_index_in_dim(out, parts[j], lax.rem(me + j, 4), 0)
    return out


def summed(value, axis, dtype=BF16):
    me = lax.axis_index(axis)
    parts = [
        lax.dynamic_index_in_dim(value, lax.rem(me + j, 4), 0, keepdims=False) for j in range(4)
    ]
    total = parts[0].astype(F32)
    for j in range(1, 4):
        total = total + turned(parts[j], axis, j).astype(F32)
    return total.astype(dtype)


def by_core(own, other):
    first = lax.axis_index("c") == 0
    return jnp.where(first, own, other), jnp.where(first, other, own)


def around(value, axis="x"):
    return [value, turned(value, axis, 3), turned(value, axis, 2), turned(value, axis, 1)]


def returned(pieces):
    total = pieces[0].astype(F32)
    for k in range(1, 4):
        total = total + turned(pieces[k], "x", k).astype(F32)
    return total


def gather_in_x(w_query, w_kv):
    seq = lax.axis_index("x")
    cols = w_query.shape[1] // 4
    rows = jnp.zeros((4, w_query.shape[0], cols + w_kv.shape[1] + 64), BF16)
    w_kv = jnp.pad(w_kv, ((0, 0), (0, 64)))
    for k in range(4):
        head_cols = lax.dynamic_slice_in_dim(w_query, lax.rem(seq + k, 4) * cols, cols, 1)
        piece = jnp.concatenate([head_cols, w_kv], axis=1)
        if k:
            piece = turned(piece, "x", k)
        rows = lax.dynamic_update_index_in_dim(rows, piece, lax.rem(seq + 4 - k, 4), 0)
    return rows


def after(value, *others):
    return lax.optimization_barrier((value, *others))[0]


def split_rows(pieces):
    first = pieces[:960].reshape(5, 4, 48, 128).transpose(1, 0, 2, 3).reshape(4, 240, 128)
    second = pieces[960:].reshape(12, 4, 12, 128).transpose(1, 0, 2, 3).reshape(4, 144, 128)
    return jnp.concatenate([first, second], axis=1)


def finish(value, cols, width):
    seq = lax.axis_index("x")
    pieces = value[:240].reshape(5, 4, 12, 128).transpose(1, 2, 0, 3).reshape(4, 12, 640)
    grad_query = jnp.zeros((4, 12, cols), F32)
    grad_kv = jnp.zeros((12, HD + VD), F32)
    for k in range(4):

        def home(z, y, c, x):
            block = 16 * c + 4 * z + y
            return block // 8, block // 2 % 4, block % 2, (x + k) % 4

        piece = lax.dynamic_index_in_dim(pieces, lax.rem(seq + k, 4), 0, keepdims=False)
        piece = moved(piece, home).astype(F32)
        grad_query = lax.dynamic_update_index_in_dim(
            grad_query, piece[:, :cols], lax.rem(seq + 4 - k, 4), 0
        )
        grad_kv = grad_kv + piece[:, cols : cols + HD + VD]
    grad_query = grad_query.transpose(1, 0, 2).reshape(12, 4 * cols)
    grad_out = value[240:].reshape(12, 12, 128).transpose(1, 0, 2).reshape(12, width)
    grad_out = moved(grad_out, lambda z, y, c, x: (x, 2 * c + z // 2, z % 2, y)).astype(F32)
    return grad_query, grad_kv, grad_out


def rms_back(value, gain, grad):
    scale = row_scale(value)
    scaled = grad * gain
    return scale * scaled - value * (scale * scale * scale) * jnp.mean(
        value * scaled, axis=-1, keepdims=True
    )


def per_device(
    bases, skip, base_table, conv_weight, conv_gain, attn_gain, w_query, w_kv, w_out, cotangent
):
    skip = skip[0]
    cot = cotangent[0]
    rows, width = skip.shape
    half = rows // 2
    cells = bases.reshape(rows, bases.shape[1] // rows)
    seq = lax.axis_index("x")
    ends = jnp.stack([seq, 3 - seq]).astype(jnp.int32)

    def ahead(value):
        return lax.ppermute(value, "x", [(i, i + 1) for i in range(3)])

    def behind(value):
        return lax.ppermute(value, "x", [(i + 1, i) for i in range(3)])

    def edge(tokens, features):
        tokens = tokens.reshape(8, -1)
        counts = [jnp.sum((tokens == b).astype(F32), axis=1, keepdims=True) for b in range(4)]
        counts = jnp.concatenate(counts + [jnp.zeros((8, 124), F32)], axis=1)
        return jnp.concatenate([features, counts.astype(BF16)], axis=1)

    span = 8 * (bases.shape[1] // rows)
    edge_prev = ahead(edge(bases[0, bases.shape[1] - span :], skip[rows - 8 :]))
    edge_next = behind(edge(bases[0, :span], skip[:8]))
    w_rows = gather_in_x(w_query, w_kv)
    out_home = moved(w_out, lambda z, y, c, x: (y, x, c, z))
    beside = lax.ppermute(after(cot, w_rows), "x", [(i, i ^ 1) for i in range(4)])
    across = lax.ppermute(jnp.stack([cot, beside]), "x", [(i, 3 - i) for i in range(4)])
    side = width // 3
    cols = w_rows.shape[2]
    chunks = out_home.reshape(12, 4, width // 4).transpose(1, 0, 2)
    pieces = jnp.stack(around(jnp.concatenate([w_rows, chunks], axis=2), "y"))
    out_rows = jnp.roll(pieces[:, :, :, cols:], lax.axis_index("y"), axis=0)
    out_rows = out_rows.transpose(0, 2, 1, 3).reshape(48, width)
    rest = pieces[:, :, :, side:cols].reshape(4, 48, cols - side)
    joint = jnp.concatenate(
        [
            pieces[:, :, :, :side].reshape(192, side),
            out_rows.reshape(48, 3, side).transpose(1, 0, 2).reshape(144, side),
            rest.transpose(1, 0, 2).reshape(48, side),
        ],
        axis=0,
    )
    near = jnp.stack(around(joint, "z"))
    table = jnp.concatenate([base_table, conv_gain[None, :], attn_gain[None, :]], axis=0)
    pooled, normed = front(
        ends, cells, skip, edge_prev, edge_next, table, conv_weight
    )
    norms = around(normed)
    far = flipped(after(near, normed, across))

    spot = [seq, lax.axis_index("c"), lax.axis_index("z"), lax.axis_index("y")]
    spot = jnp.stack(spot).astype(jnp.int32)
    w_in, full_out, cot_all, d_heads = prep(spot, (cot, beside, across), near, far)
    norms = [after(norm, w_in) for norm in norms]
    heads, *d_parts, own, other = attend(spot, norms, w_in, cot_all, d_heads)
    d_parts[1:] = [turned(d_parts[k], "x", k) for k in range(1, 4)]
    mine = (own.astype(F32) + flipped(other).astype(F32)).astype(BF16)
    total = mine[0].astype(F32)
    for k in range(1, 4):
        total = total + turned(mine[k], "z", k).astype(F32)
    mine = total.astype(BF16)
    d_normed = d_parts[0]
    for k in range(1, 4):
        d_normed = d_normed + after(d_parts[k], mine).astype(F32)
    mine = summed(split_rows(mine), "y")

    d_pooled = cot.astype(F32) + rms_back(pooled, attn_gain, d_normed)
    grad = (d_pooled * 0.5).astype(BF16)
    out_parts = mix(spot, heads, full_out)
    grad_prev, grad_next = ahead(grad[half - 16 :]), behind(grad[:16])
    grad_next = after(grad_next, mine)
    coarse = (pooled + returned(after(out_parts, grad_prev))).astype(BF16)
    skip_grad = back(cells, skip, table, grad, grad_prev, grad_next, conv_weight)

    factor = 1.0 / 32
    cols = w_query.shape[1] // 4
    grad_query, grad_kv, grad_out = finish(mine, cols, width)
    grad_query = after(grad_query, coarse)
    return (
        coarse[None],
        skip_grad[None],
        grad_query * factor,
        grad_kv * factor,
        grad_out * factor,
    )


def solution(mesh):
    inner = Mesh(mesh.devices.reshape(SIZES), AXES)
    dp = ("z", "y", "c")
    every = AXES
    placed = (
        P(dp, "x"),
        P(dp, "x", None),
        P(),
        P(),
        P(),
        P(),
        P(every, None),
        P(every, None),
        P(every, None),
        P(dp, "x", None),
    )
    return jax.shard_map(
        per_device,
        mesh=inner,
        in_specs=placed,
        out_specs=(
            P(dp, "x", None),
            P(dp, "x", None),
            P(every, None),
            P(every, None),
            P(every, None),
        ),
        check_vma=False,
    )
```

```python
import jax
import jax.numpy as jnp
from jax import lax
from jax.experimental import pallas as pl
from jax.experimental.pallas import tpu as pltpu
from jax.sharding import Mesh
from jax.sharding import PartitionSpec as P

HQ = 8
HD = 128
VD = 192
VMEM_LIMIT = 60 * 1024 * 1024
F32 = jnp.float32
BF16 = jnp.bfloat16


def ndot(left, right):
    return lax.dot_general(
        left, right, (((1,), (0,)), ((), ())), preferred_element_type=F32
    )


def rdot(left, right):
    return lax.dot_general(
        left, right, (((1,), (1,)), ((), ())), preferred_element_type=F32
    )


def tdot(left, right):
    return lax.dot_general(
        left, right, (((0,), (0,)), ((), ())), preferred_element_type=F32
    )


def embed_counts(counts, skip, table):
    state = skip.astype(F32)
    for base in range(4):
        state = state + ((counts[base] - 16.0) * 0.25) * table[base : base + 1, :]
    return state


def embed_rows(cells, skip, table):
    counts = [jnp.sum((cells == base).astype(F32), axis=1, keepdims=True) for base in range(4)]
    return embed_counts(counts, skip, table)


def row_scale(value):
    return lax.rsqrt(jnp.mean(value * value, axis=-1, keepdims=True) + 1e-06)


def front_kernel(
    ends, cells, skip, edge_prev, edge_next, table,
    weight, pooled, normed, state_buf, active_buf, lhs, weight_buf, arrived,
):
    gain, attn_gain = table.at[4:5], table.at[5:6]
    rows = skip.shape[0]
    half = rows // 2
    width = skip.shape[1]
    steps, _, _, block = weight_buf.shape

    def fetch(step):
        cols = pl.ds(pl.multiple_of(step * block, block), block)
        return pltpu.make_async_copy(weight.at[:, :, cols], weight_buf.at[step], arrived.at[step])

    for step in range(steps):
        fetch(step).start()

    def rows_in(state, at, keep):
        pre = state * row_scale(state) * gain[...]
        active = 0.5 * pre * (1.0 + lax.erf(pre * 0.7071067811865476))
        active = active.astype(BF16).astype(F32)
        if keep is not None:
            active = jnp.where(keep > 0, active, 0.0)
        count = state.shape[0]
        for tile in range(skip.shape[1] // 128):
            lanes = slice(tile * 128, (tile + 1) * 128)
            state_buf[tile, pl.ds(at, count), :] = state[:, lanes]
            active_buf[tile, pl.ds(at, count), :] = active[:, lanes]

    def edge_rows(edge):
        counts = [edge[:, width + base : width + base + 1].astype(F32) for base in range(4)]
        return embed_counts(counts, edge[:, 0:width], table)

    rows_in(edge_rows(edge_prev), 0, ends[0])
    rows_in(edge_rows(edge_next), rows + 8, ends[1])

    chunk = 64

    def one(i, carry):
        at = pl.multiple_of(i * chunk, chunk)
        state = embed_rows(cells[pl.ds(at, chunk), :], skip[pl.ds(at, chunk), :], table)
        rows_in(state, pl.multiple_of(at + 8, 8), None)
        return carry

    lax.fori_loop(0, rows // chunk, one, 0)
    for tile in range(width // 128):
        cols = slice(tile * 128, (tile + 1) * 128)
        part = [active_buf[tile, pl.ds(6 + j, half, 2), :] for j in range(6)]
        for k in range(5):
            lhs[k, :, cols] = ((part[k] + part[k + 1]) * 0.5).astype(BF16)
        pooled[:, cols] = (
            state_buf[tile, pl.ds(8, half, 2), :] + state_buf[tile, pl.ds(9, half, 2), :]
        ) * 0.5

    def one_block(step, carry):
        fetch(step).wait()
        total = ndot(lhs[0], weight_buf[step, 0])
        for k in range(1, 5):
            total = total + ndot(lhs[k], weight_buf[step, k])
        cols = pl.ds(pl.multiple_of(step * block, block), block)
        pooled[:, cols] = pooled[:, cols] + total
        return carry

    lax.fori_loop(0, steps, one_block, 0)

    def finish_rows(i, carry):
        rows_at = pl.ds(pl.multiple_of(i * 64, 64), 64)
        value = pooled[rows_at, :]
        normed[rows_at, :] = (value * row_scale(value) * attn_gain[...]).astype(BF16)
        return carry

    lax.fori_loop(0, half // 64, finish_rows, 0)


def front(ends, cells, skip, edge_prev, edge_next, table, weight, block=256):
    rows, width = skip.shape
    half = rows // 2
    whole = lambda array: pl.BlockSpec(array.shape, lambda n, s: (0,) * array.ndim)
    small = (cells, skip, edge_prev, edge_next, table)
    return pl.pallas_call(
        front_kernel,
        grid_spec=pltpu.PrefetchScalarGridSpec(
            num_scalar_prefetch=1,
            grid=(1,),
            in_specs=[whole(a) for a in small] + [pl.BlockSpec(memory_space=pl.ANY)],
            out_specs=[
                pl.BlockSpec((half, width), lambda n, s: (0, 0)),
                pl.BlockSpec((half, width), lambda n, s: (0, 0)),
            ],
            scratch_shapes=[
                pltpu.VMEM((width // 128, rows + 16, 128), F32),
                pltpu.VMEM((width // 128, rows + 16, 128), F32),
                pltpu.VMEM((5, half, width), BF16),
                pltpu.VMEM((width // block, 5, width, block), BF16),
                pltpu.SemaphoreType.DMA((width // block,)),
            ],
        ),
        out_shape=[
            jax.ShapeDtypeStruct((half, width), F32),
            jax.ShapeDtypeStruct((half, width), BF16),
        ],
        compiler_params=pltpu.CompilerParams(vmem_limit_bytes=VMEM_LIMIT),
        cost_estimate=pl.CostEstimate(
            flops=2 * half * 5 * width * width, bytes_accessed=10 * width * width + 8 * rows * width, transcendentals=rows * width
        ),
        name="front",
    )(ends, *small, weight)


def back_kernel(
    cells, skip, table, grad, grad_prev, grad_next, weight, out,
    state_buf, scaled_buf, grad_buf, turned_buf, level_buf, scale_buf, sum_buf, weight_buf, arrived,
):
    gain = table.at[4:5]
    rows, width = skip.shape
    half = rows // 2
    steps, _, block, _ = weight_buf.shape
    chunk = 64

    def fetch(step):
        at = pl.ds(pl.multiple_of(step * block, block), block)
        return pltpu.make_async_copy(weight.at[:, at, :], weight_buf.at[step], arrived.at[step])

    for step in range(steps):
        fetch(step).start()

    grad_buf[pl.ds(0, 16), :] = grad_prev[...].astype(F32)
    grad_buf[pl.ds(16, half), :] = grad[...].astype(F32)
    grad_buf[pl.ds(half + 16, 16), :] = grad_next[...].astype(F32)
    for tile in range(width // 128):
        lanes = slice(tile * 128, (tile + 1) * 128)
        before, here, later = [
            grad_buf[pl.ds(15 + shift, half), lanes].T.astype(BF16) for shift in range(3)
        ]
        pairs = ((later, later), (here, later), (here, here), (before, here), (before, before))
        for tap, (even, odd) in enumerate(pairs):
            turned_buf[tap, lanes, 0:half] = even
            turned_buf[tap, lanes, half:rows] = odd

    def one(i, carry):
        at = pl.ds(pl.multiple_of(i * chunk, chunk), chunk)
        state = embed_rows(cells[at, :], skip[at, :], table)
        state_buf[at, :] = state
        scale_buf[at, :] = row_scale(state)
        return carry

    lax.fori_loop(0, rows // chunk, one, 0, unroll=2)
    sum_buf[...] = jnp.zeros_like(sum_buf)

    def one_block(step, carry):
        fetch(step).wait()
        total = None
        for k in range(5):
            part = ndot(weight_buf[step, k], turned_buf[k])
            total = part if total is None else total + part
        for tile in range(block // 128):
            level = total[tile * 128 : (tile + 1) * 128, :].T
            level_buf[tile, pl.ds(0, half, 2), :] = level[0:half]
            level_buf[tile, pl.ds(1, half, 2), :] = level[half:]
        cols = pl.ds(pl.multiple_of(step * block, block), block)

        def two(i, carry):
            at = pl.ds(pl.multiple_of(i * 256, 256), 256)
            state = state_buf[at, cols]
            pre = state * scale_buf[at, :] * gain[:, cols]
            slope = 0.5 * (1.0 + lax.erf(pre * 0.7071067811865476)) + pre * jnp.exp(
                -0.5 * pre * pre
            ) * 0.3989422804014327
            level = jnp.concatenate([level_buf[t, at, :] for t in range(block // 128)], axis=1)
            scaled = slope * level * gain[:, cols]
            scaled_buf[at, cols] = scaled
            product = state * scaled
            folded = product[:, 0:128]
            for tile in range(1, block // 128):
                folded = folded + product[:, tile * 128 : (tile + 1) * 128]
            sum_buf[at, :] = sum_buf[at, :] + folded
            return carry

        lax.fori_loop(0, rows // 256, two, 0)
        return carry

    lax.fori_loop(0, steps, one_block, 0)

    scale = scale_buf[...]
    coef = (scale * scale * scale) * (jnp.sum(sum_buf[...], axis=1, keepdims=True) * (1.0 / width))
    for tile in range(width // 128):
        lanes = slice(tile * 128, (tile + 1) * 128)
        own = grad_buf[pl.ds(16, half), lanes]
        scaled = scaled_buf[:, lanes]
        state = state_buf[:, lanes]
        level_buf[0, pl.ds(0, half, 2), :] = own
        level_buf[0, pl.ds(1, half, 2), :] = own
        out[:, lanes] = (level_buf[0] + (scale * scaled - state * coef)).astype(BF16)


def back(cells, skip, table, grad, grad_prev, grad_next, weight, block=256):
    rows, width = skip.shape
    half = rows // 2
    whole = lambda array: pl.BlockSpec(array.shape, lambda n: (0,) * array.ndim)
    small = (cells, skip, table, grad, grad_prev, grad_next)
    return pl.pallas_call(
        back_kernel,
        grid=(1,),
        in_specs=[whole(a) for a in small] + [pl.BlockSpec(memory_space=pl.ANY)],
        out_specs=pl.BlockSpec((rows, width), lambda n: (0, 0)),
        scratch_shapes=[
            pltpu.VMEM((rows, width), F32),
            pltpu.VMEM((rows, width), F32),
            pltpu.VMEM((half + 32, width), F32),
            pltpu.VMEM((5, width, rows), BF16),
            pltpu.VMEM((block // 128, rows, 128), F32),
            pltpu.VMEM((rows, 1), F32),
            pltpu.VMEM((rows, 128), F32),
            pltpu.VMEM((width // block, 5, block, width), BF16),
            pltpu.SemaphoreType.DMA((width // block,)),
        ],
        out_shape=jax.ShapeDtypeStruct((rows, width), BF16),
        compiler_params=pltpu.CompilerParams(vmem_limit_bytes=VMEM_LIMIT),
        cost_estimate=pl.CostEstimate(
            flops=2 * half * 5 * width * width, bytes_accessed=10 * width * width + 8 * rows * width, transcendentals=2 * rows * width
        ),
        name="back",
    )(*small, weight)


def prep_kernel(place, cot0, cot1, cot2, near, far, w_in, w_out, cot, d_heads):
    seq, core, depth, level = place[0], place[1], place[2], place[3]
    half = cot0.shape[0]
    side = near.shape[2]
    cols = w_in.shape[1]

    def rows_of(index):
        return pl.ds(pl.multiple_of(index * half, half), half)

    for source, side_core in ((near, core), (far, 1 - core)):
        for turn in range(4):
            z = lax.rem(depth + turn, 4)
            for other in range(4):
                y = lax.rem(level + other, 4)
                at = pl.ds(pl.multiple_of((z * 4 + y) * 96 + side_core * 48, 16), 48)
                w_in[at, 0:side] = source[turn, other * 48 : (other + 1) * 48, :]
                w_in[at, side:cols] = source[turn, 336:384, other * 128 : (other + 1) * 128]
            at = pl.ds(pl.multiple_of(z * 96 + side_core * 48, 16), 48)
            for b in range(3):
                w_out[at, b * side : (b + 1) * side] = source[
                    turn, 192 + b * 48 : 240 + b * 48, :
                ]
    beside = seq + 1 - 2 * lax.rem(seq, 2)
    cot[rows_of(seq), :] = cot0[...]
    cot[rows_of(beside), :] = cot1[...]
    cot[rows_of(3 - seq), :] = cot2[0]
    cot[rows_of(3 - beside), :] = cot2[1]
    for head in range(d_heads.shape[0]):
        d_heads[head] = rdot(cot[...], w_out[head * VD : (head + 1) * VD, :]).astype(BF16)


def prep(place, cots, near, far):
    half, width = cots[0].shape
    rows = 4 * half
    whole = lambda array: pl.BlockSpec(array.shape, lambda n, s: (0,) * array.ndim)
    outs = [
        jax.ShapeDtypeStruct((width, near.shape[2] + 128), BF16),
        jax.ShapeDtypeStruct((2 * VD, width), BF16),
        jax.ShapeDtypeStruct((rows, width), BF16),
        jax.ShapeDtypeStruct((2, rows, VD), BF16),
    ]
    ins = (*cots, near, far)
    return pl.pallas_call(
        prep_kernel,
        grid_spec=pltpu.PrefetchScalarGridSpec(
            num_scalar_prefetch=1,
            grid=(1,),
            in_specs=[whole(a) for a in ins],
            out_specs=[whole(a) for a in outs],
        ),
        out_shape=outs,
        compiler_params=pltpu.CompilerParams(vmem_limit_bytes=VMEM_LIMIT),
        cost_estimate=pl.CostEstimate(
            flops=4 * rows * VD * width, bytes_accessed=10 * width * width, transcendentals=0
        ),
        name="prep",
    )(place, *ins)


def attend_kernel(
    place, norm0, norm1, norm2, norm3, w_in, cot, d_heads_all,
    heads, own, part1, part2, part3, near_sum, far_sum,
    d_in, normed, query_kv, acc, rows_in, rows_out,
):
    head = pl.program_id(0)
    seq, core, depth = place[0], place[1], place[2]
    inv = 1.0 / HD**0.5
    half = own.shape[0]
    cols = w_in.shape[1]
    first = cols - 128 - HD - HD

    def rows_of(index):
        return pl.ds(pl.multiple_of(index * half, half), half)

    @pl.when(head == 0)
    def _():
        for piece, value in enumerate((norm0, norm1, norm2, norm3)):
            normed[rows_of(lax.rem(seq + piece, 4)), :] = value[...]
        query_kv[...] = ndot(normed[...], w_in[...]).astype(BF16)

    keys = query_kv[:, first : first + HD]
    values = query_kv[:, first + HD : first + HD + VD]
    lanes = pl.ds(pl.multiple_of(head * HD, HD), HD)
    q = query_kv[:, lanes]
    d_heads = d_heads_all[head]
    scores = rdot(q, keys) * inv
    expo = jnp.exp(scores - jnp.max(scores, axis=1, keepdims=True))
    probs = expo * (1.0 / jnp.sum(expo, axis=1, keepdims=True))
    weights = probs.astype(BF16)
    heads[head] = ndot(weights, values).astype(BF16)
    d_probs = rdot(d_heads, values)
    inner = jnp.sum(probs * d_probs, axis=1, keepdims=True)
    d_scores = (probs * (d_probs - inner) * inv).astype(BF16)
    d_in[:, lanes] = ndot(d_scores, keys).astype(BF16)
    d_keys = tdot(d_scores, q)
    d_values = tdot(weights, d_heads)

    @pl.when(head == 0)
    def _():
        acc[:, 0:HD] = d_keys
        acc[:, HD : HD + VD] = d_values

    @pl.when(head > 0)
    def _():
        acc[:, 0:HD] += d_keys
        acc[:, HD : HD + VD] += d_values

    @pl.when(head == pl.num_programs(0) - 1)
    def _():
        d_in[:, first + HD :] = jnp.zeros((4 * half, cols - first - HD), BF16)
        d_in[:, first : first + HD + VD] = acc[...].astype(BF16)
        for piece, out in enumerate((own, part1, part2, part3)):
            rows = d_in[rows_of(lax.rem(seq + piece, 4)), :]
            out[...] = rdot(rows, w_in[...]).astype(out.dtype)
        width = cot.shape[1]
        blocks = cols // 128
        for half_core, out in ((1 - core, far_sum), (core, near_sum)):
            tall = width // 2
            lanes = pl.ds(pl.multiple_of(half_core * tall, tall), tall)
            rows_in[...] = tdot(normed[:, lanes], d_in[...]).astype(BF16)
            rows_out[...] = tdot(heads[half_core], cot[...]).astype(BF16)
            for turn in range(4):
                quarter = lax.rem(depth + turn, 4)
                count = tall // 4
                at = pl.ds(pl.multiple_of(quarter * count, count), count)
                for b in range(blocks):
                    out[turn, b * count : (b + 1) * count, :] = rows_in[at, b * 128 : (b + 1) * 128]
                base = blocks * count
                count = VD // 4
                at = pl.ds(pl.multiple_of(quarter * count, count), count)
                for b in range(width // 128):
                    out[turn, base + b * count : base + (b + 1) * count, :] = rows_out[
                        at, b * 128 : (b + 1) * 128
                    ]


def attend(place, norms, w_in, cot, d_heads):
    half, width = norms[0].shape
    rows = 4 * half
    cols = w_in.shape[1]
    heads = d_heads.shape[0]
    whole = lambda array: pl.BlockSpec(array.shape, lambda h, s: (0,) * array.ndim)
    length = cols // 128 * (width // 8) + width // 128 * (VD // 4)
    outs = (
        [
            jax.ShapeDtypeStruct((heads, rows, VD), BF16),
            jax.ShapeDtypeStruct((half, width), F32),
        ]
        + [jax.ShapeDtypeStruct((half, width), BF16)] * 3
        + [jax.ShapeDtypeStruct((4, length, 128), BF16)] * 2
    )
    specs = [whole(out) for out in outs]
    ins = (*norms, w_in, cot, d_heads)
    return pl.pallas_call(
        attend_kernel,
        grid_spec=pltpu.PrefetchScalarGridSpec(
            num_scalar_prefetch=1,
            grid=(heads,),
            in_specs=[whole(a) for a in ins],
            out_specs=specs,
            scratch_shapes=[
                pltpu.VMEM((rows, cols), BF16),
                pltpu.VMEM((rows, width), BF16),
                pltpu.VMEM((rows, cols), BF16),
                pltpu.VMEM((rows, HD + VD), F32),
                pltpu.VMEM((width // 2, cols), BF16),
                pltpu.VMEM((VD, width), BF16),
            ],
        ),
        out_shape=outs,
        compiler_params=pltpu.CompilerParams(vmem_limit_bytes=VMEM_LIMIT),
        cost_estimate=pl.CostEstimate(
            flops=2 * rows * heads * (2 * VD * width + 3 * rows * (HD + VD)) + 6 * rows * cols * width,
            bytes_accessed=8 * rows * width + 2 * heads * VD * width + 2 * cols * width,
            transcendentals=rows * heads * rows,
        ),
        name="attend",
    )(place, *ins)


def mix_kernel(place, heads, w_out, out):
    total = ndot(heads[0], w_out[0:VD, :]) + ndot(heads[1], w_out[VD : 2 * VD, :])
    out[0] = total.astype(BF16)


def mix(place, heads, w_out):
    rows = heads.shape[1] // 4
    width = w_out.shape[1]
    return pl.pallas_call(
        mix_kernel,
        grid_spec=pltpu.PrefetchScalarGridSpec(
            num_scalar_prefetch=1,
            grid=(4,),
            in_specs=[
                pl.BlockSpec((2, rows, VD), lambda n, s: (0, lax.rem(s[0] + n, 4), 0)),
                pl.BlockSpec(w_out.shape, lambda n, s: (0, 0)),
            ],
            out_specs=pl.BlockSpec((1, rows, width), lambda n, s: (n, 0, 0)),
        ),
        out_shape=jax.ShapeDtypeStruct((4, rows, width), BF16),
        compiler_params=pltpu.CompilerParams(vmem_limit_bytes=VMEM_LIMIT),
        cost_estimate=pl.CostEstimate(
            flops=16 * rows * width * VD, bytes_accessed=12 * rows * width, transcendentals=0
        ),
        name="mix",
    )(place, heads, w_out)


AXES = ("z", "y", "c", "x")
SIZES = (4, 4, 2, 4)


def place(z, y, c, x):
    return ((z * 4 + y) * 2 + c) * 4 + x


def moved(value, target):
    pairs = []
    for z in range(4):
        for y in range(4):
            for c in range(2):
                for x in range(4):
                    pairs.append((place(z, y, c, x), place(*target(z, y, c, x))))
    return lax.ppermute(value, AXES, pairs)


def flipped(value):
    return moved(value, lambda z, y, c, x: (z, y, 1 - c, x))


def turned(value, axis, by):
    return lax.ppermute(value, axis, [(i, (i + by) % 4) for i in range(4)])


def gathered(value, axis):
    me = lax.axis_index(axis)
    parts = [value, turned(value, axis, 3), turned(value, axis, 2), turned(value, axis, 1)]
    out = jnp.zeros((4, *value.shape), value.dtype)
    for j in range(4):
        out = lax.dynamic_update_index_in_dim(out, parts[j], lax.rem(me + j, 4), 0)
    return out


def summed(value, axis, dtype=BF16):
    me = lax.axis_index(axis)
    parts = [
        lax.dynamic_index_in_dim(value, lax.rem(me + j, 4), 0, keepdims=False) for j in range(4)
    ]
    total = parts[0].astype(F32)
    for j in range(1, 4):
        total = total + turned(parts[j], axis, j).astype(F32)
    return total.astype(dtype)


def by_core(own, other):
    first = lax.axis_index("c") == 0
    return jnp.where(first, own, other), jnp.where(first, other, own)


def around(value, axis="x"):
    return [value, turned(value, axis, 3), turned(value, axis, 2), turned(value, axis, 1)]


def returned(pieces):
    total = pieces[0].astype(F32)
    for k in range(1, 4):
        total = total + turned(pieces[k], "x", k).astype(F32)
    return total


def gather_in_x(w_query, w_kv):
    seq = lax.axis_index("x")
    cols = w_query.shape[1] // 4
    rows = jnp.zeros((4, w_query.shape[0], cols + w_kv.shape[1] + 64), BF16)
    w_kv = jnp.pad(w_kv, ((0, 0), (0, 64)))
    for k in range(4):
        head_cols = lax.dynamic_slice_in_dim(w_query, lax.rem(seq + k, 4) * cols, cols, 1)
        piece = jnp.concatenate([head_cols, w_kv], axis=1)
        if k:
            piece = turned(piece, "x", k)
        rows = lax.dynamic_update_index_in_dim(rows, piece, lax.rem(seq + 4 - k, 4), 0)
    return rows


def after(value, *others):
    return lax.optimization_barrier((value, *others))[0]


def split_rows(pieces):
    first = pieces[:960].reshape(5, 4, 48, 128).transpose(1, 0, 2, 3).reshape(4, 240, 128)
    second = pieces[960:].reshape(12, 4, 12, 128).transpose(1, 0, 2, 3).reshape(4, 144, 128)
    return jnp.concatenate([first, second], axis=1)


def finish(value, cols, width):
    seq = lax.axis_index("x")
    pieces = value[:240].reshape(5, 4, 12, 128).transpose(1, 2, 0, 3).reshape(4, 12, 640)
    grad_query = jnp.zeros((4, 12, cols), F32)
    grad_kv = jnp.zeros((12, HD + VD), F32)
    for k in range(4):

        def home(z, y, c, x):
            block = 16 * c + 4 * z + y
            return block // 8, block // 2 % 4, block % 2, (x + k) % 4

        piece = lax.dynamic_index_in_dim(pieces, lax.rem(seq + k, 4), 0, keepdims=False)
        piece = moved(piece, home).astype(F32)
        grad_query = lax.dynamic_update_index_in_dim(
            grad_query, piece[:, :cols], lax.rem(seq + 4 - k, 4), 0
        )
        grad_kv = grad_kv + piece[:, cols : cols + HD + VD]
    grad_query = grad_query.transpose(1, 0, 2).reshape(12, 4 * cols)
    grad_out = value[240:].reshape(12, 12, 128).transpose(1, 0, 2).reshape(12, width)
    grad_out = moved(grad_out, lambda z, y, c, x: (x, 2 * c + z // 2, z % 2, y)).astype(F32)
    return grad_query, grad_kv, grad_out


def rms_back(value, gain, grad):
    scale = row_scale(value)
    scaled = grad * gain
    return scale * scaled - value * (scale * scale * scale) * jnp.mean(
        value * scaled, axis=-1, keepdims=True
    )


def per_device(
    bases, skip, base_table, conv_weight, conv_gain, attn_gain, w_query, w_kv, w_out, cotangent
):
    skip = skip[0]
    cot = cotangent[0]
    rows, width = skip.shape
    half = rows // 2
    cells = bases.reshape(rows, bases.shape[1] // rows)
    seq = lax.axis_index("x")
    ends = jnp.stack([seq, 3 - seq]).astype(jnp.int32)

    def ahead(value):
        return lax.ppermute(value, "x", [(i, i + 1) for i in range(3)])

    def behind(value):
        return lax.ppermute(value, "x", [(i + 1, i) for i in range(3)])

    def edge(tokens, features):
        tokens = tokens.reshape(8, -1)
        counts = [jnp.sum((tokens == b).astype(F32), axis=1, keepdims=True) for b in range(4)]
        counts = jnp.concatenate(counts + [jnp.zeros((8, 124), F32)], axis=1)
        return jnp.concatenate([features, counts.astype(BF16)], axis=1)

    span = 8 * (bases.shape[1] // rows)
    edge_prev = ahead(edge(bases[0, bases.shape[1] - span :], skip[rows - 8 :]))
    edge_next = behind(edge(bases[0, :span], skip[:8]))
    w_rows = gather_in_x(w_query, w_kv)
    out_home = moved(w_out, lambda z, y, c, x: (y, x, c, z))
    w_rows = after(w_rows, cells)
    beside = lax.ppermute(after(cot, w_rows), "x", [(i, i ^ 1) for i in range(4)])
    across = lax.ppermute(jnp.stack([cot, beside]), "x", [(i, 3 - i) for i in range(4)])
    side = width // 3
    cols = w_rows.shape[2]
    chunks = out_home.reshape(12, 4, width // 4).transpose(1, 0, 2)
    pieces = jnp.stack(around(jnp.concatenate([w_rows, chunks], axis=2), "y"))
    out_rows = jnp.roll(pieces[:, :, :, cols:], lax.axis_index("y"), axis=0)
    out_rows = out_rows.transpose(0, 2, 1, 3).reshape(48, width)
    rest = pieces[:, :, :, side:cols].reshape(4, 48, cols - side)
    joint = jnp.concatenate(
        [
            pieces[:, :, :, :side].reshape(192, side),
            out_rows.reshape(48, 3, side).transpose(1, 0, 2).reshape(144, side),
            rest.transpose(1, 0, 2).reshape(48, side),
        ],
        axis=0,
    )
    near = jnp.stack(around(joint, "z"))
    table = jnp.concatenate([base_table, conv_gain[None, :], attn_gain[None, :]], axis=0)
    pooled, normed = front(
        ends, cells, skip, edge_prev, edge_next, table, conv_weight
    )
    norms = around(normed)
    far = flipped(after(near, normed, across))

    spot = [seq, lax.axis_index("c"), lax.axis_index("z"), lax.axis_index("y")]
    spot = jnp.stack(spot).astype(jnp.int32)
    w_in, full_out, cot_all, d_heads = prep(spot, (cot, beside, across), near, far)
    norms = [after(norm, w_in) for norm in norms]
    heads, *d_parts, own, other = attend(spot, norms, w_in, cot_all, d_heads)
    d_parts[1:] = [turned(d_parts[k], "x", k) for k in range(1, 4)]
    mine = (own.astype(F32) + flipped(other).astype(F32)).astype(BF16)
    total = mine[0].astype(F32)
    for k in range(1, 4):
        total = total + turned(mine[k], "z", k).astype(F32)
    mine = total.astype(BF16)
    d_normed = d_parts[0]
    for k in range(1, 4):
        d_normed = d_normed + after(d_parts[k], mine).astype(F32)
    mine = summed(split_rows(mine), "y")

    d_pooled = cot.astype(F32) + rms_back(pooled, attn_gain, d_normed)
    grad = (d_pooled * 0.5).astype(BF16)
    out_parts = mix(spot, heads, full_out)
    grad_prev, grad_next = ahead(grad[half - 16 :]), behind(grad[:16])
    grad_next = after(grad_next, mine)
    coarse = (pooled + returned(after(out_parts, grad_prev))).astype(BF16)
    skip_grad = back(cells, skip, table, grad, grad_prev, grad_next, conv_weight)

    factor = 1.0 / 32
    cols = w_query.shape[1] // 4
    grad_query, grad_kv, grad_out = finish(mine, cols, width)
    grad_query = after(grad_query, coarse)
    return (
        coarse[None],
        skip_grad[None],
        grad_query * factor,
        grad_kv * factor,
        grad_out * factor,
    )


def solution(mesh):
    inner = Mesh(mesh.devices.reshape(SIZES), AXES)
    dp = ("z", "y", "c")
    every = AXES
    placed = (
        P(dp, "x"),
        P(dp, "x", None),
        P(),
        P(),
        P(),
        P(),
        P(every, None),
        P(every, None),
        P(every, None),
        P(dp, "x", None),
    )
    return jax.shard_map(
        per_device,
        mesh=inner,
        in_specs=placed,
        out_specs=(
            P(dp, "x", None),
            P(dp, "x", None),
            P(every, None),
            P(every, None),
            P(every, None),
        ),
        check_vma=False,
    )
```

```python
import jax
import jax.numpy as jnp
from jax import lax
from jax.experimental import pallas as pl
from jax.experimental.pallas import tpu as pltpu
from jax.sharding import Mesh
from jax.sharding import PartitionSpec as P

HQ = 8
HD = 128
VD = 192
VMEM_LIMIT = 60 * 1024 * 1024
F32 = jnp.float32
BF16 = jnp.bfloat16


def ndot(left, right):
    return lax.dot_general(
        left, right, (((1,), (0,)), ((), ())), preferred_element_type=F32
    )


def rdot(left, right):
    return lax.dot_general(
        left, right, (((1,), (1,)), ((), ())), preferred_element_type=F32
    )


def tdot(left, right):
    return lax.dot_general(
        left, right, (((0,), (0,)), ((), ())), preferred_element_type=F32
    )


def embed_counts(counts, skip, table):
    state = skip.astype(F32)
    for base in range(4):
        state = state + ((counts[base] - 16.0) * 0.25) * table[base : base + 1, :]
    return state


def embed_rows(cells, skip, table):
    counts = [jnp.sum((cells == base).astype(F32), axis=1, keepdims=True) for base in range(4)]
    return embed_counts(counts, skip, table)


def row_scale(value):
    return lax.rsqrt(jnp.mean(value * value, axis=-1, keepdims=True) + 1e-06)


def front_kernel(
    ends, cells, skip, edge_prev, edge_next, table,
    weight, pooled, normed, state_buf, active_buf, lhs, weight_buf, arrived,
):
    gain, attn_gain = table.at[4:5], table.at[5:6]
    rows = skip.shape[0]
    half = rows // 2
    width = skip.shape[1]
    steps, _, _, block = weight_buf.shape

    def fetch(step):
        cols = pl.ds(pl.multiple_of(step * block, block), block)
        return pltpu.make_async_copy(weight.at[:, :, cols], weight_buf.at[step], arrived.at[step])

    for step in range(steps):
        fetch(step).start()

    def rows_in(state, at, keep):
        pre = state * row_scale(state) * gain[...]
        active = 0.5 * pre * (1.0 + lax.erf(pre * 0.7071067811865476))
        active = active.astype(BF16).astype(F32)
        if keep is not None:
            active = jnp.where(keep > 0, active, 0.0)
        count = state.shape[0]
        for tile in range(skip.shape[1] // 128):
            lanes = slice(tile * 128, (tile + 1) * 128)
            state_buf[tile, pl.ds(at, count), :] = state[:, lanes]
            active_buf[tile, pl.ds(at, count), :] = active[:, lanes]

    def edge_rows(edge):
        counts = [edge[:, width + base : width + base + 1].astype(F32) for base in range(4)]
        return embed_counts(counts, edge[:, 0:width], table)

    rows_in(edge_rows(edge_prev), 0, ends[0])
    rows_in(edge_rows(edge_next), rows + 8, ends[1])

    chunk = 64

    def one(i, carry):
        at = pl.multiple_of(i * chunk, chunk)
        state = embed_rows(cells[pl.ds(at, chunk), :], skip[pl.ds(at, chunk), :], table)
        rows_in(state, pl.multiple_of(at + 8, 8), None)
        return carry

    lax.fori_loop(0, rows // chunk, one, 0)
    for tile in range(width // 128):
        cols = slice(tile * 128, (tile + 1) * 128)
        part = [active_buf[tile, pl.ds(6 + j, half, 2), :] for j in range(6)]
        for k in range(5):
            lhs[k, :, cols] = ((part[k] + part[k + 1]) * 0.5).astype(BF16)
        pooled[:, cols] = (
            state_buf[tile, pl.ds(8, half, 2), :] + state_buf[tile, pl.ds(9, half, 2), :]
        ) * 0.5

    def one_block(step, carry):
        fetch(step).wait()
        total = ndot(lhs[0], weight_buf[step, 0])
        for k in range(1, 5):
            total = total + ndot(lhs[k], weight_buf[step, k])
        cols = pl.ds(pl.multiple_of(step * block, block), block)
        pooled[:, cols] = pooled[:, cols] + total
        return carry

    lax.fori_loop(0, steps, one_block, 0)

    def finish_rows(i, carry):
        rows_at = pl.ds(pl.multiple_of(i * 64, 64), 64)
        value = pooled[rows_at, :]
        normed[rows_at, :] = (value * row_scale(value) * attn_gain[...]).astype(BF16)
        return carry

    lax.fori_loop(0, half // 64, finish_rows, 0)


def front(ends, cells, skip, edge_prev, edge_next, table, weight, block=256):
    rows, width = skip.shape
    half = rows // 2
    whole = lambda array: pl.BlockSpec(array.shape, lambda n, s: (0,) * array.ndim)
    small = (cells, skip, edge_prev, edge_next, table)
    return pl.pallas_call(
        front_kernel,
        grid_spec=pltpu.PrefetchScalarGridSpec(
            num_scalar_prefetch=1,
            grid=(1,),
            in_specs=[whole(a) for a in small] + [pl.BlockSpec(memory_space=pl.ANY)],
            out_specs=[
                pl.BlockSpec((half, width), lambda n, s: (0, 0)),
                pl.BlockSpec((half, width), lambda n, s: (0, 0)),
            ],
            scratch_shapes=[
                pltpu.VMEM((width // 128, rows + 16, 128), F32),
                pltpu.VMEM((width // 128, rows + 16, 128), F32),
                pltpu.VMEM((5, half, width), BF16),
                pltpu.VMEM((width // block, 5, width, block), BF16),
                pltpu.SemaphoreType.DMA((width // block,)),
            ],
        ),
        out_shape=[
            jax.ShapeDtypeStruct((half, width), F32),
            jax.ShapeDtypeStruct((half, width), BF16),
        ],
        compiler_params=pltpu.CompilerParams(vmem_limit_bytes=VMEM_LIMIT),
        cost_estimate=pl.CostEstimate(
            flops=2 * half * 5 * width * width, bytes_accessed=10 * width * width + 8 * rows * width, transcendentals=rows * width
        ),
        name="front",
    )(ends, *small, weight)


def back_kernel(
    cells, skip, table, grad, grad_prev, grad_next, weight, out,
    state_buf, scaled_buf, grad_buf, turned_buf, level_buf, scale_buf, sum_buf, weight_buf, arrived,
):
    gain = table.at[4:5]
    rows, width = skip.shape
    half = rows // 2
    steps, _, block, _ = weight_buf.shape
    chunk = 64

    def fetch(step):
        at = pl.ds(pl.multiple_of(step * block, block), block)
        return pltpu.make_async_copy(weight.at[:, at, :], weight_buf.at[step], arrived.at[step])

    for step in range(steps):
        fetch(step).start()

    grad_buf[pl.ds(0, 16), :] = grad_prev[...].astype(F32)
    grad_buf[pl.ds(16, half), :] = grad[...].astype(F32)
    grad_buf[pl.ds(half + 16, 16), :] = grad_next[...].astype(F32)
    for tile in range(width // 128):
        lanes = slice(tile * 128, (tile + 1) * 128)
        before, here, later = [
            grad_buf[pl.ds(15 + shift, half), lanes].T.astype(BF16) for shift in range(3)
        ]
        pairs = ((later, later), (here, later), (here, here), (before, here), (before, before))
        for tap, (even, odd) in enumerate(pairs):
            turned_buf[tap, lanes, 0:half] = even
            turned_buf[tap, lanes, half:rows] = odd

    def one(i, carry):
        at = pl.ds(pl.multiple_of(i * chunk, chunk), chunk)
        state = embed_rows(cells[at, :], skip[at, :], table)
        state_buf[at, :] = state
        scale_buf[at, :] = row_scale(state)
        return carry

    lax.fori_loop(0, rows // chunk, one, 0, unroll=2)
    sum_buf[...] = jnp.zeros_like(sum_buf)

    def one_block(step, carry):
        fetch(step).wait()
        total = None
        for k in range(5):
            part = ndot(weight_buf[step, k], turned_buf[k])
            total = part if total is None else total + part
        for tile in range(block // 128):
            level = total[tile * 128 : (tile + 1) * 128, :].T
            level_buf[tile, pl.ds(0, half, 2), :] = level[0:half]
            level_buf[tile, pl.ds(1, half, 2), :] = level[half:]
        cols = pl.ds(pl.multiple_of(step * block, block), block)

        def two(i, carry):
            at = pl.ds(pl.multiple_of(i * 256, 256), 256)
            state = state_buf[at, cols]
            pre = state * scale_buf[at, :] * gain[:, cols]
            slope = 0.5 * (1.0 + lax.erf(pre * 0.7071067811865476)) + pre * jnp.exp(
                -0.5 * pre * pre
            ) * 0.3989422804014327
            level = jnp.concatenate([level_buf[t, at, :] for t in range(block // 128)], axis=1)
            scaled = slope * level * gain[:, cols]
            scaled_buf[at, cols] = scaled
            product = state * scaled
            folded = product[:, 0:128]
            for tile in range(1, block // 128):
                folded = folded + product[:, tile * 128 : (tile + 1) * 128]
            sum_buf[at, :] = sum_buf[at, :] + folded
            return carry

        lax.fori_loop(0, rows // 256, two, 0)
        return carry

    lax.fori_loop(0, steps, one_block, 0)

    scale = scale_buf[...]
    coef = (scale * scale * scale) * (jnp.sum(sum_buf[...], axis=1, keepdims=True) * (1.0 / width))
    for tile in range(width // 128):
        lanes = slice(tile * 128, (tile + 1) * 128)
        own = grad_buf[pl.ds(16, half), lanes]
        scaled = scaled_buf[:, lanes]
        state = state_buf[:, lanes]
        level_buf[0, pl.ds(0, half, 2), :] = own
        level_buf[0, pl.ds(1, half, 2), :] = own
        out[:, lanes] = (level_buf[0] + (scale * scaled - state * coef)).astype(BF16)


def back(cells, skip, table, grad, grad_prev, grad_next, weight, block=256):
    rows, width = skip.shape
    half = rows // 2
    whole = lambda array: pl.BlockSpec(array.shape, lambda n: (0,) * array.ndim)
    small = (cells, skip, table, grad, grad_prev, grad_next)
    return pl.pallas_call(
        back_kernel,
        grid=(1,),
        in_specs=[whole(a) for a in small] + [pl.BlockSpec(memory_space=pl.ANY)],
        out_specs=pl.BlockSpec((rows, width), lambda n: (0, 0)),
        scratch_shapes=[
            pltpu.VMEM((rows, width), F32),
            pltpu.VMEM((rows, width), F32),
            pltpu.VMEM((half + 32, width), F32),
            pltpu.VMEM((5, width, rows), BF16),
            pltpu.VMEM((block // 128, rows, 128), F32),
            pltpu.VMEM((rows, 1), F32),
            pltpu.VMEM((rows, 128), F32),
            pltpu.VMEM((width // block, 5, block, width), BF16),
            pltpu.SemaphoreType.DMA((width // block,)),
        ],
        out_shape=jax.ShapeDtypeStruct((rows, width), BF16),
        compiler_params=pltpu.CompilerParams(vmem_limit_bytes=VMEM_LIMIT),
        cost_estimate=pl.CostEstimate(
            flops=2 * half * 5 * width * width, bytes_accessed=10 * width * width + 8 * rows * width, transcendentals=2 * rows * width
        ),
        name="back",
    )(*small, weight)


def prep_kernel(place, cot0, cot1, cot2, near, far, w_in, w_out, cot, d_heads):
    seq, core, depth, level = place[0], place[1], place[2], place[3]
    half = cot0.shape[0]
    side = near.shape[2]
    cols = w_in.shape[1]

    def rows_of(index):
        return pl.ds(pl.multiple_of(index * half, half), half)

    for source, side_core in ((near, core), (far, 1 - core)):
        for turn in range(4):
            z = lax.rem(depth + turn, 4)
            for other in range(4):
                y = lax.rem(level + other, 4)
                at = pl.ds(pl.multiple_of((z * 4 + y) * 96 + side_core * 48, 16), 48)
                w_in[at, 0:side] = source[turn, other * 48 : (other + 1) * 48, :]
                w_in[at, side:cols] = source[turn, 336:384, other * 128 : (other + 1) * 128]
            at = pl.ds(pl.multiple_of(z * 96 + side_core * 48, 16), 48)
            for b in range(3):
                w_out[at, b * side : (b + 1) * side] = source[
                    turn, 192 + b * 48 : 240 + b * 48, :
                ]
    beside = seq + 1 - 2 * lax.rem(seq, 2)
    cot[rows_of(seq), :] = cot0[...]
    cot[rows_of(beside), :] = cot1[...]
    cot[rows_of(3 - seq), :] = cot2[0]
    cot[rows_of(3 - beside), :] = cot2[1]
    for head in range(d_heads.shape[0]):
        d_heads[head] = rdot(cot[...], w_out[head * VD : (head + 1) * VD, :]).astype(BF16)


def prep(place, cots, near, far):
    half, width = cots[0].shape
    rows = 4 * half
    whole = lambda array: pl.BlockSpec(array.shape, lambda n, s: (0,) * array.ndim)
    outs = [
        jax.ShapeDtypeStruct((width, near.shape[2] + 128), BF16),
        jax.ShapeDtypeStruct((2 * VD, width), BF16),
        jax.ShapeDtypeStruct((rows, width), BF16),
        jax.ShapeDtypeStruct((2, rows, VD), BF16),
    ]
    ins = (*cots, near, far)
    return pl.pallas_call(
        prep_kernel,
        grid_spec=pltpu.PrefetchScalarGridSpec(
            num_scalar_prefetch=1,
            grid=(1,),
            in_specs=[whole(a) for a in ins],
            out_specs=[whole(a) for a in outs],
        ),
        out_shape=outs,
        compiler_params=pltpu.CompilerParams(vmem_limit_bytes=VMEM_LIMIT),
        cost_estimate=pl.CostEstimate(
            flops=4 * rows * VD * width, bytes_accessed=10 * width * width, transcendentals=0
        ),
        name="prep",
    )(place, *ins)


def attend_kernel(
    place, norm0, norm1, norm2, norm3, w_in, cot, d_heads_all,
    heads, own, part1, part2, part3, near_sum, far_sum,
    d_in, normed, query_kv, acc, rows_in, rows_out,
):
    head = pl.program_id(0)
    seq, core, depth = place[0], place[1], place[2]
    inv = 1.0 / HD**0.5
    half = own.shape[0]
    cols = w_in.shape[1]
    first = cols - 128 - HD - HD

    def rows_of(index):
        return pl.ds(pl.multiple_of(index * half, half), half)

    @pl.when(head == 0)
    def _():
        for piece, value in enumerate((norm0, norm1, norm2, norm3)):
            normed[rows_of(lax.rem(seq + piece, 4)), :] = value[...]
        query_kv[...] = ndot(normed[...], w_in[...]).astype(BF16)

    keys = query_kv[:, first : first + HD]
    values = query_kv[:, first + HD : first + HD + VD]
    lanes = pl.ds(pl.multiple_of(head * HD, HD), HD)
    q = query_kv[:, lanes]
    d_heads = d_heads_all[head]
    scores = rdot(q, keys) * inv
    expo = jnp.exp(scores - jnp.max(scores, axis=1, keepdims=True))
    probs = expo * (1.0 / jnp.sum(expo, axis=1, keepdims=True))
    weights = probs.astype(BF16)
    heads[head] = ndot(weights, values).astype(BF16)
    d_probs = rdot(d_heads, values)
    inner = jnp.sum(probs * d_probs, axis=1, keepdims=True)
    d_scores = (probs * (d_probs - inner) * inv).astype(BF16)
    d_in[:, lanes] = ndot(d_scores, keys).astype(BF16)
    d_keys = tdot(d_scores, q)
    d_values = tdot(weights, d_heads)

    @pl.when(head == 0)
    def _():
        acc[:, 0:HD] = d_keys
        acc[:, HD : HD + VD] = d_values

    @pl.when(head > 0)
    def _():
        acc[:, 0:HD] += d_keys
        acc[:, HD : HD + VD] += d_values

    @pl.when(head == pl.num_programs(0) - 1)
    def _():
        d_in[:, first + HD :] = jnp.zeros((4 * half, cols - first - HD), BF16)
        d_in[:, first : first + HD + VD] = acc[...].astype(BF16)
        for piece, out in enumerate((own, part1, part2, part3)):
            rows = d_in[rows_of(lax.rem(seq + piece, 4)), :]
            out[...] = rdot(rows, w_in[...]).astype(out.dtype)
        width = cot.shape[1]
        blocks = cols // 128
        for half_core, out in ((1 - core, far_sum), (core, near_sum)):
            tall = width // 2
            lanes = pl.ds(pl.multiple_of(half_core * tall, tall), tall)
            rows_in[...] = tdot(normed[:, lanes], d_in[...]).astype(BF16)
            rows_out[...] = tdot(heads[half_core], cot[...]).astype(BF16)
            for turn in range(4):
                quarter = lax.rem(depth + turn, 4)
                count = tall // 4
                at = pl.ds(pl.multiple_of(quarter * count, count), count)
                for b in range(blocks):
                    out[turn, b * count : (b + 1) * count, :] = rows_in[at, b * 128 : (b + 1) * 128]
                base = blocks * count
                count = VD // 4
                at = pl.ds(pl.multiple_of(quarter * count, count), count)
                for b in range(width // 128):
                    out[turn, base + b * count : base + (b + 1) * count, :] = rows_out[
                        at, b * 128 : (b + 1) * 128
                    ]


def attend(place, norms, w_in, cot, d_heads):
    half, width = norms[0].shape
    rows = 4 * half
    cols = w_in.shape[1]
    heads = d_heads.shape[0]
    whole = lambda array: pl.BlockSpec(array.shape, lambda h, s: (0,) * array.ndim)
    length = cols // 128 * (width // 8) + width // 128 * (VD // 4)
    outs = (
        [
            jax.ShapeDtypeStruct((heads, rows, VD), BF16),
            jax.ShapeDtypeStruct((half, width), F32),
        ]
        + [jax.ShapeDtypeStruct((half, width), BF16)] * 3
        + [jax.ShapeDtypeStruct((4, length, 128), BF16)] * 2
    )
    specs = [whole(out) for out in outs]
    ins = (*norms, w_in, cot, d_heads)
    return pl.pallas_call(
        attend_kernel,
        grid_spec=pltpu.PrefetchScalarGridSpec(
            num_scalar_prefetch=1,
            grid=(heads,),
            in_specs=[whole(a) for a in ins],
            out_specs=specs,
            scratch_shapes=[
                pltpu.VMEM((rows, cols), BF16),
                pltpu.VMEM((rows, width), BF16),
                pltpu.VMEM((rows, cols), BF16),
                pltpu.VMEM((rows, HD + VD), F32),
                pltpu.VMEM((width // 2, cols), BF16),
                pltpu.VMEM((VD, width), BF16),
            ],
        ),
        out_shape=outs,
        compiler_params=pltpu.CompilerParams(vmem_limit_bytes=VMEM_LIMIT),
        cost_estimate=pl.CostEstimate(
            flops=2 * rows * heads * (2 * VD * width + 3 * rows * (HD + VD)) + 6 * rows * cols * width,
            bytes_accessed=8 * rows * width + 2 * heads * VD * width + 2 * cols * width,
            transcendentals=rows * heads * rows,
        ),
        name="attend",
    )(place, *ins)


def mix_kernel(place, heads, w_out, part0, part1, part2, part3):
    for turn, out in enumerate((part0, part1, part2, part3)):
        length = out.shape[0]
        at = pl.multiple_of(lax.rem(place[0] + turn, 4) * length, length)
        total = ndot(heads[0, pl.ds(at, length), :], w_out[0:VD, :])
        total = total + ndot(heads[1, pl.ds(at, length), :], w_out[VD : 2 * VD, :])
        out[...] = total.astype(BF16)


def mix(place, heads, w_out):
    rows = heads.shape[1] // 4
    width = w_out.shape[1]
    whole = lambda array: pl.BlockSpec(array.shape, lambda n, s: (0,) * array.ndim)
    outs = [jax.ShapeDtypeStruct((rows, width), BF16)] * 4
    return pl.pallas_call(
        mix_kernel,
        grid_spec=pltpu.PrefetchScalarGridSpec(
            num_scalar_prefetch=1,
            grid=(1,),
            in_specs=[whole(heads), whole(w_out)],
            out_specs=[whole(out) for out in outs],
        ),
        out_shape=outs,
        compiler_params=pltpu.CompilerParams(vmem_limit_bytes=VMEM_LIMIT),
        cost_estimate=pl.CostEstimate(
            flops=16 * rows * width * VD, bytes_accessed=12 * rows * width, transcendentals=0
        ),
        name="mix",
    )(place, heads, w_out)


AXES = ("z", "y", "c", "x")
SIZES = (4, 4, 2, 4)


def place(z, y, c, x):
    return ((z * 4 + y) * 2 + c) * 4 + x


def moved(value, target):
    pairs = []
    for z in range(4):
        for y in range(4):
            for c in range(2):
                for x in range(4):
                    pairs.append((place(z, y, c, x), place(*target(z, y, c, x))))
    return lax.ppermute(value, AXES, pairs)


def flipped(value):
    return moved(value, lambda z, y, c, x: (z, y, 1 - c, x))


def turned(value, axis, by):
    return lax.ppermute(value, axis, [(i, (i + by) % 4) for i in range(4)])


def gathered(value, axis):
    me = lax.axis_index(axis)
    parts = [value, turned(value, axis, 3), turned(value, axis, 2), turned(value, axis, 1)]
    out = jnp.zeros((4, *value.shape), value.dtype)
    for j in range(4):
        out = lax.dynamic_update_index_in_dim(out, parts[j], lax.rem(me + j, 4), 0)
    return out


def summed(value, axis, dtype=BF16):
    me = lax.axis_index(axis)
    parts = [
        lax.dynamic_index_in_dim(value, lax.rem(me + j, 4), 0, keepdims=False) for j in range(4)
    ]
    total = parts[0].astype(F32)
    for j in range(1, 4):
        total = total + turned(parts[j], axis, j).astype(F32)
    return total.astype(dtype)


def by_core(own, other):
    first = lax.axis_index("c") == 0
    return jnp.where(first, own, other), jnp.where(first, other, own)


def around(value, axis="x"):
    return [value, turned(value, axis, 3), turned(value, axis, 2), turned(value, axis, 1)]


def returned(pieces):
    total = pieces[0].astype(F32)
    for k in range(1, 4):
        total = total + turned(pieces[k], "x", k).astype(F32)
    return total


def gather_in_x(w_query, w_kv):
    seq = lax.axis_index("x")
    cols = w_query.shape[1] // 4
    rows = jnp.zeros((4, w_query.shape[0], cols + w_kv.shape[1] + 64), BF16)
    w_kv = jnp.pad(w_kv, ((0, 0), (0, 64)))
    for k in range(4):
        head_cols = lax.dynamic_slice_in_dim(w_query, lax.rem(seq + k, 4) * cols, cols, 1)
        piece = jnp.concatenate([head_cols, w_kv], axis=1)
        if k:
            piece = turned(piece, "x", k)
        rows = lax.dynamic_update_index_in_dim(rows, piece, lax.rem(seq + 4 - k, 4), 0)
    return rows


def after(value, *others):
    return lax.optimization_barrier((value, *others))[0]


def split_rows(pieces):
    first = pieces[:960].reshape(5, 4, 48, 128).transpose(1, 0, 2, 3).reshape(4, 240, 128)
    second = pieces[960:].reshape(12, 4, 12, 128).transpose(1, 0, 2, 3).reshape(4, 144, 128)
    return jnp.concatenate([first, second], axis=1)


def finish(value, cols, width):
    seq = lax.axis_index("x")
    pieces = value[:240].reshape(5, 4, 12, 128).transpose(1, 2, 0, 3).reshape(4, 12, 640)
    grad_query = jnp.zeros((4, 12, cols), F32)
    grad_kv = jnp.zeros((12, HD + VD), F32)
    for k in range(4):

        def home(z, y, c, x):
            block = 16 * c + 4 * z + y
            return block // 8, block // 2 % 4, block % 2, (x + k) % 4

        piece = lax.dynamic_index_in_dim(pieces, lax.rem(seq + k, 4), 0, keepdims=False)
        piece = moved(piece, home).astype(F32)
        grad_query = lax.dynamic_update_index_in_dim(
            grad_query, piece[:, :cols], lax.rem(seq + 4 - k, 4), 0
        )
        grad_kv = grad_kv + piece[:, cols : cols + HD + VD]
    grad_query = grad_query.transpose(1, 0, 2).reshape(12, 4 * cols)
    grad_out = value[240:].reshape(12, 12, 128).transpose(1, 0, 2).reshape(12, width)
    grad_out = moved(grad_out, lambda z, y, c, x: (x, 2 * c + z // 2, z % 2, y)).astype(F32)
    return grad_query, grad_kv, grad_out


def rms_back(value, gain, grad):
    scale = row_scale(value)
    scaled = grad * gain
    return scale * scaled - value * (scale * scale * scale) * jnp.mean(
        value * scaled, axis=-1, keepdims=True
    )


def per_device(
    bases, skip, base_table, conv_weight, conv_gain, attn_gain, w_query, w_kv, w_out, cotangent
):
    skip = skip[0]
    cot = cotangent[0]
    rows, width = skip.shape
    half = rows // 2
    cells = bases.reshape(rows, bases.shape[1] // rows)
    seq = lax.axis_index("x")
    ends = jnp.stack([seq, 3 - seq]).astype(jnp.int32)

    def ahead(value):
        return lax.ppermute(value, "x", [(i, i + 1) for i in range(3)])

    def behind(value):
        return lax.ppermute(value, "x", [(i + 1, i) for i in range(3)])

    def edge(tokens, features):
        tokens = tokens.reshape(8, -1)
        counts = [jnp.sum((tokens == b).astype(F32), axis=1, keepdims=True) for b in range(4)]
        counts = jnp.concatenate(counts + [jnp.zeros((8, 124), F32)], axis=1)
        return jnp.concatenate([features, counts.astype(BF16)], axis=1)

    span = 8 * (bases.shape[1] // rows)
    edge_prev = ahead(edge(bases[0, bases.shape[1] - span :], skip[rows - 8 :]))
    edge_next = behind(edge(bases[0, :span], skip[:8]))
    w_rows = gather_in_x(w_query, w_kv)
    out_home = moved(w_out, lambda z, y, c, x: (y, x, c, z))
    beside = lax.ppermute(after(cot, w_rows), "x", [(i, i ^ 1) for i in range(4)])
    across = lax.ppermute(jnp.stack([cot, beside]), "x", [(i, 3 - i) for i in range(4)])
    side = width // 3
    cols = w_rows.shape[2]
    chunks = out_home.reshape(12, 4, width // 4).transpose(1, 0, 2)
    pieces = jnp.stack(around(jnp.concatenate([w_rows, chunks], axis=2), "y"))
    out_rows = jnp.roll(pieces[:, :, :, cols:], lax.axis_index("y"), axis=0)
    out_rows = out_rows.transpose(0, 2, 1, 3).reshape(48, width)
    rest = pieces[:, :, :, side:cols].reshape(4, 48, cols - side)
    joint = jnp.concatenate(
        [
            pieces[:, :, :, :side].reshape(192, side),
            out_rows.reshape(48, 3, side).transpose(1, 0, 2).reshape(144, side),
            rest.transpose(1, 0, 2).reshape(48, side),
        ],
        axis=0,
    )
    near = jnp.stack(around(joint, "z"))
    table = jnp.concatenate([base_table, conv_gain[None, :], attn_gain[None, :]], axis=0)
    pooled, normed = front(
        ends, cells, skip, edge_prev, edge_next, table, conv_weight
    )
    norms = around(normed)
    far = flipped(after(near, normed, across))

    spot = [seq, lax.axis_index("c"), lax.axis_index("z"), lax.axis_index("y")]
    spot = jnp.stack(spot).astype(jnp.int32)
    w_in, full_out, cot_all, d_heads = prep(spot, (cot, beside, across), near, far)
    norms = [after(norm, w_in) for norm in norms]
    heads, *d_parts, own, other = attend(spot, norms, w_in, cot_all, d_heads)
    d_parts[1:] = [turned(d_parts[k], "x", k) for k in range(1, 4)]
    other = flipped(other)
    mine = [(own[k].astype(F32) + other[k].astype(F32)).astype(BF16) for k in range(4)]
    total = mine[0].astype(F32)
    for k in range(1, 4):
        total = total + turned(mine[k], "z", k).astype(F32)
    mine = total.astype(BF16)
    out_parts = mix(spot, heads, full_out)
    d_normed = d_parts[0]
    for k in range(1, 4):
        d_normed = d_normed + after(d_parts[k], mine, out_parts[0]).astype(F32)
    mine = summed(split_rows(mine), "y")

    d_pooled = cot.astype(F32) + rms_back(pooled, attn_gain, d_normed)
    grad = (d_pooled * 0.5).astype(BF16)
    grad_prev, grad_next = ahead(grad[half - 16 :]), behind(grad[:16])
    grad_next = after(grad_next, mine)
    coarse = (pooled + returned([after(part, grad_prev) for part in out_parts])).astype(BF16)
    skip_grad = back(cells, skip, table, grad, grad_prev, grad_next, conv_weight)

    factor = 1.0 / 32
    cols = w_query.shape[1] // 4
    grad_query, grad_kv, grad_out = finish(mine, cols, width)
    grad_query = after(grad_query, coarse)
    return (
        coarse[None],
        skip_grad[None],
        grad_query * factor,
        grad_kv * factor,
        grad_out * factor,
    )


def solution(mesh):
    inner = Mesh(mesh.devices.reshape(SIZES), AXES)
    dp = ("z", "y", "c")
    every = AXES
    placed = (
        P(dp, "x"),
        P(dp, "x", None),
        P(),
        P(),
        P(),
        P(),
        P(every, None),
        P(every, None),
        P(every, None),
        P(dp, "x", None),
    )
    return jax.shard_map(
        per_device,
        mesh=inner,
        in_specs=placed,
        out_specs=(
            P(dp, "x", None),
            P(dp, "x", None),
            P(every, None),
            P(every, None),
            P(every, None),
        ),
        check_vma=False,
    )
```
